32 devices in a mesh: seq: 8 (over z, core), tensor: 4 (over y, x).
Axes of the slice: x: 2, y: 2, z: 4, core: 2. Of those that a mesh axis runs over, the one named last changes fastest.
Arguments:
- queries: bfloat16 [2048, 1024], P('seq', 'tensor'), may hold values from -6 to 6
- keys: bfloat16 [2048, 1024], P('seq', 'tensor'), may hold values from -6 to 6
- values: bfloat16 [2048, 1024], P('seq', 'tensor'), may hold values from -6 to 6
- log_decay: float32 [8, 2048], P('tensor', 'seq'), may hold values from -1.6 to 0, as said below
- norm_gain: float32 [1024], P('tensor'), may hold values from 0.1 to 1.9
- out_weight: bfloat16 [1024, 6144], P('tensor'), may hold values from -0.25 to 0.25
- out_grad: bfloat16 [2048, 6144], P('seq', 'tensor'), may hold values from -6 to 6
Outputs:
- layer_out: bfloat16 [2048, 6144], P('seq', 'tensor')
- query_grad: bfloat16 [2048, 1024], P('seq', 'tensor')
- key_grad: bfloat16 [2048, 1024], P('seq', 'tensor')
- value_grad: bfloat16 [2048, 1024], P('seq', 'tensor')
The draws below stay inside these ranges and needn't reach their ends.
Inputs may be any that keep to these rules, and one draw needn't show every extreme that they name: `log_decay`: strictly negative.
All inputs are finite; a program needn't handle non-finite values.
Results may differ from the reference program's by a relative error of at most 0.015.
Values may be sent and summed in bfloat16 or wider, within the bound.
No kernel may reach another device: no remote copies, remote signals or barrier semaphores. Data moves between devices by JAX's collectives and lax.ppermute only.
A program may use at most 64 MiB of HBM per device.

```python
import jax
import jax.numpy as jnp
from jax import lax

D = 6144
HD = 128
HEAD_DEV = 2
TOK_DEV = 256
HEADS = 8
TOKEN_COUNT = 2048
N_TENSOR = 4


def draw_log_decay(key, part):
    key = jax.random.fold_in(key, 17)
    keys = jax.random.split(key, 7)
    blocks = TOKEN_COUNT // TOK_DEV
    share = 0.5
    quick = jax.random.uniform(keys[0], (HEADS, 1)) < share
    quick_rate = jnp.exp(jax.random.uniform(keys[1], (HEADS, 1), minval=jnp.log(1.0 / 50.0), maxval=jnp.log(1.0 / 25.0)))
    slow_rate = jnp.exp(jax.random.uniform(keys[2], (HEADS, 1), minval=jnp.log(0.15), maxval=jnp.log(0.6))) / TOKEN_COUNT
    starting_index = jnp.where(quick, quick_rate, slow_rate)
    device_portion = jnp.exp(jax.random.uniform(keys[3], (HEADS, blocks, 1), minval=jnp.log(0.5), maxval=jnp.log(2.0)))
    device_portion = jnp.broadcast_to(device_portion, (HEADS, blocks, TOK_DEV)).reshape(HEADS, TOKEN_COUNT)
    approximate_guess = jnp.exp(jax.random.uniform(keys[4], (HEADS, TOKEN_COUNT), minval=jnp.log(0.6), maxval=jnp.log(1.6)))
    target_locations = jax.random.randint(keys[5], (HEADS, 2, 1), 0, TOKEN_COUNT)
    tree_layer_index = jax.random.uniform(keys[6], (HEADS, 2, 1), minval=0.22, maxval=0.69)
    cluster_batches = jnp.sum(jnp.where(jnp.arange(TOKEN_COUNT)[None, None, :] == target_locations, tree_layer_index, 0.0), axis=1)
    return -(starting_index * device_portion * approximate_guess + cluster_batches)


def raised(array, key, source, target, blocks, factor):
    owner, partner = [(jnp.arange(array.shape[dim]) // (array.shape[dim] // blocks)).reshape([-1 if axis == dim else 1 for axis in range(array.ndim)]) for dim in (source, target)]
    chosen = jax.random.permutation(key, blocks)[partner]
    strong = (owner == chosen) | (owner == (partner + blocks // 2) % blocks)
    return jnp.where(strong, factor * array, array)


def levels(own_key, dims, shards, low, largest):
    loudness, own = 1.0, jax.random.fold_in(own_key, 6)
    for axis_at, shards_of in shards:
        steps = jnp.exp(jax.random.uniform(jax.random.fold_in(own, axis_at), (shards_of,), jnp.float32, low / len(shards), largest / len(shards)))
        loudness = loudness * jnp.repeat(steps, dims[axis_at] // shards_of).reshape([-1 if axis == axis_at else 1 for axis in range(len(dims))])
    return loudness


def noise(stream_key, dims, scale, bound, cuts=(), held_as=jnp.bfloat16):
    entries = scale * jax.random.normal(stream_key, dims, jnp.float32)
    if cuts:
        entries = entries * levels(stream_key, dims, cuts, -0.22, 0.18)
    return jnp.clip(entries, -bound, bound).astype(held_as)


def bell_draw_with(rng, shape, scale, reach, cuts, heavy, kind=jnp.bfloat16):
    entries = scale * jax.random.normal(rng, shape, jnp.float32)
    if cuts:
        entries = entries * levels(rng, shape, cuts, -0.22, 0.18)
    return jnp.clip(raised(entries, jax.random.fold_in(rng, 3), *heavy), -reach, reach).astype(kind)


def setup_inputs(seed: int = 0) -> dict:
    arg_keys = jax.random.split(jax.random.key(seed), 8)
    return {
        "queries": noise(arg_keys[0], (TOKEN_COUNT, HEADS * HD), 1.0, 6.0, ((0, 8), (1, 4))),
        "keys": noise(arg_keys[1], (TOKEN_COUNT, HEADS * HD), 1.0, 6.0, ((0, 8), (1, 4))),
        "values": noise(arg_keys[2], (TOKEN_COUNT, HEADS * HD), 1.0, 6.0, ((0, 8), (1, 4))),
        "log_decay": draw_log_decay(jax.random.fold_in(arg_keys[7], 71), 0),
        "norm_gain": jnp.clip(1.0 + 0.18 * jax.random.normal(arg_keys[4], (HEADS * HD,), jnp.float32), 0.1, 1.9),
        "out_weight": bell_draw_with(arg_keys[5], (HEADS * HD, D), (HEADS * HD) ** -0.5, 0.25, ((0, 4),), (0, 1, 4, 2.0)),
        "out_grad": noise(arg_keys[6], (TOKEN_COUNT, D), 1.0, 6.0, ((0, 8), (1, 4))),
    }


EXACT = lax.Precision.HIGHEST
EPSILON = 1e-05

def attend(queries, keys, values, log_decay):
    blocks = TOKEN_COUNT // TOK_DEV

    def arrange(rows):
        return rows.reshape(blocks, TOK_DEV, HEADS, HD).transpose(0, 2, 1, 3)
    decays = log_decay.reshape(HEADS, blocks, TOK_DEV).transpose(1, 0, 2)
    lower = jnp.arange(TOK_DEV)[:, None] >= jnp.arange(TOK_DEV)[None, :]

    def advance(state, item):
        query_rows, key_rows, value_rows, decay_rows = item
        running = jnp.cumsum(decay_rows, axis=1)
        last = running[:, -1:]
        weight = jnp.exp(jnp.where(lower, running[:, :, None] - running[:, None, :], -1e+30))
        scores = jnp.einsum('hte,hse->hts', query_rows, key_rows, precision=EXACT) * weight
        inner = jnp.einsum('hts,hse->hte', scores, value_rows, precision=EXACT)
        carried = jnp.einsum('hte,hef->htf', query_rows * jnp.exp(running)[:, :, None], state, precision=EXACT)
        fresh = jnp.einsum('hse,hsf->hef', key_rows * jnp.exp(last - running)[:, :, None], value_rows, precision=EXACT)
        state = jnp.exp(last)[:, :, None] * state + fresh
        return (state, inner + carried)
    start = jnp.zeros((HEADS, HD, HD), jnp.float32)
    ignored, results = lax.scan(advance, start, (arrange(queries), arrange(keys), arrange(values), decays))
    return results.transpose(0, 2, 1, 3).reshape(TOKEN_COUNT, HEADS, HD)

def reference(queries, keys, values, log_decay, norm_gain, out_weight, out_grad):
    gain = norm_gain.reshape(HEADS, HD)

    def forward(query_all, key_all, value_all):
        mixed = attend(query_all, key_all, value_all, log_decay)
        scale = lax.rsqrt(lax.optimization_barrier(jnp.mean(mixed * mixed, axis=-1, keepdims=True)) + EPSILON)
        return mixed * scale * gain
    normed, pullback = jax.vjp(forward, queries.astype(jnp.float32), keys.astype(jnp.float32), values.astype(jnp.float32))
    normed = normed.reshape(TOKEN_COUNT, HEADS * HD).astype(jnp.bfloat16)
    width = HEAD_DEV * HD

    def add_group(group, summed):
        begin = (group * width).astype(jnp.int32)
        columns_part = lax.dynamic_slice_in_dim(normed, begin, width, 1)
        weight_rows = lax.dynamic_slice_in_dim(out_weight, begin, width, 0)
        rounded = lax.optimization_barrier(jnp.dot(columns_part, weight_rows, preferred_element_type=jnp.float32).astype(jnp.bfloat16))
        return summed + rounded.astype(jnp.float32)
    layer_out = lax.fori_loop(0, N_TENSOR, add_group, jnp.zeros((TOKEN_COUNT, D), jnp.float32)).astype(jnp.bfloat16)
    grad_normed = jnp.dot(out_grad, out_weight.T, preferred_element_type=jnp.float32).reshape(TOKEN_COUNT, HEADS, HD)
    grad_query, grad_key, grad_value = pullback(grad_normed)
    return (layer_out, grad_query.reshape(TOKEN_COUNT, HEADS * HD).astype(jnp.bfloat16), grad_key.reshape(TOKEN_COUNT, HEADS * HD).astype(jnp.bfloat16), grad_value.reshape(TOKEN_COUNT, HEADS * HD).astype(jnp.bfloat16))
```

```python
import functools

import jax
import jax.numpy as jnp
from jax import lax
from jax.experimental import pallas as pl
from jax.experimental.pallas import tpu as pltpu
from jax.sharding import PartitionSpec as P

EXACT = lax.Precision.HIGHEST
EPSILON = 1e-05
F32 = jnp.float32
BF16 = jnp.bfloat16
TAIL = 16

NN = (((1,), (0,)), ((), ()))
NT = (((1,), (1,)), ((), ()))
TN = (((0,), (0,)), ((), ()))


def dot(a, b, dims):
    return lax.dot_general(a, b, dims, preferred_element_type=F32)


def split(x):
    high = x.astype(BF16)
    return high, (x - high.astype(F32)).astype(BF16)


def dot_fb(a, b, dims):
    high, low = split(a)
    return dot(high, b, dims) + dot(low, b, dims)


def dot_bf(a, b, dims):
    high, low = split(b)
    return dot(a, high, dims) + dot(a, low, dims)


def dot_ff(a, b, dims):
    ah, al = split(a)
    bh, bl = split(b)
    return dot(ah, bh, dims) + (dot(ah, bl, dims) + dot(al, bh, dims))


def triangle(length):
    rows = lax.broadcasted_iota(jnp.int32, (length, length), 0)
    cols = lax.broadcasted_iota(jnp.int32, (length, length), 1)
    return rows >= cols


def running_columns(decay, lower):
    return lax.dot_general(lower.astype(F32), decay, NT, precision=EXACT, preferred_element_type=F32)


def running_rows(decay, lower):
    return lax.dot_general(decay, lower.astype(F32), NT, precision=EXACT, preferred_element_type=F32)


def put_totals(ref, base, totals):
    rows = []
    for total in totals:
        first = total.astype(BF16).astype(F32)
        second = (total - first).astype(BF16).astype(F32)
        rows += [first, second, total - first - second]
    at = lax.broadcasted_iota(jnp.int32, (TAIL, 128), 0)
    tail = jnp.zeros((TAIL, 128), F32)
    for number, row in enumerate(rows):
        tail = jnp.where(at == number, row, tail)
    ref[base : base + TAIL, :] = tail.astype(BF16)


def get_totals(ref, base, heads):
    tail = ref[base : base + TAIL, :].astype(F32)
    return [
        tail[3 * h : 3 * h + 1] + tail[3 * h + 1 : 3 * h + 2] + tail[3 * h + 2 : 3 * h + 3]
        for h in range(heads)
    ]


def head(ref, h):
    return ref[:, h * 128 : (h + 1) * 128]


def total_row(columns, h):
    length = columns.shape[0]
    return jnp.broadcast_to(columns[length - 1 : length, h : h + 1], (1, 128))


def fresh_kernel(k_ref, v_ref, decay_ref, message_ref):
    heads, length = decay_ref.shape
    lower = triangle(length)
    columns = running_columns(decay_ref[...], lower)
    totals = []
    for h in range(heads):
        total = total_row(columns, h)
        totals.append(total)
        fade = jnp.exp(total - columns[:, h : h + 1])
        state = dot_bf(head(k_ref, h), fade * head(v_ref, h).astype(F32), TN)
        message_ref[h * 128 : (h + 1) * 128, :] = state.astype(BF16)
    put_totals(message_ref, heads * 128, totals)


def join_kernel(heads, later, core, own_ref, other_ref, message_ref):
    base = heads * 128
    own_totals = get_totals(own_ref, base, heads)
    other_totals = get_totals(other_ref, base, heads)
    first = core == 0
    for h in range(heads):
        rows = slice(h * 128, (h + 1) * 128)
        own = own_ref[rows, :].astype(F32)
        other = other_ref[rows, :].astype(F32)
        if later:
            decays_own = jnp.logical_not(first)
        else:
            decays_own = first
        shrink = jnp.exp(jnp.where(decays_own, other_totals[h], own_totals[h]))
        joined = jnp.where(decays_own, shrink * own + other, own + shrink * other)
        message_ref[rows, :] = joined.astype(BF16)
    put_totals(message_ref, base, [own_totals[h] + other_totals[h] for h in range(heads)])


def gather_state(heads, partner_ref, chip_refs, inside):
    base = heads * 128
    states = []
    partner_totals = get_totals(partner_ref, base, heads)
    chip_totals = [get_totals(ref, base, heads) for ref in chip_refs]
    for h in range(heads):
        rows = slice(h * 128, (h + 1) * 128)
        summed = jnp.zeros((128, 128), F32)
        passed = jnp.zeros((1, 128), F32)
        for number, ref in enumerate(chip_refs):
            summed = summed + jnp.exp(passed) * ref[rows, :].astype(F32)
            passed = passed + chip_totals[number][h]
        within = partner_ref[rows, :].astype(F32) + jnp.exp(partner_totals[h]) * summed
        states.append(jnp.where(inside, within, summed))
    return states


def inner_kernel(q_ref, k_ref, v_ref, decay_ref, inner_ref):
    heads, length = decay_ref.shape
    lower = triangle(length)
    columns = running_columns(decay_ref[...], lower)
    across = running_rows(decay_ref[...], lower)
    for h in range(heads):
        weight = jnp.exp(jnp.where(lower, columns[:, h : h + 1] - across[h : h + 1, :], -1e30))
        scores = dot(head(q_ref, h), head(k_ref, h), NT) * weight
        inner_ref[:, h * 128 : (h + 1) * 128] = dot_fb(scores, head(v_ref, h), NN)


def mixed_kernel(heads, chips, where_ref, q_ref, decay_ref, inner_ref, gain_ref, partner_ref, *refs):
    chip_refs = refs[:chips]
    mixed_ref, normed_ref, state_ref = refs[chips:]
    length = decay_ref.shape[1]
    inside = where_ref[0] == 1
    states = gather_state(heads, partner_ref, chip_refs, inside)
    lower = triangle(length)
    columns = running_columns(decay_ref[...], lower)
    for h in range(heads):
        lanes = slice(h * 128, (h + 1) * 128)
        grow = jnp.exp(columns[:, h : h + 1])
        mixed = inner_ref[:, lanes] + grow * dot_bf(head(q_ref, h), states[h], NN)
        scale = lax.rsqrt(jnp.mean(mixed * mixed, axis=-1, keepdims=True) + EPSILON)
        mixed_ref[:, lanes] = mixed
        normed_ref[:, lanes] = (mixed * scale * gain_ref[:, lanes]).astype(BF16)
        state_ref[lanes, :] = states[h]


def own_partial_kernel(grad_ref, weight_ref, out_ref):
    out_ref[...] = dot(grad_ref[...], weight_ref[...], NT)


def partial_kernel(where_ref, grad_ref, mine_ref, theirs_ref, out_ref):
    core = where_ref[0]
    half = mine_ref.shape[0]
    grad = grad_ref[...]
    out_ref[:, pl.ds(pl.multiple_of(core * half, half), half)] = dot(grad, mine_ref[...], NT).astype(BF16)
    out_ref[:, pl.ds(pl.multiple_of((1 - core) * half, half), half)] = dot(grad, theirs_ref[...], NT).astype(BF16)


def grad_mixed_kernel(heads, parts, q_ref, decay_ref, gain_ref, mixed_ref, own_ref, *refs):
    part_refs = refs[:parts]
    grad_ref, message_ref = refs[parts:]
    length = decay_ref.shape[1]
    lower = triangle(length)
    columns = running_columns(decay_ref[...], lower)
    totals = []
    for h in range(heads):
        lanes = slice(h * 128, (h + 1) * 128)
        normed = own_ref[:, lanes]
        for ref in part_refs:
            normed = normed + ref[:, lanes].astype(F32)
        lifted = normed * gain_ref[:, lanes]
        mixed = mixed_ref[:, lanes]
        scale = lax.rsqrt(jnp.mean(mixed * mixed, axis=-1, keepdims=True) + EPSILON)
        unit = mixed * scale
        grad = scale * (lifted - unit * jnp.mean(unit * lifted, axis=-1, keepdims=True))
        grad_ref[:, lanes] = grad
        upward = dot_bf(head(q_ref, h), jnp.exp(columns[:, h : h + 1]) * grad, TN)
        message_ref[lanes, :] = upward.astype(BF16)
        totals.append(total_row(columns, h))
    put_totals(message_ref, heads * 128, totals)


def inner_grad_kernel(q_ref, k_ref, v_ref, decay_ref, grad_ref, state_ref, dq_ref, dk_ref, dv_ref):
    heads, length = decay_ref.shape
    lower = triangle(length)
    columns = running_columns(decay_ref[...], lower)
    across = running_rows(decay_ref[...], lower)
    for h in range(heads):
        lanes = slice(h * 128, (h + 1) * 128)
        q, k, v, grad = head(q_ref, h), head(k_ref, h), head(v_ref, h), grad_ref[:, lanes]
        weight = jnp.exp(jnp.where(lower, columns[:, h : h + 1] - across[h : h + 1, :], -1e30))
        scores = dot(q, k, NT) * weight
        grad_scores = dot_fb(grad, v, NT) * weight
        carried = jnp.exp(columns[:, h : h + 1]) * dot_ff(grad, state_ref[lanes, :], NT)
        dq_ref[:, lanes] = (dot_fb(grad_scores, k, NN) + carried).astype(BF16)
        dk_ref[:, lanes] = dot_fb(grad_scores, q, TN)
        dv_ref[:, lanes] = dot_ff(scores, grad, TN)


def outer_grad_kernel(heads, chips, where_ref, k_ref, v_ref, decay_ref, dk_in, dv_in, partner_ref, *refs):
    chip_refs = refs[:chips]
    dk_ref, dv_ref = refs[chips:]
    length = decay_ref.shape[1]
    inside = where_ref[0] == 0
    states = gather_state(heads, partner_ref, chip_refs, inside)
    lower = triangle(length)
    columns = running_columns(decay_ref[...], lower)
    for h in range(heads):
        lanes = slice(h * 128, (h + 1) * 128)
        fade = jnp.exp(total_row(columns, h) - columns[:, h : h + 1])
        dk_ref[:, lanes] = (dk_in[:, lanes] + fade * dot_bf(head(v_ref, h), states[h], NT)).astype(BF16)
        dv_ref[:, lanes] = (dv_in[:, lanes] + fade * dot_bf(head(k_ref, h), states[h], NN)).astype(BF16)


def layer_kernel(others, where_ref, normed_ref, weight_ref, *refs):
    normed_refs = refs[:others]
    mine_refs = refs[others : 2 * others]
    theirs_refs = refs[2 * others : 3 * others]
    out_ref = refs[3 * others]
    core = where_ref[0]
    half = weight_ref.shape[0] // 2
    mine = pl.ds(pl.multiple_of(core * half, half), half)
    theirs = pl.ds(pl.multiple_of((1 - core) * half, half), half)
    width = weight_ref.shape[1]
    step = 384
    for begin in range(0, width, step):
        lanes = slice(begin, begin + step)
        total = dot(normed_ref[...], weight_ref[:, lanes], NN)
        for k in range(others):
            total = total + dot(normed_refs[k][:, mine], mine_refs[k][:, lanes], NN)
            total = total + dot(normed_refs[k][:, theirs], theirs_refs[k][:, lanes], NN)
        out_ref[:, lanes] = total.astype(BF16)


SMEM = pl.BlockSpec(memory_space=pltpu.SMEM)
VMEM = pl.BlockSpec(memory_space=pltpu.VMEM)


def call(kernel, name, outs, args, flops, scalars=0):
    moved = sum(a.size * a.dtype.itemsize for a in args) + sum(o.size * o.dtype.itemsize for o in outs)
    return pl.pallas_call(
        kernel,
        name=name,
        out_shape=outs,
        in_specs=[SMEM] * scalars + [VMEM] * (len(args) - scalars),
        out_specs=[VMEM] * len(outs),
        compiler_params=pltpu.CompilerParams(vmem_limit_bytes=40 * 2**20),
        cost_estimate=pl.CostEstimate(flops=int(flops), bytes_accessed=moved, transcendentals=0),
    )(*args)


def on_device(queries, keys, values, log_decay, norm_gain, out_weight, out_grad):
    length, columns = queries.shape
    heads = log_decay.shape[0]
    seq = lax.axis_size("seq")
    tensor = lax.axis_size("tensor")
    chips = seq // 2
    model = out_weight.shape[1]
    width = model // tensor
    half = columns // 2
    place = lax.axis_index("tensor")
    core = lax.rem(lax.axis_index("seq"), 2)
    where = core.astype(jnp.int32).reshape(1)
    gain = norm_gain.reshape(1, columns)

    def swap_tensor(value, k):
        return lax.ppermute(value, "tensor", [(i, i ^ k) for i in range(tensor)])

    def swap_core(value):
        return lax.ppermute(value, "seq", [(i, i ^ 1) for i in range(seq)])

    def to_chip(value, k):
        return lax.ppermute(
            value, "seq", [(i, i + 2 * k) for i in range(seq) if 0 <= i + 2 * k < seq]
        )

    def shape(rows, cols, dtype):
        return jax.ShapeDtypeStruct((rows, cols), dtype)

    others = range(1, tensor)
    message = shape(columns + TAIL, 128, BF16)

    mine = [
        swap_tensor(
            lax.dynamic_slice(out_weight, (core * half, (place ^ k) * width), (half, width)), k
        )
        for k in others
    ]
    (fresh,) = call(fresh_kernel, "fresh_state", [message], [keys, values, log_decay], 40e6)
    fresh_other = swap_core(fresh)

    def joined(own, other, later):
        def kernel(where_ref, own_ref, other_ref, message_ref):
            join_kernel(heads, later, where_ref[0], own_ref, other_ref, message_ref)

        (out,) = call(kernel, "join_states", [message], [where, own, other], 1e6, 1)
        return out

    chip_state = joined(fresh, fresh_other, False)
    arrived = [to_chip(chip_state, k) for k in range(1, chips)]
    (inner,) = call(
        inner_kernel, "inner", [shape(length, columns, F32)], [queries, keys, values, log_decay], 80e6
    )
    mixed, normed, state_in = call(
        functools.partial(mixed_kernel, heads, chips - 1),
        "mixed",
        [shape(length, columns, F32), shape(length, columns, BF16), shape(columns, 128, F32)],
        [where, queries, log_decay, inner, gain, fresh_other, *arrived],
        40e6,
        1,
    )
    weight_own = lax.dynamic_slice(out_weight, (0, place * width), (columns, width))
    (own_partial,) = call(
        own_partial_kernel, "own_partial", [shape(length, columns, F32)], [out_grad, weight_own], 2 * length * columns * width
    )
    theirs = [swap_core(piece) for piece in mine]
    partials = []
    for k in others:
        (partial,) = call(
            partial_kernel,
            "partial",
            [shape(length, columns, BF16)],
            [where, out_grad, mine[k - 1], theirs[k - 1]],
            2 * length * columns * width,
            1,
        )
        partials.append(swap_tensor(partial, k))
    normed_others = [swap_tensor(normed, k) for k in others]
    grad_mixed, upward = call(
        functools.partial(grad_mixed_kernel, heads, tensor - 1),
        "grad_mixed",
        [shape(length, columns, F32), message],
        [queries, log_decay, gain, mixed, own_partial, *partials],
        40e6,
    )
    upward_other = swap_core(upward)
    chip_upward = joined(upward, upward_other, True)
    returned = [to_chip(chip_upward, -k) for k in range(1, chips)]
    query_grad, dk_inner, dv_inner = call(
        inner_grad_kernel,
        "inner_grad",
        [shape(length, columns, BF16), shape(length, columns, F32), shape(length, columns, F32)],
        [queries, keys, values, log_decay, grad_mixed, state_in],
        400e6,
    )
    (layer_out,) = call(
        functools.partial(layer_kernel, tensor - 1),
        "layer",
        [shape(length, width, BF16)],
        [where, normed, weight_own, *normed_others, *mine, *theirs],
        2 * length * columns * tensor * width,
        1,
    )
    key_grad, value_grad = call(
        functools.partial(outer_grad_kernel, heads, chips - 1),
        "outer_grad",
        [shape(length, columns, BF16), shape(length, columns, BF16)],
        [where, keys, values, log_decay, dk_inner, dv_inner, upward_other, *returned],
        80e6,
        1,
    )
    return layer_out, query_grad, key_grad, value_grad


def solution(mesh):
    in_specs = (
        P("seq", "tensor"),
        P("seq", "tensor"),
        P("seq", "tensor"),
        P("tensor", "seq"),
        P("tensor"),
        P("tensor", None),
        P("seq", "tensor"),
    )
    out_specs = (P("seq", "tensor"), P("seq", "tensor"), P("seq", "tensor"), P("seq", "tensor"))
    return jax.shard_map(
        on_device, mesh=mesh, in_specs=in_specs, out_specs=out_specs, check_vma=False
    )
```

```python
import functools

import jax
import jax.numpy as jnp
from jax import lax
from jax.experimental import pallas as pl
from jax.experimental.pallas import tpu as pltpu
from jax.sharding import PartitionSpec as P

EXACT = lax.Precision.HIGHEST
EPSILON = 1e-05
F32 = jnp.float32
BF16 = jnp.bfloat16
TAIL = 16
HD = 128

NN = (((1,), (0,)), ((), ()))
NT = (((1,), (1,)), ((), ()))
TN = (((0,), (0,)), ((), ()))


def dot(a, b, dims):
    return lax.dot_general(a, b, dims, preferred_element_type=F32)


def split(x):
    high = x.astype(BF16)
    return high, (x - high.astype(F32)).astype(BF16)


def dot_fb(a, b, dims):
    high, low = split(a)
    return dot(high, b, dims) + dot(low, b, dims)


def dot_bf(a, b, dims):
    high, low = split(b)
    return dot(a, high, dims) + dot(a, low, dims)


def dot_ff(a, b, dims):
    ah, al = split(a)
    bh, bl = split(b)
    return dot(ah, bh, dims) + (dot(ah, bl, dims) + dot(al, bh, dims))


def triangle(length):
    rows = lax.broadcasted_iota(jnp.int32, (length, length), 0)
    cols = lax.broadcasted_iota(jnp.int32, (length, length), 1)
    return rows >= cols


def running_columns(decay, lower):
    return lax.dot_general(lower.astype(F32), decay, NT, precision=EXACT, preferred_element_type=F32)


def running_rows(decay, lower):
    return lax.dot_general(decay, lower.astype(F32), NT, precision=EXACT, preferred_element_type=F32)


def put_total(ref, base, total):
    first = total.astype(BF16).astype(F32)
    second = (total - first).astype(BF16).astype(F32)
    third = total - first - second
    at = lax.broadcasted_iota(jnp.int32, (TAIL, 128), 0)
    tail = jnp.where(at == 0, first, jnp.where(at == 1, second, jnp.where(at == 2, third, 0.0)))
    ref[base : base + TAIL, :] = tail.astype(BF16)


def get_total(ref, base):
    tail = ref[base : base + TAIL, :].astype(F32)
    return tail[0:1] + tail[1:2] + tail[2:3]


def total_of(columns, block):
    length = columns.shape[0]
    return jnp.broadcast_to(columns[length - 1 : length, block : block + 1], (1, HD))


def chip_sum(chip, ref, later):
    chips = ref.shape[0]
    summed = jnp.zeros((HD, HD), F32)
    for number in reversed(range(chips)) if later else range(chips):
        block = ref.at[number]
        joined = jnp.exp(get_total(block, HD)) * summed + block[0:HD, :].astype(F32)
        summed = jnp.where(number > chip if later else number < chip, joined, summed)
    return summed


def put_message(ref, state, total):
    state = state.astype(BF16)
    for number in range(ref.shape[0]):
        block = ref.at[number]
        block[0:HD, :] = state
        put_total(block, HD, total)


def lanes_of(number):
    return pl.ds(pl.multiple_of(number * HD, HD), HD)


def fresh_kernel(
    where_ref, q_ref, k_ref, v_ref, q_got, k_got, v_got, decay_ref, decay_got_ref, q_out, k_out, v_out, col_ref, row_ref, first_ref, message_ref
):
    core = where_ref[0]
    length = q_ref.shape[0]
    for out, ref, got in ((q_out, q_ref, q_got), (k_out, k_ref, k_got), (v_out, v_ref, v_got)):
        out[core] = ref[:, lanes_of(core)]
        out[1 - core] = got[:, lanes_of(core)]
    mine = jnp.where(core == 0, decay_ref[0:1, :], decay_ref[1:2, :])
    theirs = jnp.where(core == 0, decay_got_ref[0:1, :], decay_got_ref[1:2, :])
    block = lax.broadcasted_iota(jnp.int32, (2, length), 0)
    decay = jnp.where(block == core, mine, theirs)
    lower = triangle(length)
    columns = running_columns(decay, lower)
    col_ref[...] = columns
    row_ref[...] = running_rows(decay, lower)
    states = []
    for b in range(2):
        fade = jnp.exp(columns[length - 1 : length, b : b + 1] - columns[:, b : b + 1])
        states.append(dot_bf(k_out[b], fade * v_out[b].astype(F32), TN))
    totals = [total_of(columns, b) for b in range(2)]
    first_ref[...] = states[0]
    put_message(message_ref, jnp.exp(totals[1]) * states[0] + states[1], totals[0] + totals[1])


def weights(columns, across, lower, b):
    return jnp.exp(jnp.where(lower, columns[:, b : b + 1] - across[b : b + 1, :], -1e30))


def inner_kernel(q_ref, k_ref, v_ref, col_ref, row_ref, first_ref, inner_ref):
    columns, across = col_ref[...], row_ref[...]
    lower = triangle(columns.shape[0])
    for b in range(2):
        scores = dot(q_ref[b], k_ref[b], NT) * weights(columns, across, lower, b)
        inner = dot_fb(scores, v_ref[b], NN)
        if b == 1:
            inner = inner + jnp.exp(columns[:, 1:2]) * dot_bf(q_ref[b], first_ref[...], NN)
        inner_ref[b] = inner


def scale_of(mixed):
    return lax.rsqrt(jnp.mean(mixed * mixed, axis=-1, keepdims=True) + EPSILON)


def mixed_kernel(where_ref, q_ref, col_ref, inner_ref, gain_ref, first_ref, chips_ref, mixed_ref, keep_ref, send_ref, state_ref):
    core = where_ref[0]
    columns = col_ref[...]
    gain = gain_ref[:, lanes_of(core)]
    state = chip_sum(where_ref[1], chips_ref, False)
    high, low = split(state)
    shrink = jnp.exp(total_of(columns, 0))
    state_ref[0] = state
    state_ref[1] = shrink * state + first_ref[...]
    normed = []
    for b in range(2):
        grow = jnp.exp(columns[:, b : b + 1])
        if b == 1:
            grow = grow * shrink
        mixed = inner_ref[b] + grow * (dot(q_ref[b], high, NN) + dot(q_ref[b], low, NN))
        mixed_ref[b] = mixed
        normed.append((mixed * scale_of(mixed) * gain))
    keep_ref[...] = jnp.where(core == 0, normed[0], normed[1]).astype(BF16)
    send_ref[...] = jnp.where(core == 0, normed[1], normed[0]).astype(BF16)


def order_kernel(where_ref, keep_ref, got_ref, *out_refs):
    core = where_ref[0]
    for number, ref in enumerate(out_refs):
        part = slice(number * HD, (number + 1) * HD)
        ref[:, lanes_of(core)] = keep_ref[:, part]
        ref[:, lanes_of(1 - core)] = got_ref[:, part]


def own_partial_kernel(where_ref, grad_ref, got_ref, weight_ref, out_ref):
    core = where_ref[0]
    weight = weight_ref[pl.ds(pl.multiple_of(core * HD, HD), HD), :]
    out_ref[core] = dot(grad_ref[...], weight, NT)
    out_ref[1 - core] = dot(got_ref[...], weight, NT)


def partial_kernel(where_ref, grad_ref, got_ref, weight_ref, out_ref):
    core = where_ref[0]
    weight = weight_ref[...]
    out_ref[core] = dot(grad_ref[...], weight, NT).astype(BF16)
    out_ref[1 - core] = dot(got_ref[...], weight, NT).astype(BF16)


def grad_mixed_kernel(where_ref, q_ref, col_ref, gain_ref, mixed_ref, own_ref, *refs):
    part_refs, (grad_ref, second_ref, message_ref) = refs[:-3], refs[-3:]
    columns = col_ref[...]
    gain = gain_ref[:, lanes_of(where_ref[0])]
    ups = []
    for b in range(2):
        normed = own_ref[b]
        for ref in part_refs:
            normed = normed + ref[b].astype(F32)
        lifted = normed * gain
        mixed = mixed_ref[b]
        scale = scale_of(mixed)
        unit = mixed * scale
        grad = scale * (lifted - unit * jnp.mean(unit * lifted, axis=-1, keepdims=True))
        grad_ref[b] = grad
        ups.append(dot_bf(q_ref[b], jnp.exp(columns[:, b : b + 1]) * grad, TN))
    second_ref[...] = ups[1]
    totals = [total_of(columns, b) for b in range(2)]
    put_message(message_ref, ups[0] + jnp.exp(totals[0]) * ups[1], totals[0] + totals[1])


def inner_grad_kernel(
    where_ref, q_ref, k_ref, v_ref, col_ref, row_ref, grad_ref, state_ref, second_ref, keep_ref, send_ref, dk_ref, dv_ref
):
    core = where_ref[0]
    columns, across = col_ref[...], row_ref[...]
    length = columns.shape[0]
    lower = triangle(length)
    queries = []
    for b in range(2):
        q, k, v, grad = q_ref[b], k_ref[b], v_ref[b], grad_ref[b]
        weight = weights(columns, across, lower, b)
        scores = dot(q, k, NT) * weight
        grad_scores = dot_fb(grad, v, NT) * weight
        carried = jnp.exp(columns[:, b : b + 1]) * dot_ff(grad, state_ref[b], NT)
        queries.append(dot_fb(grad_scores, k, NN) + carried)
        dk = dot_fb(grad_scores, q, TN)
        dv = dot_ff(scores, grad, TN)
        if b == 0:
            fade = jnp.exp(columns[length - 1 : length, 0:1] - columns[:, 0:1])
            dk = dk + fade * dot_bf(v, second_ref[...], NT)
            dv = dv + fade * dot_bf(k, second_ref[...], NN)
        dk_ref[b] = dk
        dv_ref[b] = dv
    keep_ref[...] = jnp.where(core == 0, queries[0], queries[1]).astype(BF16)
    send_ref[...] = jnp.where(core == 0, queries[1], queries[0]).astype(BF16)


def outer_grad_kernel(where_ref, k_ref, v_ref, col_ref, dk_ref, dv_ref, chips_ref, keep_ref, send_ref):
    core = where_ref[0]
    columns = col_ref[...]
    length = columns.shape[0]
    high, low = split(chip_sum(where_ref[1], chips_ref, True))
    keys, values = [], []
    for b in range(2):
        fade = jnp.exp(columns[length - 1 : length, b : b + 1] - columns[:, b : b + 1])
        if b == 0:
            fade = fade * jnp.exp(total_of(columns, 1))
        keys.append(dk_ref[b] + fade * (dot(v_ref[b], high, NT) + dot(v_ref[b], low, NT)))
        values.append(dv_ref[b] + fade * (dot(k_ref[b], high, NN) + dot(k_ref[b], low, NN)))
    for number, pair in enumerate((keys, values)):
        part = slice(number * HD, (number + 1) * HD)
        keep_ref[:, part] = jnp.where(core == 0, pair[0], pair[1]).astype(BF16)
        send_ref[:, part] = jnp.where(core == 0, pair[1], pair[0]).astype(BF16)


def layer_kernel(others, where_ref, normed_ref, weight_ref, *refs):
    normed_refs = refs[:others]
    mine_refs = refs[others : 2 * others]
    theirs_refs = refs[2 * others : 3 * others]
    out_ref = refs[3 * others]
    core = where_ref[0]
    width = weight_ref.shape[1]
    step = 384 if width % 384 == 0 else 128
    for begin in range(0, width, step):
        lanes = slice(begin, begin + step)
        total = dot(normed_ref[...], weight_ref[:, lanes], NN)
        for k in range(others):
            total = total + dot(normed_refs[k][:, lanes_of(core)], mine_refs[k][:, lanes], NN)
            total = total + dot(normed_refs[k][:, lanes_of(1 - core)], theirs_refs[k][:, lanes], NN)
        out_ref[:, lanes] = total.astype(BF16)


SMEM = pl.BlockSpec(memory_space=pltpu.SMEM)
VMEM = pl.BlockSpec(memory_space=pltpu.VMEM)


def call(kernel, name, outs, args):
    return pl.pallas_call(
        kernel,
        name=name,
        out_shape=outs,
        in_specs=[SMEM] + [VMEM] * (len(args) - 1),
        out_specs=[VMEM] * len(outs),
        compiler_params=pltpu.CompilerParams(vmem_limit_bytes=40 * 2**20),
        cost_estimate=pl.CostEstimate(flops=1, bytes_accessed=1, transcendentals=0),
    )(*args)


def without_where(kernel):
    return lambda where_ref, *refs: kernel(*refs)


def after(values, *earlier):
    tied = lax.optimization_barrier((tuple(values), earlier))
    return list(tied[0])


def on_device(queries, keys, values, log_decay, norm_gain, out_weight, out_grad):
    length, columns = queries.shape
    seq = lax.axis_size("seq")
    tensor = lax.axis_size("tensor")
    chips = seq // 2
    model = out_weight.shape[1]
    width = model // tensor
    place = lax.axis_index("tensor")
    core = lax.rem(lax.axis_index("seq"), 2)
    where = jnp.stack([core, lax.axis_index("seq") // 2]).astype(jnp.int32)
    gain = norm_gain.reshape(1, columns)

    def swap_tensor(value, k):
        return lax.ppermute(value, "tensor", [(i, i ^ k) for i in range(tensor)])

    def swap_core(value):
        return lax.ppermute(value, "seq", [(i, i ^ 1) for i in range(seq)])

    def swap_chips(value):
        groups = [[i for i in range(seq) if i % 2 == side] for side in range(2)]
        return lax.all_to_all(value, "seq", 0, 0, axis_index_groups=groups)

    def shape(dtype, *dims):
        return jax.ShapeDtypeStruct(dims, dtype)

    others = range(1, tensor)
    message = shape(BF16, chips, HD + TAIL, HD)
    pair16 = shape(BF16, 2, length, HD)
    pair32 = shape(F32, 2, length, HD)
    one16 = shape(BF16, length, HD)
    both16 = shape(BF16, length, columns)

    slices = [
        lax.dynamic_slice(out_weight, (core * HD, (place ^ step) * width), (HD, width))
        for step in others
    ]
    mine = [swap_tensor(piece, step) for piece, step in zip(slices, others)]
    got = [swap_core(rows) for rows in (queries, keys, values)]
    decay_got = swap_core(log_decay)
    (out_grad,) = after([out_grad], *slices)
    grad_got = swap_core(out_grad)
    q, k, v, col, row, first, fresh = call(
        fresh_kernel,
        "fresh",
        [pair16, pair16, pair16, shape(F32, length, 2), shape(F32, 2, length), shape(F32, HD, HD), message],
        [where, queries, keys, values, *got, log_decay, decay_got],
    )
    arrived = swap_chips(fresh)
    (inner,) = call(without_where(inner_kernel), "inner", [pair32], [where, q, k, v, col, row, first])
    weight_own = lax.dynamic_slice(out_weight, (0, place * width), (columns, width))
    (own_partial,) = call(own_partial_kernel, "own_partial", [pair32], [where, out_grad, grad_got, weight_own])
    (arrived,) = after([arrived], inner, own_partial)
    mixed, normed_keep, normed_send, states = call(
        mixed_kernel,
        "mixed",
        [pair32, one16, one16, shape(F32, 2, HD, HD)],
        [where, q, col, inner, gain, first, arrived],
    )
    normed_got = swap_core(normed_send)
    (normed,) = call(order_kernel, "order", [both16], [where, normed_keep, normed_got])
    partials, theirs = [], []
    for number, piece in enumerate(mine):
        (piece,) = after([piece], mixed if number else arrived, *partials, *theirs[: max(number - 1, 0)])
        theirs.append(swap_core(piece))
        (partial,) = call(partial_kernel, "partial", [pair16], [where, out_grad, grad_got, piece])
        partials.append(partial)
    sent = [swap_tensor(partial, step) for partial, step in zip(partials, others)]
    sent = after(sent, *theirs)
    grad_mixed, second, upward = call(
        grad_mixed_kernel,
        "grad_mixed",
        [pair32, shape(F32, HD, HD), message],
        [where, q, col, gain, mixed, own_partial, *sent],
    )
    returned = swap_chips(upward)
    (normed,) = after([normed], grad_mixed)
    normed_others = [swap_tensor(normed, step) for step in others]
    dq_keep, dq_send, dk_inner, dv_inner = call(
        inner_grad_kernel,
        "inner_grad",
        [one16, one16, pair32, pair32],
        [where, q, k, v, col, row, grad_mixed, states, second],
    )
    dq_got = swap_core(dq_send)
    (layer_out,) = call(
        functools.partial(layer_kernel, tensor - 1),
        "layer",
        [shape(BF16, length, width)],
        [where, normed, weight_own, *normed_others, *mine, *theirs],
    )
    (query_grad,) = call(order_kernel, "order", [both16], [where, dq_keep, dq_got])
    keep, send = call(
        outer_grad_kernel,
        "outer_grad",
        [both16, both16],
        [where, k, v, col, dk_inner, dv_inner, returned],
    )
    got = swap_core(send)
    key_grad, value_grad = call(order_kernel, "order", [both16, both16], [where, keep, got])
    return layer_out, query_grad, key_grad, value_grad


def solution(mesh):
    in_specs = (
        P("seq", "tensor"),
        P("seq", "tensor"),
        P("seq", "tensor"),
        P("tensor", "seq"),
        P("tensor"),
        P("tensor", None),
        P("seq", "tensor"),
    )
    out_specs = (P("seq", "tensor"), P("seq", "tensor"), P("seq", "tensor"), P("seq", "tensor"))
    return jax.shard_map(
        on_device, mesh=mesh, in_specs=in_specs, out_specs=out_specs, check_vma=False
    )
```

```python
import functools

import jax
import jax.numpy as jnp
from jax import lax
from jax.experimental import pallas as pl
from jax.experimental.pallas import tpu as pltpu
from jax.sharding import PartitionSpec as P

EXACT = lax.Precision.HIGHEST
EPSILON = 1e-05
F32 = jnp.float32
BF16 = jnp.bfloat16
TAIL = 16
HD = 128

NN = (((1,), (0,)), ((), ()))
NT = (((1,), (1,)), ((), ()))
TN = (((0,), (0,)), ((), ()))


def dot(a, b, dims):
    return lax.dot_general(a, b, dims, preferred_element_type=F32)


def split(x):
    high = x.astype(BF16)
    return high, (x - high.astype(F32)).astype(BF16)


def dot_fb(a, b, dims):
    high, low = split(a)
    return dot(high, b, dims) + dot(low, b, dims)


def dot_bf(a, b, dims):
    high, low = split(b)
    return dot(a, high, dims) + dot(a, low, dims)


def dot_ff(a, b, dims):
    ah, al = split(a)
    bh, bl = split(b)
    return dot(ah, bh, dims) + (dot(ah, bl, dims) + dot(al, bh, dims))


def triangle(length):
    rows = lax.broadcasted_iota(jnp.int32, (length, length), 0)
    cols = lax.broadcasted_iota(jnp.int32, (length, length), 1)
    return rows >= cols


def running_columns(decay, lower):
    return lax.dot_general(lower.astype(F32), decay, NT, precision=EXACT, preferred_element_type=F32)


def running_rows(decay, lower):
    return lax.dot_general(decay, lower.astype(F32), NT, precision=EXACT, preferred_element_type=F32)


def put_total(ref, base, total):
    first = total.astype(BF16).astype(F32)
    second = (total - first).astype(BF16).astype(F32)
    third = total - first - second
    at = lax.broadcasted_iota(jnp.int32, (TAIL, 128), 0)
    tail = jnp.where(at == 0, first, jnp.where(at == 1, second, jnp.where(at == 2, third, 0.0)))
    ref[base : base + TAIL, :] = tail.astype(BF16)


def get_total(ref, base):
    tail = ref[base : base + TAIL, :].astype(F32)
    return tail[0:1] + tail[1:2] + tail[2:3]


def total_of(columns, block):
    length = columns.shape[0]
    return jnp.broadcast_to(columns[length - 1 : length, block : block + 1], (1, HD))


def chip_sum(refs):
    summed = jnp.zeros((HD, HD), F32)
    passed = jnp.zeros((1, HD), F32)
    for ref in refs:
        summed = summed + jnp.exp(passed) * ref[0:HD, :].astype(F32)
        passed = passed + get_total(ref, HD)
    return summed


def put_message(ref, state, total):
    ref[0:HD, :] = state.astype(BF16)
    put_total(ref, HD, total)


def join_kernel(own_ref, got_ref, out_ref):
    total = get_total(own_ref, HD)
    state = own_ref[0:HD, :].astype(F32) + jnp.exp(total) * got_ref[0:HD, :].astype(F32)
    put_message(out_ref, state, total + get_total(got_ref, HD))


def stitch_kernel(where_ref, mine_ref, theirs_ref, out_ref):
    side = where_ref[1]
    rows = mine_ref.shape[0]
    out_ref[pl.ds(pl.multiple_of(side * rows, rows), rows), :] = mine_ref[...]
    out_ref[pl.ds(pl.multiple_of((1 - side) * rows, rows), rows), :] = theirs_ref[...]


def lanes_of(number):
    return pl.ds(pl.multiple_of(number * HD, HD), HD)


def fresh_kernel(
    where_ref, q_ref, k_ref, v_ref, q_got, k_got, v_got, decay_ref, decay_got_ref, q_out, k_out, v_out, col_ref, row_ref, first_ref, message_ref
):
    core = where_ref[0]
    length = q_ref.shape[0]
    for out, ref, got in ((q_out, q_ref, q_got), (k_out, k_ref, k_got), (v_out, v_ref, v_got)):
        out[core] = ref[:, lanes_of(core)]
        out[1 - core] = got[:, lanes_of(core)]
    mine = jnp.where(core == 0, decay_ref[0:1, :], decay_ref[1:2, :])
    theirs = jnp.where(core == 0, decay_got_ref[0:1, :], decay_got_ref[1:2, :])
    block = lax.broadcasted_iota(jnp.int32, (2, length), 0)
    decay = jnp.where(block == core, mine, theirs)
    lower = triangle(length)
    columns = running_columns(decay, lower)
    col_ref[...] = columns
    row_ref[...] = running_rows(decay, lower)
    states = []
    for b in range(2):
        fade = jnp.exp(columns[length - 1 : length, b : b + 1] - columns[:, b : b + 1])
        states.append(dot_bf(k_out[b], fade * v_out[b].astype(F32), TN))
    totals = [total_of(columns, b) for b in range(2)]
    first_ref[...] = states[0]
    put_message(message_ref, jnp.exp(totals[1]) * states[0] + states[1], totals[0] + totals[1])


def weights(columns, across, lower, b):
    return jnp.exp(jnp.where(lower, columns[:, b : b + 1] - across[b : b + 1, :], -1e30))


def inner_kernel(q_ref, k_ref, v_ref, col_ref, row_ref, first_ref, inner_ref):
    columns, across = col_ref[...], row_ref[...]
    lower = triangle(columns.shape[0])
    for b in range(2):
        scores = dot(q_ref[b], k_ref[b], NT) * weights(columns, across, lower, b)
        inner = dot_fb(scores, v_ref[b], NN)
        if b == 1:
            inner = inner + jnp.exp(columns[:, 1:2]) * dot_bf(q_ref[b], first_ref[...], NN)
        inner_ref[b] = inner


def scale_of(mixed):
    return lax.rsqrt(jnp.mean(mixed * mixed, axis=-1, keepdims=True) + EPSILON)


def mixed_kernel(where_ref, q_ref, col_ref, inner_ref, gain_ref, first_ref, *refs):
    chip_refs, (mixed_ref, keep_ref, send_ref, state_ref) = refs[:-4], refs[-4:]
    core = where_ref[0]
    columns = col_ref[...]
    gain = gain_ref[:, lanes_of(core)]
    state = chip_sum(chip_refs)
    high, low = split(state)
    shrink = jnp.exp(total_of(columns, 0))
    state_ref[0] = state
    state_ref[1] = shrink * state + first_ref[...]
    normed = []
    for b in range(2):
        grow = jnp.exp(columns[:, b : b + 1])
        if b == 1:
            grow = grow * shrink
        mixed = inner_ref[b] + grow * (dot(q_ref[b], high, NN) + dot(q_ref[b], low, NN))
        mixed_ref[b] = mixed
        normed.append((mixed * scale_of(mixed) * gain))
    keep_ref[...] = jnp.where(core == 0, normed[0], normed[1]).astype(BF16)
    send_ref[...] = jnp.where(core == 0, normed[1], normed[0]).astype(BF16)


def order_kernel(where_ref, keep_ref, got_ref, *out_refs):
    core = where_ref[0]
    for number, ref in enumerate(out_refs):
        part = slice(number * HD, (number + 1) * HD)
        ref[:, lanes_of(core)] = keep_ref[:, part]
        ref[:, lanes_of(1 - core)] = got_ref[:, part]


def partial_kernel(where_ref, grad_ref, got_ref, *refs):
    core = where_ref[0]
    first_ref, second_ref, first_out, second_out = refs
    first = first_ref[pl.ds(pl.multiple_of(core * HD, HD), HD), :] if first_ref.shape[0] > HD else first_ref[...]
    weight = jnp.concatenate([first, second_ref[...]], axis=0)
    for block, ref in ((core, grad_ref), (1 - core, got_ref)):
        product = dot(ref[...], weight, NT)
        first_out[block] = product[:, :HD].astype(first_out.dtype)
        second_out[block] = product[:, HD:].astype(second_out.dtype)


def grad_mixed_kernel(where_ref, q_ref, col_ref, gain_ref, mixed_ref, own_ref, *refs):
    part_refs, (grad_ref, second_ref, message_ref) = refs[:-3], refs[-3:]
    columns = col_ref[...]
    gain = gain_ref[:, lanes_of(where_ref[0])]
    ups = []
    for b in range(2):
        normed = own_ref[b]
        for ref in part_refs:
            normed = normed + ref[b].astype(F32)
        lifted = normed * gain
        mixed = mixed_ref[b]
        scale = scale_of(mixed)
        unit = mixed * scale
        grad = scale * (lifted - unit * jnp.mean(unit * lifted, axis=-1, keepdims=True))
        grad_ref[b] = grad
        ups.append(dot_bf(q_ref[b], jnp.exp(columns[:, b : b + 1]) * grad, TN))
    second_ref[...] = ups[1]
    totals = [total_of(columns, b) for b in range(2)]
    put_message(message_ref, ups[0] + jnp.exp(totals[0]) * ups[1], totals[0] + totals[1])


def inner_grad_kernel(
    where_ref, q_ref, k_ref, v_ref, col_ref, row_ref, grad_ref, state_ref, second_ref, keep_ref, send_ref, dk_ref, dv_ref
):
    core = where_ref[0]
    columns, across = col_ref[...], row_ref[...]
    length = columns.shape[0]
    lower = triangle(length)
    queries = []
    for b in range(2):
        q, k, v, grad = q_ref[b], k_ref[b], v_ref[b], grad_ref[b]
        weight = weights(columns, across, lower, b)
        scores = dot(q, k, NT) * weight
        grad_scores = dot_fb(grad, v, NT) * weight
        carried = jnp.exp(columns[:, b : b + 1]) * dot_ff(grad, state_ref[b], NT)
        queries.append(dot_fb(grad_scores, k, NN) + carried)
        dk = dot_fb(grad_scores, q, TN)
        dv = dot_ff(scores, grad, TN)
        if b == 0:
            fade = jnp.exp(columns[length - 1 : length, 0:1] - columns[:, 0:1])
            dk = dk + fade * dot_bf(v, second_ref[...], NT)
            dv = dv + fade * dot_bf(k, second_ref[...], NN)
        dk_ref[b] = dk
        dv_ref[b] = dv
    keep_ref[...] = jnp.where(core == 0, queries[0], queries[1]).astype(BF16)
    send_ref[...] = jnp.where(core == 0, queries[1], queries[0]).astype(BF16)


def outer_grad_kernel(where_ref, k_ref, v_ref, col_ref, dk_ref, dv_ref, *refs):
    chip_refs, (keep_ref, send_ref) = refs[:-2], refs[-2:]
    core = where_ref[0]
    columns = col_ref[...]
    length = columns.shape[0]
    high, low = split(chip_sum(chip_refs))
    keys, values = [], []
    for b in range(2):
        fade = jnp.exp(columns[length - 1 : length, b : b + 1] - columns[:, b : b + 1])
        if b == 0:
            fade = fade * jnp.exp(total_of(columns, 1))
        keys.append(dk_ref[b] + fade * (dot(v_ref[b], high, NT) + dot(v_ref[b], low, NT)))
        values.append(dv_ref[b] + fade * (dot(k_ref[b], high, NN) + dot(k_ref[b], low, NN)))
    for number, pair in enumerate((keys, values)):
        part = slice(number * HD, (number + 1) * HD)
        keep_ref[:, part] = jnp.where(core == 0, pair[0], pair[1]).astype(BF16)
        send_ref[:, part] = jnp.where(core == 0, pair[1], pair[0]).astype(BF16)


def layer_kernel(others, where_ref, normed_ref, weight_ref, *refs):
    normed_refs = refs[:others]
    mine_refs = refs[others : 2 * others]
    theirs_refs = refs[2 * others : 3 * others]
    out_ref = refs[3 * others]
    core = where_ref[0]
    width = weight_ref.shape[1]
    step = 384 if width % 384 == 0 else 128
    for begin in range(0, width, step):
        lanes = slice(begin, begin + step)
        total = dot(normed_ref[...], weight_ref[:, lanes], NN)
        for k in range(others):
            total = total + dot(normed_refs[k][:, lanes_of(core)], mine_refs[k][:, lanes], NN)
            total = total + dot(normed_refs[k][:, lanes_of(1 - core)], theirs_refs[k][:, lanes], NN)
        out_ref[:, lanes] = total.astype(BF16)


SMEM = pl.BlockSpec(memory_space=pltpu.SMEM)
VMEM = pl.BlockSpec(memory_space=pltpu.VMEM)


def call(kernel, name, outs, args):
    return pl.pallas_call(
        kernel,
        name=name,
        out_shape=outs,
        in_specs=[SMEM] + [VMEM] * (len(args) - 1),
        out_specs=[VMEM] * len(outs),
        compiler_params=pltpu.CompilerParams(vmem_limit_bytes=16 * 2**20),
        cost_estimate=pl.CostEstimate(flops=1, bytes_accessed=1, transcendentals=0),
    )(*args)


def without_where(kernel):
    return lambda where_ref, *refs: kernel(*refs)


def after(values, *earlier):
    tied = lax.optimization_barrier((tuple(values), earlier))
    return list(tied[0])


def on_device(queries, keys, values, log_decay, norm_gain, out_weight, out_grad):
    length, columns = queries.shape
    seq = lax.axis_size("seq")
    tensor = lax.axis_size("tensor")
    chips = seq // 2
    model = out_weight.shape[1]
    width = model // tensor
    place = lax.axis_index("tensor")
    core = lax.rem(lax.axis_index("seq"), 2)
    side = lax.rem(lax.axis_index("seq") // 2, 2)
    where = jnp.stack([core, side]).astype(jnp.int32)
    gain = norm_gain.reshape(1, columns)

    def swap_tensor(value, k):
        return lax.ppermute(value, "tensor", [(i, i ^ k) for i in range(tensor)])

    def swap_core(value):
        return lax.ppermute(value, "seq", [(i, i ^ 1) for i in range(seq)])

    def swap_side(value):
        return lax.ppermute(value, "seq", [(i, i ^ 2) for i in range(seq)])

    def to_chip(value, step):
        return lax.ppermute(
            value, "seq", [(i, i + 2 * step) for i in range(seq) if 0 <= i + 2 * step < seq]
        )

    def carry(own, sign):
        messages = []
        step = 1
        while step < chips:
            messages.append(to_chip(own, sign * step))
            step *= 2
            if step < chips:
                (own,) = call(without_where(join_kernel), "join", [message], [where, own, messages[-1]])
        return messages

    def shape(dtype, *dims):
        return jax.ShapeDtypeStruct(dims, dtype)

    others = range(1, tensor)
    message = shape(BF16, HD + TAIL, HD)
    pair16 = shape(BF16, 2, length, HD)
    pair32 = shape(F32, 2, length, HD)
    one16 = shape(BF16, length, HD)
    both16 = shape(BF16, length, columns)

    far = [step for step in others if step & (step - 1)]
    near = [step for step in others if not step & (step - 1)]
    order = far + near

    def fetch(step, source):
        rows = HD // 2 if step in far else HD
        begin = core * HD + side * rows if step in far else core * HD
        piece = lax.dynamic_slice(source, (begin, (place ^ step) * width), (rows, width))
        return piece, swap_tensor(piece, step)

    slices, arriving = [], []
    for step in order:
        (source,) = after([out_weight], *slices[-1:])
        piece, coming = fetch(step, source)
        slices.append(piece)
        arriving.append(coming)
    got = [swap_core(rows) for rows in (queries, keys, values)]
    decay_got = swap_core(log_decay)
    (out_grad,) = after([out_grad], *slices)
    grad_got = swap_core(out_grad)
    got = after(got, grad_got)
    q, k, v, col, row, first, fresh = call(
        fresh_kernel,
        "fresh",
        [pair16, pair16, pair16, shape(F32, length, 2), shape(F32, 2, length), shape(F32, HD, HD), message],
        [where, queries, keys, values, *got, log_decay, decay_got],
    )
    arrived = [to_chip(fresh, step) for step in range(1, chips)]
    (inner,) = call(without_where(inner_kernel), "inner", [pair32], [where, q, k, v, col, row, first])
    weight_own = lax.dynamic_slice(out_weight, (0, place * width), (columns, width))
    mine = []
    for step, piece in zip(order, arriving):
        if step in far:
            (piece,) = call(stitch_kernel, "stitch", [shape(BF16, HD, width)], [where, piece, swap_side(piece)])
        mine.append(piece)
    mixed, normed_keep, normed_send, states = call(
        mixed_kernel,
        "mixed",
        [pair32, one16, one16, shape(F32, 2, HD, HD)],
        [where, q, col, inner, gain, first, *arrived],
    )
    normed_got = swap_core(normed_send)
    (normed,) = call(order_kernel, "order", [both16], [where, normed_keep, normed_got])
    pieces = [weight_own, *mine]
    partials, theirs = [], []
    for number in range(0, tensor, 2):
        pair = after(pieces[number : number + 2], mixed if number else arrived[-1], *partials)
        theirs += [swap_core(piece) for piece in (pair if number else pair[1:])]
        partials += call(
            partial_kernel,
            "partial",
            [pair16 if number else pair32, pair16],
            [where, out_grad, grad_got, *pair],
        )
    own_partial, *partials = partials
    sent = [swap_tensor(partial, step) for partial, step in zip(partials, order)]
    sent = after(sent, *theirs)
    grad_mixed, second, upward = call(
        grad_mixed_kernel,
        "grad_mixed",
        [pair32, shape(F32, HD, HD), message],
        [where, q, col, gain, mixed, own_partial, *sent],
    )
    returned = carry(upward, -1)
    (normed,) = after([normed], *partials)
    normed_others = [swap_tensor(normed, step) for step in order]
    dq_keep, dq_send, dk_inner, dv_inner = call(
        inner_grad_kernel,
        "inner_grad",
        [one16, one16, pair32, pair32],
        [where, q, k, v, col, row, grad_mixed, states, second],
    )
    dq_got = swap_core(dq_send)
    (layer_out,) = call(
        functools.partial(layer_kernel, tensor - 1),
        "layer",
        [shape(BF16, length, width)],
        [where, normed, weight_own, *normed_others, *mine, *theirs],
    )
    (query_grad,) = call(order_kernel, "order", [both16], [where, dq_keep, dq_got])
    keep, send = call(
        outer_grad_kernel,
        "outer_grad",
        [both16, both16],
        [where, k, v, col, dk_inner, dv_inner, *returned],
    )
    got = swap_core(send)
    key_grad, value_grad = call(order_kernel, "order", [both16, both16], [where, keep, got])
    return layer_out, query_grad, key_grad, value_grad


def solution(mesh):
    in_specs = (
        P("seq", "tensor"),
        P("seq", "tensor"),
        P("seq", "tensor"),
        P("tensor", "seq"),
        P("tensor"),
        P("tensor", None),
        P("seq", "tensor"),
    )
    out_specs = (P("seq", "tensor"), P("seq", "tensor"), P("seq", "tensor"), P("seq", "tensor"))
    return jax.shard_map(
        on_device, mesh=mesh, in_specs=in_specs, out_specs=out_specs, check_vma=False
    )
```

```python
import functools

import jax
import jax.numpy as jnp
from jax import lax
from jax.experimental import pallas as pl
from jax.experimental.pallas import tpu as pltpu
from jax.sharding import PartitionSpec as P

EXACT = lax.Precision.HIGHEST
EPSILON = 1e-05
F32 = jnp.float32
BF16 = jnp.bfloat16
TAIL = 16
HD = 128

NN = (((1,), (0,)), ((), ()))
NT = (((1,), (1,)), ((), ()))
TN = (((0,), (0,)), ((), ()))


def dot(a, b, dims):
    return lax.dot_general(a, b, dims, preferred_element_type=F32)


def split(x):
    high = x.astype(BF16)
    return high, (x - high.astype(F32)).astype(BF16)


def dot_fb(a, b, dims):
    high, low = split(a)
    return dot(high, b, dims) + dot(low, b, dims)


def dot_bf(a, b, dims):
    high, low = split(b)
    return dot(a, high, dims) + dot(a, low, dims)


def dot_ff(a, b, dims):
    ah, al = split(a)
    bh, bl = split(b)
    return dot(ah, bh, dims) + (dot(ah, bl, dims) + dot(al, bh, dims))


def triangle(length):
    rows = lax.broadcasted_iota(jnp.int32, (length, length), 0)
    cols = lax.broadcasted_iota(jnp.int32, (length, length), 1)
    return rows >= cols


def running_columns(decay, lower):
    return lax.dot_general(lower.astype(F32), decay, NT, precision=EXACT, preferred_element_type=F32)


def running_rows(decay, lower):
    return lax.dot_general(decay, lower.astype(F32), NT, precision=EXACT, preferred_element_type=F32)


def put_total(ref, base, total):
    first = total.astype(BF16).astype(F32)
    second = (total - first).astype(BF16).astype(F32)
    third = total - first - second
    at = lax.broadcasted_iota(jnp.int32, (TAIL, 128), 0)
    tail = jnp.where(at == 0, first, jnp.where(at == 1, second, jnp.where(at == 2, third, 0.0)))
    ref[base : base + TAIL, :] = tail.astype(BF16)


def get_total(ref, base):
    tail = ref[base : base + TAIL, :].astype(F32)
    return tail[0:1] + tail[1:2] + tail[2:3]


def total_of(columns, block):
    length = columns.shape[0]
    return jnp.broadcast_to(columns[length - 1 : length, block : block + 1], (1, HD))


def chip_sum(refs):
    summed = jnp.zeros((HD, HD), F32)
    passed = jnp.zeros((1, HD), F32)
    for ref in refs:
        summed = summed + jnp.exp(passed) * ref[0:HD, :].astype(F32)
        passed = passed + get_total(ref, HD)
    return summed


def put_message(ref, state, total):
    ref[0:HD, :] = state.astype(BF16)
    put_total(ref, HD, total)


def lanes_of(number):
    return pl.ds(pl.multiple_of(number * HD, HD), HD)


def rows_of(number, count):
    return pl.ds(pl.multiple_of(number * count, count), count)


def stage_kernel(plan, where_ref, decay_source, weight_ref, q_ref, k_ref, v_ref, *refs):
    *piece_refs, own_ref, send_ref, keep_ref, decay_ref, tail_ref, sems = refs
    core, side, place = where_ref[0], where_ref[1], where_ref[2]
    width = own_ref.shape[1]
    length = keep_ref.shape[0]
    copies = []

    def start(source, target):
        copies.append(pltpu.make_async_copy(source, target, sems.at[len(copies)]))
        copies[-1].start()

    start(decay_source, decay_ref)
    for (step, halves), ref in zip(plan, piece_refs):
        rows = rows_of(core * 2 + side if halves else core, ref.shape[0])
        start(weight_ref.at[rows, rows_of(place ^ step, width)], ref)
    for number, source in enumerate((q_ref, k_ref, v_ref)):
        part = slice(number * HD, (number + 1) * HD)
        start(source.at[:, lanes_of(1 - core)], send_ref.at[0:length, part])
        start(source.at[:, lanes_of(core)], keep_ref.at[:, part])
    start(weight_ref.at[:, rows_of(place, width)], own_ref)
    copies[0].wait()
    decay = jnp.where(core == 0, decay_ref[1:2, :], decay_ref[0:1, :])
    first = decay.astype(BF16).astype(F32)
    second = (decay - first).astype(BF16).astype(F32)
    third = decay - first - second
    at = lax.broadcasted_iota(jnp.int32, (TAIL, length), 0)
    tail = jnp.where(at == 0, first, jnp.where(at == 1, second, jnp.where(at == 2, third, 0.0)))
    tail_ref[...] = jnp.zeros(tail_ref.shape, BF16)
    tail_ref[:, 0:length] = tail.astype(BF16)
    start(tail_ref, send_ref.at[length : length + TAIL, :])
    for copy in copies[1:]:
        copy.wait()


def fresh_kernel(where_ref, keep_ref, got_ref, decay_ref, q_out, k_out, v_out, col_ref, row_ref, first_ref, message_ref):
    core = where_ref[0]
    length = keep_ref.shape[0]
    for number, out in enumerate((q_out, k_out, v_out)):
        part = slice(number * HD, (number + 1) * HD)
        out[core] = keep_ref[:, part]
        out[1 - core] = got_ref[0:length, part]
    mine = jnp.where(core == 0, decay_ref[0:1, :], decay_ref[1:2, :])
    tail = got_ref[length : length + TAIL, 0:length].astype(F32)
    theirs = tail[0:1] + tail[1:2] + tail[2:3]
    block = lax.broadcasted_iota(jnp.int32, (2, length), 0)
    decay = jnp.where(block == core, mine, theirs)
    lower = triangle(length)
    columns = running_columns(decay, lower)
    col_ref[...] = columns
    row_ref[...] = running_rows(decay, lower)
    states = []
    for b in range(2):
        fade = jnp.exp(columns[length - 1 : length, b : b + 1] - columns[:, b : b + 1])
        states.append(dot_bf(k_out[b], fade * v_out[b].astype(F32), TN))
    totals = [total_of(columns, b) for b in range(2)]
    first_ref[...] = states[0]
    put_message(message_ref, jnp.exp(totals[1]) * states[0] + states[1], totals[0] + totals[1])


def weights(columns, across, lower, b):
    return jnp.exp(jnp.where(lower, columns[:, b : b + 1] - across[b : b + 1, :], -1e30))


def inner_kernel(q_ref, k_ref, v_ref, col_ref, row_ref, first_ref, inner_ref):
    columns, across = col_ref[...], row_ref[...]
    lower = triangle(columns.shape[0])
    for b in range(2):
        scores = dot(q_ref[b], k_ref[b], NT) * weights(columns, across, lower, b)
        inner = dot_fb(scores, v_ref[b], NN)
        if b == 1:
            inner = inner + jnp.exp(columns[:, 1:2]) * dot_bf(q_ref[b], first_ref[...], NN)
        inner_ref[b] = inner


def scale_of(mixed):
    return lax.rsqrt(jnp.mean(mixed * mixed, axis=-1, keepdims=True) + EPSILON)


def mixed_kernel(where_ref, q_ref, col_ref, inner_ref, gain_ref, first_ref, *refs):
    chip_refs, (mixed_ref, normed_ref, state_ref) = refs[:-3], refs[-3:]
    core = where_ref[0]
    columns = col_ref[...]
    gain = gain_ref[:, lanes_of(core)]
    state = chip_sum(chip_refs)
    high, low = split(state)
    shrink = jnp.exp(total_of(columns, 0))
    state_ref[0] = state
    state_ref[1] = shrink * state + first_ref[...]
    for b in range(2):
        grow = jnp.exp(columns[:, b : b + 1])
        if b == 1:
            grow = grow * shrink
        mixed = inner_ref[b] + grow * (dot(q_ref[b], high, NN) + dot(q_ref[b], low, NN))
        mixed_ref[b] = mixed
        normed_ref[b] = (mixed * scale_of(mixed) * gain).astype(BF16)


def partial_kernel(kinds, where_ref, grad_ref, got_ref, *refs):
    core, side = where_ref[0], where_ref[1]
    refs = list(refs)
    inputs = [[refs.pop(0) for _ in range(2 if kind == "halves" else 1)] for kind in kinds]
    products = [refs.pop(0), refs.pop(0)]
    weights = []
    for kind, sources in zip(kinds, inputs):
        if kind == "own":
            weights.append(sources[0][rows_of(core, HD), :])
        elif kind == "halves":
            mine, theirs = sources[0][...], sources[1][...]
            weight = jnp.concatenate([jnp.where(side == 0, mine, theirs), jnp.where(side == 0, theirs, mine)], axis=0)
            refs.pop(0)[...] = weight
            weights.append(weight)
        else:
            weights.append(sources[0][...])
    weight = jnp.concatenate(weights, axis=0)
    for block, ref in ((core, grad_ref), (1 - core, got_ref)):
        product = dot(ref[...], weight, NT)
        for number, out in enumerate(products):
            out[block] = product[:, number * HD : (number + 1) * HD].astype(out.dtype)


def grad_mixed_kernel(where_ref, q_ref, col_ref, gain_ref, mixed_ref, own_ref, *refs):
    part_refs, (grad_ref, second_ref, message_ref) = refs[:-3], refs[-3:]
    columns = col_ref[...]
    gain = gain_ref[:, lanes_of(where_ref[0])]
    ups = []
    for b in range(2):
        normed = own_ref[b]
        for ref in part_refs:
            normed = normed + ref[b].astype(F32)
        lifted = normed * gain
        mixed = mixed_ref[b]
        scale = scale_of(mixed)
        unit = mixed * scale
        grad = scale * (lifted - unit * jnp.mean(unit * lifted, axis=-1, keepdims=True))
        grad_ref[b] = grad
        ups.append(dot_bf(q_ref[b], jnp.exp(columns[:, b : b + 1]) * grad, TN))
    second_ref[...] = ups[1]
    totals = [total_of(columns, b) for b in range(2)]
    put_message(message_ref, ups[0] + jnp.exp(totals[0]) * ups[1], totals[0] + totals[1])


def inner_grad_kernel(
    where_ref, q_ref, k_ref, v_ref, col_ref, row_ref, grad_ref, state_ref, second_ref, keep_ref, send_ref
):
    core = where_ref[0]
    columns, across = col_ref[...], row_ref[...]
    length = columns.shape[0]
    lower = triangle(length)
    parts = []
    for b in range(2):
        q, k, v, grad = q_ref[b], k_ref[b], v_ref[b], grad_ref[b]
        weight = weights(columns, across, lower, b)
        scores = dot(q, k, NT) * weight
        grad_scores = dot_fb(grad, v, NT) * weight
        carried = jnp.exp(columns[:, b : b + 1]) * dot_ff(grad, state_ref[b], NT)
        dq = dot_fb(grad_scores, k, NN) + carried
        dk = dot_fb(grad_scores, q, TN)
        dv = dot_ff(scores, grad, TN)
        if b == 0:
            fade = jnp.exp(columns[length - 1 : length, 0:1] - columns[:, 0:1])
            dk = dk + fade * dot_bf(v, second_ref[...], NT)
            dv = dv + fade * dot_bf(k, second_ref[...], NN)
        parts.append((dq, dk, dv))
    for number, (early, late) in enumerate(zip(*parts)):
        part = slice(number * HD, (number + 1) * HD)
        keep_ref[:, part] = jnp.where(core == 0, early, late)
        send_ref[:, part] = jnp.where(core == 0, late, early)


def outer_grad_kernel(count, where_ref, keep_ref, send_ref, col_ref, col_got_ref, inner_ref, inner_got_ref, *refs):
    core = where_ref[0]
    length = keep_ref.shape[0]
    outs = refs[2 * count :]
    for head, rows, cols, inner, chip_refs in (
        (core, keep_ref, col_ref, inner_ref, refs[:count]),
        (1 - core, send_ref, col_got_ref, inner_got_ref, refs[count : 2 * count]),
    ):
        columns = cols[...]
        high, low = split(chip_sum(chip_refs))
        end = columns[length - 1 : length, :]
        block = jnp.where(core == 0, columns[:, 0:1], columns[:, 1:2])
        fade = jnp.exp(jnp.where(core == 0, end[:, 0:1] + end[:, 1:2], end[:, 1:2]) - block)
        k, v = rows[0:length, HD : 2 * HD], rows[0:length, 2 * HD : 3 * HD]
        outs[0][:, lanes_of(head)] = inner[:, 0:HD].astype(BF16)
        key = inner[:, HD : 2 * HD] + fade * (dot(v, high, NT) + dot(v, low, NT))
        outs[1][:, lanes_of(head)] = key.astype(BF16)
        value = inner[:, 2 * HD : 3 * HD] + fade * (dot(k, high, NN) + dot(k, low, NN))
        outs[2][:, lanes_of(head)] = value.astype(BF16)


def layer_kernel(others, where_ref, weight_ref, *refs):
    groups = [refs[number * others : (number + 1) * others] for number in range(2)]
    mine_refs, theirs_refs = groups
    normed_refs = refs[2 * others : 3 * others + 1]
    got_refs = refs[3 * others + 1 : 4 * others + 2]
    out_ref = refs[4 * others + 2]
    core = where_ref[0]
    normed = []
    for mine, theirs in zip(normed_refs, got_refs):
        normed += [mine[core], theirs[core]]
    normed = jnp.concatenate(normed, axis=1)
    width = weight_ref.shape[1]
    step = 512 if width % 512 == 0 else 128
    for begin in range(0, width, step):
        lanes = slice(begin, begin + step)
        weight = [weight_ref[rows_of(core, HD), lanes], weight_ref[rows_of(1 - core, HD), lanes]]
        for mine, theirs in zip(mine_refs, theirs_refs):
            weight += [mine[:, lanes], theirs[:, lanes]]
        out_ref[:, lanes] = dot(normed, jnp.concatenate(weight, axis=0), NN).astype(BF16)


SMEM = pl.BlockSpec(memory_space=pltpu.SMEM)
VMEM = pl.BlockSpec(memory_space=pltpu.VMEM)
HBM = pl.BlockSpec(memory_space=pltpu.HBM)


def call(kernel, name, outs, args, direct=(), copies=0, grant=16, scratch=(), landing=None):
    return pl.pallas_call(
        kernel,
        name=name,
        out_shape=outs,
        in_specs=[SMEM] + [HBM if number in direct else VMEM for number in range(1, len(args))],
        out_specs=[landing or VMEM] * len(outs),
        scratch_shapes=[*scratch] + ([pltpu.SemaphoreType.DMA((copies,))] if copies else []),
        compiler_params=pltpu.CompilerParams(vmem_limit_bytes=grant * 2**20),
        cost_estimate=pl.CostEstimate(flops=1, bytes_accessed=1, transcendentals=0),
    )(*args)


def without_where(kernel):
    return lambda where_ref, *refs: kernel(*refs)


def after(values, *earlier):
    tied = lax.optimization_barrier((tuple(values), earlier))
    return list(tied[0])


def on_device(queries, keys, values, log_decay, norm_gain, out_weight, out_grad):
    length, columns = queries.shape
    seq = lax.axis_size("seq")
    tensor = lax.axis_size("tensor")
    chips = seq // 2
    model = out_weight.shape[1]
    width = model // tensor
    place = lax.axis_index("tensor")
    core = lax.rem(lax.axis_index("seq"), 2)
    side = lax.rem(lax.axis_index("seq") // 2, 2)
    where = jnp.stack([core, side, place]).astype(jnp.int32)
    gain = norm_gain.reshape(1, columns)

    def swap_tensor(value, k):
        return lax.ppermute(value, "tensor", [(i, i ^ k) for i in range(tensor)])

    def swap_core(value):
        return lax.ppermute(value, "seq", [(i, i ^ 1) for i in range(seq)])

    def swap_side(value):
        return lax.ppermute(value, "seq", [(i, i ^ 2) for i in range(seq)])

    def to_chip(value, step):
        return lax.ppermute(
            value, "seq", [(i, i + 2 * step) for i in range(seq) if 0 <= i + 2 * step < seq]
        )

    def shape(dtype, *dims):
        return jax.ShapeDtypeStruct(dims, dtype)

    others = range(1, tensor)
    message = shape(BF16, HD + TAIL, HD)
    pair16 = shape(BF16, 2, length, HD)
    pair32 = shape(F32, 2, length, HD)
    one16 = shape(BF16, length, HD)
    both16 = shape(BF16, length, columns)

    far = [step for step in others if step & (step - 1)]
    near = [step for step in others if not step & (step - 1)]
    order = far + near
    plan = [(step, step in far) for step in order]
    *slices, weight_own, send, keep = call(
        functools.partial(stage_kernel, plan),
        "stage",
        [shape(BF16, HD // 2 if halves else HD, width) for _, halves in plan]
        + [shape(BF16, columns, width), shape(BF16, length + TAIL, 3 * HD), shape(BF16, length, 3 * HD)],
        [where, log_decay, out_weight, queries, keys, values],
        direct=(1, 2, 3, 4, 5),
        copies=len(plan) + 9,
        grant=60,
        scratch=[pltpu.VMEM(log_decay.shape, F32), pltpu.VMEM((TAIL, 3 * HD), BF16)],
        landing=HBM,
    )
    arriving = [swap_tensor(piece, step) for piece, step in zip(slices, order)]
    got = swap_core(send)
    (out_grad,) = after([out_grad], send)
    grad_got = swap_core(out_grad)
    (got,) = after([got], grad_got)
    q, k, v, col, row, first, fresh = call(
        fresh_kernel,
        "fresh",
        [pair16, pair16, pair16, shape(F32, length, 2), shape(F32, 2, length), shape(F32, HD, HD), message],
        [where, keep, got, log_decay],
    )
    arrived = [to_chip(fresh, step) for step in range(1, chips)]
    col_got = swap_core(col)
    (inner,) = call(without_where(inner_kernel), "inner", [pair32], [where, q, k, v, col, row, first])
    mixed, normed, states = call(
        mixed_kernel,
        "mixed",
        [pair32, pair16, shape(F32, 2, HD, HD)],
        [where, q, col, inner, gain, first, *arrived],
    )
    normed_mine = swap_core(normed)
    pieces = [("own", [weight_own])]
    for (step, halves), piece in zip(plan, arriving):
        pieces.append(("halves", [piece, swap_side(piece)]) if halves else ("whole", [piece]))
    partials, mine = [], []
    for number in range(0, tensor, 2):
        kinds, sources = zip(*pieces[number : number + 2])
        sources = sum(sources, [])
        sources = after(sources, normed_mine if number else arrived[-1], col_got, *partials)
        stitched = [shape(BF16, HD, width)] * kinds.count("halves")
        outs = call(
            functools.partial(partial_kernel, kinds),
            "partial",
            [pair16 if number else pair32, pair16, *stitched],
            [where, out_grad, grad_got, *sources],
        )
        partials += outs[:2]
        stitched = list(outs[2:])
        for kind in kinds:
            if kind == "halves":
                mine.append(stitched.pop(0))
                sources = sources[2:]
            else:
                mine.append(sources[0])
                sources = sources[1:]
    mine = mine[1:]
    own_partial, *partials = partials
    sent = [swap_tensor(partial, step) for partial, step in zip(partials, order)]
    (normed_sent,) = after([normed], *partials)
    normed_all = [normed] + [swap_tensor(normed_sent, step) for step in order]
    grad_mixed, second, upward = call(
        grad_mixed_kernel,
        "grad_mixed",
        [pair32, shape(F32, HD, HD), message],
        [where, q, col, gain, mixed, own_partial, *sent],
    )
    returned = [to_chip(upward, -step) for step in range(1, chips)]
    inner_keep, inner_send = call(
        inner_grad_kernel,
        "inner_grad",
        [shape(F32, length, 3 * HD)] * 2,
        [where, q, k, v, col, row, grad_mixed, states, second],
    )
    inner_got = swap_core(inner_send)
    theirs = [swap_core(piece) for piece in after(mine, grad_mixed)]
    normed_got = [normed_mine] + [swap_core(rows) for rows in normed_all[1:]]
    (layer_out,) = call(
        functools.partial(layer_kernel, tensor - 1),
        "layer",
        [shape(BF16, length, width)],
        [where, weight_own, *mine, *theirs, *normed_all, *normed_got],
    )
    returned_got = after([swap_core(rows) for rows in returned], layer_out)
    query_grad, key_grad, value_grad = call(
        functools.partial(outer_grad_kernel, chips - 1),
        "outer_grad",
        [both16] * 3,
        [where, keep, send, col, col_got, inner_keep, inner_got, *returned, *returned_got],
    )
    return layer_out, query_grad, key_grad, value_grad


def solution(mesh):
    in_specs = (
        P("seq", "tensor"),
        P("seq", "tensor"),
        P("seq", "tensor"),
        P("tensor", "seq"),
        P("tensor"),
        P("tensor", None),
        P("seq", "tensor"),
    )
    out_specs = (P("seq", "tensor"), P("seq", "tensor"), P("seq", "tensor"), P("seq", "tensor"))
    return jax.shard_map(
        on_device, mesh=mesh, in_specs=in_specs, out_specs=out_specs, check_vma=False
    )
```

```python
import functools

import jax
import jax.numpy as jnp
from jax import lax
from jax.experimental import pallas as pl
from jax.experimental.pallas import tpu as pltpu
from jax.sharding import PartitionSpec as P

EXACT = lax.Precision.HIGHEST
EPSILON = 1e-05
F32 = jnp.float32
BF16 = jnp.bfloat16
TAIL = 16
HD = 128

NN = (((1,), (0,)), ((), ()))
NT = (((1,), (1,)), ((), ()))
TN = (((0,), (0,)), ((), ()))


def dot(a, b, dims):
    return lax.dot_general(a, b, dims, preferred_element_type=F32)


def split(x):
    high = x.astype(BF16)
    return high, (x - high.astype(F32)).astype(BF16)


def dot_fb(a, b, dims):
    high, low = split(a)
    return dot(high, b, dims) + dot(low, b, dims)


def dot_bf(a, b, dims):
    high, low = split(b)
    return dot(a, high, dims) + dot(a, low, dims)


def dot_ff(a, b, dims):
    ah, al = split(a)
    bh, bl = split(b)
    return dot(ah, bh, dims) + (dot(ah, bl, dims) + dot(al, bh, dims))


def triangle(length):
    rows = lax.broadcasted_iota(jnp.int32, (length, length), 0)
    cols = lax.broadcasted_iota(jnp.int32, (length, length), 1)
    return rows >= cols


def running_columns(decay, lower):
    return lax.dot_general(lower.astype(F32), decay, NT, precision=EXACT, preferred_element_type=F32)


def running_rows(decay, lower):
    return lax.dot_general(decay, lower.astype(F32), NT, precision=EXACT, preferred_element_type=F32)


def put_total(ref, base, total):
    first = total.astype(BF16).astype(F32)
    second = (total - first).astype(BF16).astype(F32)
    third = total - first - second
    at = lax.broadcasted_iota(jnp.int32, (TAIL, 128), 0)
    tail = jnp.where(at == 0, first, jnp.where(at == 1, second, jnp.where(at == 2, third, 0.0)))
    ref[base : base + TAIL, :] = tail.astype(BF16)


def get_total(ref, base):
    tail = ref[base : base + TAIL, :].astype(F32)
    return tail[0:1] + tail[1:2] + tail[2:3]


def total_of(columns, block):
    length = columns.shape[0]
    return jnp.broadcast_to(columns[length - 1 : length, block : block + 1], (1, HD))


def chip_sum(refs):
    summed = jnp.zeros((HD, HD), F32)
    passed = jnp.zeros((1, HD), F32)
    for ref in refs:
        summed = summed + jnp.exp(passed) * ref[0:HD, :].astype(F32)
        passed = passed + get_total(ref, HD)
    return summed


def put_message(ref, state, total):
    ref[0:HD, :] = state.astype(BF16)
    put_total(ref, HD, total)


def lanes_of(number):
    return pl.ds(pl.multiple_of(number * HD, HD), HD)


def rows_of(number, count):
    return pl.ds(pl.multiple_of(number * count, count), count)


def pack_kernel(where_ref, decay_ref, q_ref, k_ref, v_ref, send_ref, keep_ref):
    core = where_ref[0]
    length = keep_ref.shape[0]
    for number, ref in enumerate((q_ref, k_ref, v_ref)):
        part = slice(number * HD, (number + 1) * HD)
        send_ref[0:length, part] = ref[:, lanes_of(1 - core)]
        keep_ref[:, part] = ref[:, lanes_of(core)]
    decay = jnp.where(core == 0, decay_ref[1:2, :], decay_ref[0:1, :])
    first = decay.astype(BF16).astype(F32)
    second = (decay - first).astype(BF16).astype(F32)
    third = decay - first - second
    at = lax.broadcasted_iota(jnp.int32, (TAIL, length), 0)
    tail = jnp.where(at == 0, first, jnp.where(at == 1, second, jnp.where(at == 2, third, 0.0)))
    send_ref[length : length + TAIL, :] = jnp.zeros((TAIL, send_ref.shape[1]), BF16)
    send_ref[length : length + TAIL, 0:length] = tail.astype(BF16)


def fresh_kernel(where_ref, keep_ref, got_ref, decay_ref, q_out, k_out, v_out, col_ref, row_ref, first_ref, message_ref):
    core = where_ref[0]
    length = keep_ref.shape[0]
    for number, out in enumerate((q_out, k_out, v_out)):
        part = slice(number * HD, (number + 1) * HD)
        out[core] = keep_ref[:, part]
        out[1 - core] = got_ref[0:length, part]
    mine = jnp.where(core == 0, decay_ref[0:1, :], decay_ref[1:2, :])
    tail = got_ref[length : length + TAIL, 0:length].astype(F32)
    theirs = tail[0:1] + tail[1:2] + tail[2:3]
    block = lax.broadcasted_iota(jnp.int32, (2, length), 0)
    decay = jnp.where(block == core, mine, theirs)
    lower = triangle(length)
    columns = running_columns(decay, lower)
    col_ref[...] = columns
    row_ref[...] = running_rows(decay, lower)
    states = []
    for b in range(2):
        fade = jnp.exp(columns[length - 1 : length, b : b + 1] - columns[:, b : b + 1])
        states.append(dot_bf(k_out[b], fade * v_out[b].astype(F32), TN))
    totals = [total_of(columns, b) for b in range(2)]
    first_ref[...] = states[0]
    put_message(message_ref, jnp.exp(totals[1]) * states[0] + states[1], totals[0] + totals[1])


def weights(columns, across, lower, b):
    return jnp.exp(jnp.where(lower, columns[:, b : b + 1] - across[b : b + 1, :], -1e30))


def inner_kernel(q_ref, k_ref, v_ref, col_ref, row_ref, first_ref, inner_ref):
    columns, across = col_ref[...], row_ref[...]
    lower = triangle(columns.shape[0])
    for b in range(2):
        scores = dot(q_ref[b], k_ref[b], NT) * weights(columns, across, lower, b)
        inner = dot_fb(scores, v_ref[b], NN)
        if b == 1:
            inner = inner + jnp.exp(columns[:, 1:2]) * dot_bf(q_ref[b], first_ref[...], NN)
        inner_ref[b] = inner


def scale_of(mixed):
    return lax.rsqrt(jnp.mean(mixed * mixed, axis=-1, keepdims=True) + EPSILON)


def mixed_kernel(where_ref, q_ref, col_ref, inner_ref, gain_ref, first_ref, *refs):
    chip_refs, (mixed_ref, normed_ref, state_ref) = refs[:-3], refs[-3:]
    core = where_ref[0]
    columns = col_ref[...]
    gain = gain_ref[:, lanes_of(core)]
    state = chip_sum(chip_refs)
    high, low = split(state)
    shrink = jnp.exp(total_of(columns, 0))
    state_ref[0] = state
    state_ref[1] = shrink * state + first_ref[...]
    for b in range(2):
        grow = jnp.exp(columns[:, b : b + 1])
        if b == 1:
            grow = grow * shrink
        mixed = inner_ref[b] + grow * (dot(q_ref[b], high, NN) + dot(q_ref[b], low, NN))
        mixed_ref[b] = mixed
        normed_ref[b] = (mixed * scale_of(mixed) * gain).astype(BF16)


def partial_kernel(kinds, where_ref, grad_ref, got_ref, normed_ref, *refs):
    core, side = where_ref[0], where_ref[1]
    refs = list(refs)
    inputs = [[refs.pop(0) for _ in range(2 if kind == "halves" else 1)] for kind in kinds]
    *products, weight_out = refs
    weights = []
    for kind, sources in zip(kinds, inputs):
        if kind == "own":
            weights.append(sources[0][rows_of(core, HD), :])
        elif kind == "halves":
            mine, theirs = sources[0][...], sources[1][...]
            weights += [jnp.where(side == 0, mine, theirs), jnp.where(side == 0, theirs, mine)]
        else:
            weights.append(sources[0][...])
    weight = jnp.concatenate(weights, axis=0)
    weight_out[...] = weight[2 * HD - weight_out.shape[0] :]
    for block, ref in ((core, grad_ref), (1 - core, got_ref)):
        product = dot(ref[...], weight, NT)
        for number, out in enumerate(products):
            out[block] = product[:, number * HD : (number + 1) * HD].astype(out.dtype)
    for out in products:
        if out.shape[0] == 4:
            out[2:4] = normed_ref[...]


def grad_mixed_kernel(where_ref, q_ref, col_ref, gain_ref, mixed_ref, normed_ref, own_ref, *refs):
    part_refs, (grad_ref, second_ref, message_ref, cross_ref) = refs[:-4], refs[-4:]
    columns = col_ref[...]
    other = 1 - where_ref[0]
    cross_ref[0] = normed_ref[other]
    for number, ref in enumerate(part_refs):
        cross_ref[number + 1] = ref[2 + other]
    gain = gain_ref[:, lanes_of(where_ref[0])]
    ups = []
    for b in range(2):
        normed = own_ref[b]
        for ref in part_refs:
            normed = normed + ref[b].astype(F32)
        lifted = normed * gain
        mixed = mixed_ref[b]
        scale = scale_of(mixed)
        unit = mixed * scale
        grad = scale * (lifted - unit * jnp.mean(unit * lifted, axis=-1, keepdims=True))
        grad_ref[b] = grad
        ups.append(dot_bf(q_ref[b], jnp.exp(columns[:, b : b + 1]) * grad, TN))
    second_ref[...] = ups[1]
    totals = [total_of(columns, b) for b in range(2)]
    put_message(message_ref, ups[0] + jnp.exp(totals[0]) * ups[1], totals[0] + totals[1])


def inner_grad_kernel(
    where_ref, q_ref, k_ref, v_ref, col_ref, row_ref, grad_ref, state_ref, second_ref, keep_ref, send_ref
):
    core = where_ref[0]
    columns, across = col_ref[...], row_ref[...]
    length = columns.shape[0]
    lower = triangle(length)
    parts = []
    ends = [columns[length - 1 : length, b : b + 1] for b in range(2)]
    for b in range(2):
        q, k, v, grad = q_ref[b], k_ref[b], v_ref[b], grad_ref[b]
        weight = weights(columns, across, lower, b)
        scores = dot(q, k, NT) * weight
        grad_scores = dot_fb(grad, v, NT) * weight
        carried = jnp.exp(columns[:, b : b + 1]) * dot_ff(grad, state_ref[b], NT)
        dq = dot_fb(grad_scores, k, NN) + carried
        dk = dot_fb(grad_scores, q, TN)
        dv = dot_ff(scores, grad, TN)
        fade = jnp.exp(ends[b] - columns[:, b : b + 1])
        if b == 0:
            dk = dk + fade * dot_bf(v, second_ref[...], NT)
            dv = dv + fade * dot_bf(k, second_ref[...], NN)
            fade = fade * jnp.exp(ends[1])
        parts.append((dq, dk, dv, jnp.broadcast_to(fade, (length, HD))))
    for number, (early, late) in enumerate(zip(*parts)):
        part = slice(number * HD, (number + 1) * HD)
        keep_ref[:, part] = jnp.where(core == 0, early, late)
        send_ref[:, part] = jnp.where(core == 0, late, early)


def outer_grad_kernel(count, where_ref, keep_ref, send_ref, inner_ref, inner_got_ref, *refs):
    core = where_ref[0]
    length = keep_ref.shape[0]
    outs = refs[2 * count :]
    for head, rows, inner, chip_refs in (
        (core, keep_ref, inner_ref, refs[:count]),
        (1 - core, send_ref, inner_got_ref, refs[count : 2 * count]),
    ):
        high, low = split(chip_sum(chip_refs))
        fade = inner[:, 3 * HD : 4 * HD]
        k, v = rows[0:length, HD : 2 * HD], rows[0:length, 2 * HD : 3 * HD]
        outs[0][:, lanes_of(head)] = inner[:, 0:HD].astype(BF16)
        key = inner[:, HD : 2 * HD] + fade * (dot(v, high, NT) + dot(v, low, NT))
        outs[1][:, lanes_of(head)] = key.astype(BF16)
        value = inner[:, 2 * HD : 3 * HD] + fade * (dot(k, high, NN) + dot(k, low, NN))
        outs[2][:, lanes_of(head)] = value.astype(BF16)


def layer_kernel(pairs, where_ref, own_ref, *refs):
    mine_refs, theirs_refs = refs[:pairs], refs[pairs : 2 * pairs]
    normed_ref, *sent_refs, got_ref, out_ref = refs[2 * pairs :]
    core = where_ref[0]
    mine = [normed_ref[core]] + [ref[2 + core] for ref in sent_refs]
    theirs = [got_ref[number] for number in range(got_ref.shape[0])]
    normed = [mine[0], theirs[0], mine[1], theirs[1]]
    for begin in range(2, len(mine), 2):
        normed += mine[begin : begin + 2] + theirs[begin : begin + 2]
    normed = jnp.concatenate(normed, axis=1)
    width = own_ref.shape[1]
    step = 512 if width % 512 == 0 else 128
    for begin in range(0, width, step):
        lanes = slice(begin, begin + step)
        weight = [own_ref[rows_of(core, HD), lanes], own_ref[rows_of(1 - core, HD), lanes]]
        for mine_ref, theirs_ref in zip(mine_refs, theirs_refs):
            weight += [mine_ref[:, lanes], theirs_ref[:, lanes]]
        out_ref[:, lanes] = dot(normed, jnp.concatenate(weight, axis=0), NN).astype(BF16)


SMEM = pl.BlockSpec(memory_space=pltpu.SMEM)
VMEM = pl.BlockSpec(memory_space=pltpu.VMEM)


def call(kernel, name, outs, args, grant=16):
    return pl.pallas_call(
        kernel,
        name=name,
        out_shape=outs,
        in_specs=[SMEM] + [VMEM] * (len(args) - 1),
        out_specs=[VMEM] * len(outs),
        compiler_params=pltpu.CompilerParams(vmem_limit_bytes=grant * 2**20),
        cost_estimate=pl.CostEstimate(flops=1, bytes_accessed=1, transcendentals=0),
    )(*args)


def without_where(kernel):
    return lambda where_ref, *refs: kernel(*refs)


def after(values, *earlier):
    tied = lax.optimization_barrier((tuple(values), earlier))
    return list(tied[0])


def on_device(queries, keys, values, log_decay, norm_gain, out_weight, out_grad):
    length, columns = queries.shape
    seq = lax.axis_size("seq")
    tensor = lax.axis_size("tensor")
    chips = seq // 2
    model = out_weight.shape[1]
    width = model // tensor
    place = lax.axis_index("tensor")
    core = lax.rem(lax.axis_index("seq"), 2)
    side = lax.rem(lax.axis_index("seq") // 2, 2)
    where = jnp.stack([core, side]).astype(jnp.int32)
    gain = norm_gain.reshape(1, columns)

    def swap_tensor(value, k):
        return lax.ppermute(value, "tensor", [(i, i ^ k) for i in range(tensor)])

    def swap_core(value):
        return lax.ppermute(value, "seq", [(i, i ^ 1) for i in range(seq)])

    def swap_side(value):
        return lax.ppermute(value, "seq", [(i, i ^ 2) for i in range(seq)])

    def to_chip(value, step):
        return lax.ppermute(
            value, "seq", [(i, i + 2 * step) for i in range(seq) if 0 <= i + 2 * step < seq]
        )

    def shape(dtype, *dims):
        return jax.ShapeDtypeStruct(dims, dtype)

    others = range(1, tensor)
    message = shape(BF16, HD + TAIL, HD)
    pair16 = shape(BF16, 2, length, HD)
    pair32 = shape(F32, 2, length, HD)
    one16 = shape(BF16, length, HD)
    both16 = shape(BF16, length, columns)

    far = [step for step in others if step & (step - 1)]
    near = [step for step in others if not step & (step - 1)]
    order = far + near
    plan = [(step, step in far) for step in order]

    def slice_for(step, halves):
        rows = HD // 2 if halves else HD
        begin = core * HD + side * rows if halves else core * HD
        return lax.dynamic_slice(out_weight, (begin, (place ^ step) * width), (rows, width))

    slices = [slice_for(step, halves) for step, halves in plan]
    arriving = [swap_tensor(piece, step) for piece, step in zip(slices, order)]
    queries, keys, values, out_grad = after([queries, keys, values, out_grad], *slices)
    send, keep = call(
        pack_kernel,
        "pack",
        [shape(BF16, length + TAIL, 3 * HD), shape(BF16, length, 3 * HD)],
        [where, log_decay, queries, keys, values],
        grant=60,
    )
    got = swap_core(send)
    grad_got = swap_core(out_grad)
    (got,) = after([got], grad_got)
    q, k, v, col, row, first, fresh = call(
        fresh_kernel,
        "fresh",
        [pair16, pair16, pair16, shape(F32, length, 2), shape(F32, 2, length), shape(F32, HD, HD), message],
        [where, keep, got, log_decay],
    )
    arrived = [to_chip(fresh, step) for step in range(1, chips)]
    (inner,) = call(without_where(inner_kernel), "inner", [pair32], [where, q, k, v, col, row, first])
    mixed, normed, states = call(
        mixed_kernel,
        "mixed",
        [pair32, pair16, shape(F32, 2, HD, HD)],
        [where, q, col, inner, gain, first, *arrived],
    )
    weight_own = lax.dynamic_slice(out_weight, (0, place * width), (columns, width))
    pieces = [("own", [weight_own])]
    for (step, halves), piece in zip(plan, arriving):
        if halves:
            (piece,) = after([piece], fresh)
        pieces.append(("halves", [piece, swap_side(piece)]) if halves else ("whole", [piece]))
    partials, mine, theirs = [], [], []
    for number in range(0, tensor, 2):
        kinds, sources = zip(*pieces[number : number + 2])
        sources = after(sum(sources, []), mixed, *partials)
        *outs, weight = call(
            functools.partial(partial_kernel, kinds),
            "partial",
            [
                shape(BF16, 4, length, HD) if number else pair32,
                shape(BF16, 4, length, HD),
                shape(BF16, 2 * HD if number else HD, width),
            ],
            [where, out_grad, grad_got, normed, *sources],
        )
        partials += outs
        mine.append(weight)
        if number == 0:
            theirs.append(swap_core(weight))
    own_partial, *partials = partials
    sent = [swap_tensor(partial, step) for partial, step in zip(partials, order)]
    theirs += [swap_core(weight) for weight in mine[1:]]
    grad_mixed, second, upward, cross = call(
        grad_mixed_kernel,
        "grad_mixed",
        [pair32, shape(F32, HD, HD), message, shape(BF16, tensor, length, HD)],
        [where, q, col, gain, mixed, normed, own_partial, *after(sent, *theirs)],
    )
    returned = [to_chip(upward, -step) for step in range(1, chips)]
    cross_got = swap_core(cross)
    inner_keep, inner_send = call(
        inner_grad_kernel,
        "inner_grad",
        [shape(F32, length, 4 * HD)] * 2,
        [where, q, k, v, col, row, grad_mixed, states, second],
    )
    inner_got = swap_core(*after([inner_send], *returned))
    (layer_out,) = call(
        functools.partial(layer_kernel, tensor // 2),
        "layer",
        [shape(BF16, length, width)],
        [where, weight_own, *mine, *theirs, normed, *sent, cross_got],
    )
    returned_got = after([swap_core(rows) for rows in returned], layer_out)
    query_grad, key_grad, value_grad = call(
        functools.partial(outer_grad_kernel, chips - 1),
        "outer_grad",
        [both16] * 3,
        [where, keep, send, inner_keep, inner_got, *returned, *returned_got],
    )
    return layer_out, query_grad, key_grad, value_grad


def solution(mesh):
    in_specs = (
        P("seq", "tensor"),
        P("seq", "tensor"),
        P("seq", "tensor"),
        P("tensor", "seq"),
        P("tensor"),
        P("tensor", None),
        P("seq", "tensor"),
    )
    out_specs = (P("seq", "tensor"), P("seq", "tensor"), P("seq", "tensor"), P("seq", "tensor"))
    return jax.shard_map(
        on_device, mesh=mesh, in_specs=in_specs, out_specs=out_specs, check_vma=False
    )
```

```python
import functools

import jax
import jax.numpy as jnp
from jax import lax
from jax.experimental import pallas as pl
from jax.experimental.pallas import tpu as pltpu
from jax.sharding import PartitionSpec as P

EXACT = lax.Precision.HIGHEST
EPSILON = 1e-05
F32 = jnp.float32
BF16 = jnp.bfloat16
TAIL = 16
HD = 128

NN = (((1,), (0,)), ((), ()))
NT = (((1,), (1,)), ((), ()))
TN = (((0,), (0,)), ((), ()))


def dot(a, b, dims):
    return lax.dot_general(a, b, dims, preferred_element_type=F32)


def split(x):
    high = x.astype(BF16)
    return high, (x - high.astype(F32)).astype(BF16)


def dot_fb(a, b, dims):
    high, low = split(a)
    return dot(high, b, dims) + dot(low, b, dims)


def dot_bf(a, b, dims):
    high, low = split(b)
    return dot(a, high, dims) + dot(a, low, dims)


def dot_ff(a, b, dims):
    ah, al = split(a)
    bh, bl = split(b)
    return dot(ah, bh, dims) + (dot(ah, bl, dims) + dot(al, bh, dims))


def triangle(length):
    rows = lax.broadcasted_iota(jnp.int32, (length, length), 0)
    cols = lax.broadcasted_iota(jnp.int32, (length, length), 1)
    return rows >= cols


def running_columns(decay, lower):
    return lax.dot_general(lower.astype(F32), decay, NT, precision=EXACT, preferred_element_type=F32)


def running_rows(decay, lower):
    return lax.dot_general(decay, lower.astype(F32), NT, precision=EXACT, preferred_element_type=F32)


def put_total(ref, base, total):
    first = total.astype(BF16).astype(F32)
    second = (total - first).astype(BF16).astype(F32)
    third = total - first - second
    at = lax.broadcasted_iota(jnp.int32, (TAIL, 128), 0)
    tail = jnp.where(at == 0, first, jnp.where(at == 1, second, jnp.where(at == 2, third, 0.0)))
    ref[base : base + TAIL, :] = tail.astype(BF16)


def get_total(ref, base):
    tail = ref[base : base + TAIL, :].astype(F32)
    return tail[0:1] + tail[1:2] + tail[2:3]


def total_of(columns, block):
    length = columns.shape[0]
    return jnp.broadcast_to(columns[length - 1 : length, block : block + 1], (1, HD))


def chip_sum(refs):
    summed = jnp.zeros((HD, HD), F32)
    passed = jnp.zeros((1, HD), F32)
    for ref in refs:
        summed = summed + jnp.exp(passed) * ref[0:HD, :].astype(F32)
        passed = passed + get_total(ref, HD)
    return summed


def put_message(ref, state, total):
    ref[0:HD, :] = state.astype(BF16)
    put_total(ref, HD, total)


def lanes_of(number):
    return pl.ds(pl.multiple_of(number * HD, HD), HD)


def rows_of(number, count):
    return pl.ds(pl.multiple_of(number * count, count), count)


def fresh_kernel(
    where_ref, q_ref, k_ref, v_ref, q_got, k_got, v_got, decay_ref, decay_got, q_out, k_out, v_out, col_ref, row_ref, first_ref, message_ref
):
    core = where_ref[0]
    length = q_ref.shape[0]
    for out, ref, got in ((q_out, q_ref, q_got), (k_out, k_ref, k_got), (v_out, v_ref, v_got)):
        out[core] = ref[:, lanes_of(core)]
        out[1 - core] = got[:, lanes_of(core)]
    mine = jnp.where(core == 0, decay_ref[0:1, :], decay_ref[1:2, :])
    theirs = jnp.where(core == 0, decay_got[0:1, :], decay_got[1:2, :])
    block = lax.broadcasted_iota(jnp.int32, (2, length), 0)
    decay = jnp.where(block == core, mine, theirs)
    lower = triangle(length)
    columns = running_columns(decay, lower)
    col_ref[...] = columns
    row_ref[...] = running_rows(decay, lower)
    states = []
    for b in range(2):
        fade = jnp.exp(columns[length - 1 : length, b : b + 1] - columns[:, b : b + 1])
        states.append(dot_bf(k_out[b], fade * v_out[b].astype(F32), TN))
    totals = [total_of(columns, b) for b in range(2)]
    first_ref[...] = states[0]
    put_message(message_ref, jnp.exp(totals[1]) * states[0] + states[1], totals[0] + totals[1])


def weights(columns, across, lower, b):
    return jnp.exp(jnp.where(lower, columns[:, b : b + 1] - across[b : b + 1, :], -1e30))


def inner_kernel(q_ref, k_ref, v_ref, col_ref, row_ref, first_ref, inner_ref):
    columns, across = col_ref[...], row_ref[...]
    lower = triangle(columns.shape[0])
    for b in range(2):
        scores = dot(q_ref[b], k_ref[b], NT) * weights(columns, across, lower, b)
        inner = dot_fb(scores, v_ref[b], NN)
        if b == 1:
            inner = inner + jnp.exp(columns[:, 1:2]) * dot_bf(q_ref[b], first_ref[...], NN)
        inner_ref[b] = inner


def scale_of(mixed):
    return lax.rsqrt(jnp.mean(mixed * mixed, axis=-1, keepdims=True) + EPSILON)


def mixed_kernel(where_ref, q_ref, col_ref, inner_ref, gain_ref, first_ref, *refs):
    chip_refs, (mixed_ref, normed_ref, state_ref) = refs[:-3], refs[-3:]
    core = where_ref[0]
    columns = col_ref[...]
    gain = gain_ref[:, lanes_of(core)]
    state = chip_sum(chip_refs)
    high, low = split(state)
    shrink = jnp.exp(total_of(columns, 0))
    state_ref[0] = state
    state_ref[1] = shrink * state + first_ref[...]
    for b in range(2):
        grow = jnp.exp(columns[:, b : b + 1])
        if b == 1:
            grow = grow * shrink
        mixed = inner_ref[b] + grow * (dot(q_ref[b], high, NN) + dot(q_ref[b], low, NN))
        mixed_ref[b] = mixed
        normed_ref[b] = (mixed * scale_of(mixed) * gain).astype(BF16)


def partial_kernel(kinds, where_ref, grad_ref, got_ref, *refs):
    core, side = where_ref[0], where_ref[1]
    refs = list(refs)
    inputs = [[refs.pop(0) for _ in range(2 if kind == "halves" else 1)] for kind in kinds]
    *products, weight_out = refs
    weights = []
    for kind, sources in zip(kinds, inputs):
        if kind == "own":
            weights.append(sources[0][rows_of(core, HD), :])
        elif kind == "halves":
            mine, theirs = sources[0][...], sources[1][...]
            weights += [jnp.where(side == 0, mine, theirs), jnp.where(side == 0, theirs, mine)]
        else:
            weights.append(sources[0][...])
    weight = jnp.concatenate(weights, axis=0)
    weight_out[...] = weight[2 * HD - weight_out.shape[0] :]
    for block, ref in ((core, grad_ref), (1 - core, got_ref)):
        product = dot(ref[...], weight, NT)
        for number, out in enumerate(products):
            out[block] = product[:, number * HD : (number + 1) * HD].astype(out.dtype)


def grad_mixed_kernel(where_ref, q_ref, col_ref, gain_ref, mixed_ref, own_ref, *refs):
    part_refs, (grad_ref, second_ref, message_ref) = refs[:-3], refs[-3:]
    columns = col_ref[...]
    gain = gain_ref[:, lanes_of(where_ref[0])]
    ups = []
    for b in range(2):
        normed = own_ref[b]
        for ref in part_refs:
            normed = normed + ref[b].astype(F32)
        lifted = normed * gain
        mixed = mixed_ref[b]
        scale = scale_of(mixed)
        unit = mixed * scale
        grad = scale * (lifted - unit * jnp.mean(unit * lifted, axis=-1, keepdims=True))
        grad_ref[b] = grad
        ups.append(dot_bf(q_ref[b], jnp.exp(columns[:, b : b + 1]) * grad, TN))
    second_ref[...] = ups[1]
    totals = [total_of(columns, b) for b in range(2)]
    put_message(message_ref, ups[0] + jnp.exp(totals[0]) * ups[1], totals[0] + totals[1])


def inner_grad_kernel(
    where_ref, q_ref, k_ref, v_ref, col_ref, row_ref, grad_ref, state_ref, second_ref, *refs
):
    normed_refs, (keep_ref, send_ref, cross_ref) = refs[:-3], refs[-3:]
    core = where_ref[0]
    for number, ref in enumerate(normed_refs):
        cross_ref[number] = ref[1 - core]
    columns, across = col_ref[...], row_ref[...]
    length = columns.shape[0]
    lower = triangle(length)
    parts = []
    ends = [columns[length - 1 : length, b : b + 1] for b in range(2)]
    for b in range(2):
        q, k, v, grad = q_ref[b], k_ref[b], v_ref[b], grad_ref[b]
        weight = weights(columns, across, lower, b)
        scores = dot(q, k, NT) * weight
        grad_scores = dot_fb(grad, v, NT) * weight
        carried = jnp.exp(columns[:, b : b + 1]) * dot_ff(grad, state_ref[b], NT)
        dq = dot_fb(grad_scores, k, NN) + carried
        dk = dot_fb(grad_scores, q, TN)
        dv = dot_ff(scores, grad, TN)
        fade = jnp.exp(ends[b] - columns[:, b : b + 1])
        if b == 0:
            dk = dk + fade * dot_bf(v, second_ref[...], NT)
            dv = dv + fade * dot_bf(k, second_ref[...], NN)
            fade = fade * jnp.exp(ends[1])
        parts.append((dq, dk, dv, jnp.broadcast_to(fade, (length, HD))))
    for number, (early, late) in enumerate(zip(*parts)):
        part = slice(number * HD, (number + 1) * HD)
        keep_ref[:, part] = jnp.where(core == 0, early, late)
        send_ref[:, part] = jnp.where(core == 0, late, early)


def outer_grad_kernel(count, where_ref, k_ref, v_ref, inner_ref, inner_got_ref, *refs):
    core = where_ref[0]
    outs = refs[2 * count :]
    for head, inner, chip_refs in (
        (core, inner_ref, refs[:count]),
        (1 - core, inner_got_ref, refs[count : 2 * count]),
    ):
        high, low = split(chip_sum(chip_refs))
        fade = inner[:, 3 * HD : 4 * HD]
        k, v = k_ref[:, lanes_of(head)], v_ref[:, lanes_of(head)]
        outs[0][:, lanes_of(head)] = inner[:, 0:HD].astype(BF16)
        key = inner[:, HD : 2 * HD] + fade * (dot(v, high, NT) + dot(v, low, NT))
        outs[1][:, lanes_of(head)] = key.astype(BF16)
        value = inner[:, 2 * HD : 3 * HD] + fade * (dot(k, high, NN) + dot(k, low, NN))
        outs[2][:, lanes_of(head)] = value.astype(BF16)


def layer_kernel(pairs, where_ref, own_ref, *refs):
    mine_refs, theirs_refs = refs[:pairs], refs[pairs : 2 * pairs]
    *normed_refs, got_ref, out_ref = refs[2 * pairs :]
    core = where_ref[0]
    mine = [ref[core] for ref in normed_refs]
    theirs = [got_ref[number] for number in range(got_ref.shape[0])]
    normed = [mine[0], theirs[0], mine[1], theirs[1]]
    for begin in range(2, len(mine), 2):
        normed += mine[begin : begin + 2] + theirs[begin : begin + 2]
    normed = jnp.concatenate(normed, axis=1)
    width = own_ref.shape[1]
    step = 512 if width % 512 == 0 else 128
    for begin in range(0, width, step):
        lanes = slice(begin, begin + step)
        weight = [own_ref[rows_of(core, HD), lanes], own_ref[rows_of(1 - core, HD), lanes]]
        for mine_ref, theirs_ref in zip(mine_refs, theirs_refs):
            weight += [mine_ref[:, lanes], theirs_ref[:, lanes]]
        out_ref[:, lanes] = dot(normed, jnp.concatenate(weight, axis=0), NN).astype(BF16)


SMEM = pl.BlockSpec(memory_space=pltpu.SMEM)
VMEM = pl.BlockSpec(memory_space=pltpu.VMEM)


def call(kernel, name, outs, args, grant=16):
    return pl.pallas_call(
        kernel,
        name=name,
        out_shape=outs,
        in_specs=[SMEM] + [VMEM] * (len(args) - 1),
        out_specs=[VMEM] * len(outs),
        compiler_params=pltpu.CompilerParams(vmem_limit_bytes=grant * 2**20),
        cost_estimate=pl.CostEstimate(flops=1, bytes_accessed=1, transcendentals=0),
    )(*args)


def without_where(kernel):
    return lambda where_ref, *refs: kernel(*refs)


def after(values, *earlier):
    tied = lax.optimization_barrier((tuple(values), earlier))
    return list(tied[0])


def on_device(queries, keys, values, log_decay, norm_gain, out_weight, out_grad):
    length, columns = queries.shape
    seq = lax.axis_size("seq")
    tensor = lax.axis_size("tensor")
    chips = seq // 2
    model = out_weight.shape[1]
    width = model // tensor
    place = lax.axis_index("tensor")
    core = lax.rem(lax.axis_index("seq"), 2)
    side = lax.rem(lax.axis_index("seq") // 2, 2)
    where = jnp.stack([core, side]).astype(jnp.int32)
    gain = norm_gain.reshape(1, columns)

    def swap_tensor(value, k):
        return lax.ppermute(value, "tensor", [(i, i ^ k) for i in range(tensor)])

    def swap_core(value):
        return lax.ppermute(value, "seq", [(i, i ^ 1) for i in range(seq)])

    def swap_side(value):
        return lax.ppermute(value, "seq", [(i, i ^ 2) for i in range(seq)])

    def to_chip(value, step):
        return lax.ppermute(
            value, "seq", [(i, i + 2 * step) for i in range(seq) if 0 <= i + 2 * step < seq]
        )

    def shape(dtype, *dims):
        return jax.ShapeDtypeStruct(dims, dtype)

    others = range(1, tensor)
    message = shape(BF16, HD + TAIL, HD)
    pair16 = shape(BF16, 2, length, HD)
    pair32 = shape(F32, 2, length, HD)
    one16 = shape(BF16, length, HD)
    both16 = shape(BF16, length, columns)

    far = [step for step in others if step & (step - 1)]
    near = [step for step in others if not step & (step - 1)]
    order = far + near
    plan = [(step, step in far) for step in order]

    def slice_for(step, halves):
        rows = HD // 2 if halves else HD
        begin = core * HD + side * rows if halves else core * HD
        return lax.dynamic_slice(out_weight, (begin, (place ^ step) * width), (rows, width))

    slices = [slice_for(step, halves) for step, halves in plan]
    arriving = [swap_tensor(piece, step) for piece, step in zip(slices, order)]
    got = [swap_core(rows) for rows in (queries, keys, values)]
    got.append(swap_core(log_decay))
    (weight,) = after([out_weight], *slices)
    weight_own = lax.dynamic_slice(weight, (0, place * width), (columns, width))
    got = after(got, weight_own)
    (grad,) = after([out_grad], *got)
    grad_got = swap_core(grad)
    q, k, v, col, row, first, fresh = call(
        fresh_kernel,
        "fresh",
        [pair16, pair16, pair16, shape(F32, length, 2), shape(F32, 2, length), shape(F32, HD, HD), message],
        [where, queries, keys, values, *got[:3], log_decay, got[3]],
    )
    (fresh,) = after([fresh], grad_got)
    arrived = [to_chip(fresh, step) for step in range(1, chips)]
    (inner,) = call(without_where(inner_kernel), "inner", [pair32], [where, q, k, v, col, row, first])
    pieces = [("own", [weight_own])]
    for (step, halves), piece in zip(plan, arriving):
        if halves:
            (piece,) = after([piece], fresh)
        pieces.append(("halves", [piece, swap_side(piece)]) if halves else ("whole", [piece]))
    partials, mine, theirs = [], [], []
    for number in range(0, tensor, 2):
        kinds, sources = zip(*pieces[number : number + 2])
        sources = after(sum(sources, []), *arrived, inner, *partials)
        *outs, weight = call(
            functools.partial(partial_kernel, kinds),
            "partial",
            [pair16 if number else pair32, pair16, shape(BF16, 2 * HD if number else HD, width)],
            [where, out_grad, grad_got, *sources],
        )
        partials += outs
        mine.append(weight)
        if number == 0:
            theirs.append(swap_core(weight))
    own_partial, *partials = partials
    sent = [swap_tensor(partial, step) for partial, step in zip(partials, order)]
    mixed, normed, states = call(
        mixed_kernel,
        "mixed",
        [pair32, pair16, shape(F32, 2, HD, HD)],
        [where, q, col, inner, gain, first, *after(arrived, *partials)],
    )
    normed_all = [normed] + [swap_tensor(normed, step) for step in order]
    grad_mixed, second, upward = call(
        grad_mixed_kernel,
        "grad_mixed",
        [pair32, shape(F32, HD, HD), message],
        [where, q, col, gain, mixed, own_partial, *sent],
    )
    (upward,) = after([upward], *normed_all)
    returned = [to_chip(upward, -step) for step in range(1, chips)]
    theirs += [swap_core(weight) for weight in after(mine[1:], upward)]
    inner_keep, inner_send, cross = call(
        inner_grad_kernel,
        "inner_grad",
        [shape(F32, length, 4 * HD)] * 2 + [shape(BF16, tensor, length, HD)],
        [where, q, k, v, col, row, grad_mixed, states, second, *normed_all],
    )
    cross_got = swap_core(cross)
    inner_got = swap_core(*after([inner_send], *returned))
    (layer_out,) = call(
        functools.partial(layer_kernel, tensor // 2),
        "layer",
        [shape(BF16, length, width)],
        [where, weight_own, *mine, *theirs, *normed_all, cross_got],
    )
    returned_got = after([swap_core(rows) for rows in returned], layer_out)
    query_grad, key_grad, value_grad = call(
        functools.partial(outer_grad_kernel, chips - 1),
        "outer_grad",
        [both16] * 3,
        [where, keys, values, inner_keep, inner_got, *returned, *returned_got],
    )
    return layer_out, query_grad, key_grad, value_grad


def solution(mesh):
    in_specs = (
        P("seq", "tensor"),
        P("seq", "tensor"),
        P("seq", "tensor"),
        P("tensor", "seq"),
        P("tensor"),
        P("tensor", None),
        P("seq", "tensor"),
    )
    out_specs = (P("seq", "tensor"), P("seq", "tensor"), P("seq", "tensor"), P("seq", "tensor"))
    return jax.shard_map(
        on_device, mesh=mesh, in_specs=in_specs, out_specs=out_specs, check_vma=False
    )
```

```python
import functools

import jax
import jax.numpy as jnp
from jax import lax
from jax.experimental import pallas as pl
from jax.experimental.pallas import tpu as pltpu
from jax.sharding import PartitionSpec as P

EXACT = lax.Precision.HIGHEST
EPSILON = 1e-05
F32 = jnp.float32
BF16 = jnp.bfloat16
TAIL = 16
HD = 128

NN = (((1,), (0,)), ((), ()))
NT = (((1,), (1,)), ((), ()))
TN = (((0,), (0,)), ((), ()))


def dot(a, b, dims):
    return lax.dot_general(a, b, dims, preferred_element_type=F32)


def split(x):
    high = x.astype(BF16)
    return high, (x - high.astype(F32)).astype(BF16)


def dot_fb(a, b, dims):
    high, low = split(a)
    return dot(high, b, dims) + dot(low, b, dims)


def dot_bf(a, b, dims):
    high, low = split(b)
    return dot(a, high, dims) + dot(a, low, dims)


def dot_ff(a, b, dims):
    ah, al = split(a)
    bh, bl = split(b)
    return dot(ah, bh, dims) + (dot(ah, bl, dims) + dot(al, bh, dims))


def triangle(length):
    rows = lax.broadcasted_iota(jnp.int32, (length, length), 0)
    cols = lax.broadcasted_iota(jnp.int32, (length, length), 1)
    return rows >= cols


def running_columns(decay, lower):
    return lax.dot_general(lower.astype(F32), decay, NT, precision=EXACT, preferred_element_type=F32)


def running_rows(decay, lower):
    return lax.dot_general(decay, lower.astype(F32), NT, precision=EXACT, preferred_element_type=F32)


def put_total(ref, base, total):
    first = total.astype(BF16).astype(F32)
    second = (total - first).astype(BF16).astype(F32)
    third = total - first - second
    at = lax.broadcasted_iota(jnp.int32, (TAIL, 128), 0)
    tail = jnp.where(at == 0, first, jnp.where(at == 1, second, jnp.where(at == 2, third, 0.0)))
    ref[base : base + TAIL, :] = tail.astype(BF16)


def get_total(ref, base):
    tail = ref[base : base + TAIL, :].astype(F32)
    return tail[0:1] + tail[1:2] + tail[2:3]


def total_of(columns, block):
    length = columns.shape[0]
    return jnp.broadcast_to(columns[length - 1 : length, block : block + 1], (1, HD))


def chip_sum(refs):
    summed = jnp.zeros((HD, HD), F32)
    passed = jnp.zeros((1, HD), F32)
    for ref in refs:
        summed = summed + jnp.exp(passed) * ref[0:HD, :].astype(F32)
        passed = passed + get_total(ref, HD)
    return summed


def put_message(ref, state, total):
    ref[0:HD, :] = state.astype(BF16)
    put_total(ref, HD, total)


def lanes_of(number):
    return pl.ds(pl.multiple_of(number * HD, HD), HD)


def rows_of(number, count):
    return pl.ds(pl.multiple_of(number * count, count), count)


def fresh_kernel(
    where_ref, q_ref, k_ref, v_ref, q_got, k_got, v_got, decay_ref, decay_got, q_out, k_out, v_out, col_ref, row_ref, first_ref, message_ref
):
    core = where_ref[0]
    length = q_ref.shape[0]
    for out, ref, got in ((q_out, q_ref, q_got), (k_out, k_ref, k_got), (v_out, v_ref, v_got)):
        out[core] = ref[:, lanes_of(core)]
        out[1 - core] = got[:, lanes_of(core)]
    mine = jnp.where(core == 0, decay_ref[0:1, :], decay_ref[1:2, :])
    theirs = jnp.where(core == 0, decay_got[0:1, :], decay_got[1:2, :])
    block = lax.broadcasted_iota(jnp.int32, (2, length), 0)
    decay = jnp.where(block == core, mine, theirs)
    lower = triangle(length)
    columns = running_columns(decay, lower)
    col_ref[...] = columns
    row_ref[...] = running_rows(decay, lower)
    states = []
    for b in range(2):
        fade = jnp.exp(columns[length - 1 : length, b : b + 1] - columns[:, b : b + 1])
        states.append(dot_bf(k_out[b], fade * v_out[b].astype(F32), TN))
    totals = [total_of(columns, b) for b in range(2)]
    first_ref[...] = states[0]
    put_message(message_ref, jnp.exp(totals[1]) * states[0] + states[1], totals[0] + totals[1])


def weights(columns, across, lower, b):
    return jnp.exp(jnp.where(lower, columns[:, b : b + 1] - across[b : b + 1, :], -1e30))


def inner_kernel(q_ref, k_ref, v_ref, col_ref, row_ref, first_ref, inner_ref):
    columns, across = col_ref[...], row_ref[...]
    lower = triangle(columns.shape[0])
    for b in range(2):
        scores = dot(q_ref[b], k_ref[b], NT) * weights(columns, across, lower, b)
        inner = dot_fb(scores, v_ref[b], NN)
        if b == 1:
            inner = inner + jnp.exp(columns[:, 1:2]) * dot_bf(q_ref[b], first_ref[...], NN)
        inner_ref[b] = inner


def scale_of(mixed):
    return lax.rsqrt(jnp.mean(mixed * mixed, axis=-1, keepdims=True) + EPSILON)


def mixed_kernel(where_ref, q_ref, col_ref, inner_ref, gain_ref, first_ref, *refs):
    chip_refs, (mixed_ref, normed_ref, state_ref) = refs[:-3], refs[-3:]
    core = where_ref[0]
    columns = col_ref[...]
    gain = gain_ref[:, lanes_of(core)]
    state = chip_sum(chip_refs)
    high, low = split(state)
    shrink = jnp.exp(total_of(columns, 0))
    state_ref[0] = state
    state_ref[1] = shrink * state + first_ref[...]
    for b in range(2):
        grow = jnp.exp(columns[:, b : b + 1])
        if b == 1:
            grow = grow * shrink
        mixed = inner_ref[b] + grow * (dot(q_ref[b], high, NN) + dot(q_ref[b], low, NN))
        mixed_ref[b] = mixed
        normed_ref[b] = (mixed * scale_of(mixed) * gain).astype(BF16)


def partial_kernel(kinds, where_ref, grad_ref, got_ref, *refs):
    core, side = where_ref[0], where_ref[1]
    refs = list(refs)
    inputs = [[refs.pop(0) for _ in range(2 if kind == "halves" else 1)] for kind in kinds]
    *products, weight_out = refs
    weights = []
    for kind, sources in zip(kinds, inputs):
        if kind == "own":
            weights.append(sources[0][rows_of(core, HD), :])
        elif kind == "halves":
            mine, theirs = sources[0][...], sources[1][...]
            weights += [jnp.where(side == 0, mine, theirs), jnp.where(side == 0, theirs, mine)]
        else:
            weights.append(sources[0][...])
    weight = jnp.concatenate(weights, axis=0)
    weight_out[...] = weight[2 * HD - weight_out.shape[0] :]
    for block, ref in ((core, grad_ref), (1 - core, got_ref)):
        product = dot(ref[...], weight, NT)
        for number, out in enumerate(products):
            out[block] = product[:, number * HD : (number + 1) * HD].astype(out.dtype)


def grad_mixed_kernel(where_ref, q_ref, col_ref, gain_ref, mixed_ref, own_ref, *refs):
    part_refs, (grad_ref, second_ref, message_ref) = refs[:-3], refs[-3:]
    columns = col_ref[...]
    gain = gain_ref[:, lanes_of(where_ref[0])]
    ups = []
    for b in range(2):
        normed = own_ref[b]
        for ref in part_refs:
            normed = normed + ref[b].astype(F32)
        lifted = normed * gain
        mixed = mixed_ref[b]
        scale = scale_of(mixed)
        unit = mixed * scale
        grad = scale * (lifted - unit * jnp.mean(unit * lifted, axis=-1, keepdims=True))
        grad_ref[b] = grad
        ups.append(dot_bf(q_ref[b], jnp.exp(columns[:, b : b + 1]) * grad, TN))
    second_ref[...] = ups[1]
    totals = [total_of(columns, b) for b in range(2)]
    put_message(message_ref, ups[0] + jnp.exp(totals[0]) * ups[1], totals[0] + totals[1])


def inner_grad_kernel(
    where_ref, q_ref, k_ref, v_ref, col_ref, row_ref, grad_ref, state_ref, second_ref, *refs
):
    normed_refs, (keep_ref, send_ref, cross_ref) = refs[:-3], refs[-3:]
    core = where_ref[0]
    for number, ref in enumerate(normed_refs):
        cross_ref[number] = ref[1 - core]
    columns, across = col_ref[...], row_ref[...]
    length = columns.shape[0]
    lower = triangle(length)
    parts = []
    ends = [columns[length - 1 : length, b : b + 1] for b in range(2)]
    for b in range(2):
        q, k, v, grad = q_ref[b], k_ref[b], v_ref[b], grad_ref[b]
        weight = weights(columns, across, lower, b)
        scores = dot(q, k, NT) * weight
        grad_scores = dot_fb(grad, v, NT) * weight
        carried = jnp.exp(columns[:, b : b + 1]) * dot_ff(grad, state_ref[b], NT)
        dq = dot_fb(grad_scores, k, NN) + carried
        dk = dot_fb(grad_scores, q, TN)
        dv = dot_ff(scores, grad, TN)
        fade = jnp.exp(ends[b] - columns[:, b : b + 1])
        if b == 0:
            dk = dk + fade * dot_bf(v, second_ref[...], NT)
            dv = dv + fade * dot_bf(k, second_ref[...], NN)
            fade = fade * jnp.exp(ends[1])
        parts.append((dq, dk, dv, jnp.broadcast_to(fade, (length, HD))))
    for number, (early, late) in enumerate(zip(*parts)):
        part = slice(number * HD, (number + 1) * HD)
        keep_ref[:, part] = jnp.where(core == 0, early, late)
        send_ref[:, part] = jnp.where(core == 0, late, early)


def outer_grad_kernel(count, where_ref, k_ref, v_ref, inner_ref, inner_got_ref, *refs):
    core = where_ref[0]
    outs = refs[2 * count :]
    for head, inner, chip_refs in (
        (core, inner_ref, refs[:count]),
        (1 - core, inner_got_ref, refs[count : 2 * count]),
    ):
        high, low = split(chip_sum(chip_refs))
        fade = inner[:, 3 * HD : 4 * HD]
        k, v = k_ref[:, lanes_of(head)], v_ref[:, lanes_of(head)]
        outs[0][:, lanes_of(head)] = inner[:, 0:HD].astype(BF16)
        key = inner[:, HD : 2 * HD] + fade * (dot(v, high, NT) + dot(v, low, NT))
        outs[1][:, lanes_of(head)] = key.astype(BF16)
        value = inner[:, 2 * HD : 3 * HD] + fade * (dot(k, high, NN) + dot(k, low, NN))
        outs[2][:, lanes_of(head)] = value.astype(BF16)


def layer_kernel(pairs, where_ref, own_ref, *refs):
    mine_refs, theirs_refs = refs[:pairs], refs[pairs : 2 * pairs]
    *normed_refs, got_ref, out_ref = refs[2 * pairs :]
    core = where_ref[0]
    mine = [ref[core] for ref in normed_refs]
    theirs = [got_ref[number] for number in range(got_ref.shape[0])]
    normed = [mine[0], theirs[0], mine[1], theirs[1]]
    for begin in range(2, len(mine), 2):
        normed += mine[begin : begin + 2] + theirs[begin : begin + 2]
    normed = jnp.concatenate(normed, axis=1)
    width = own_ref.shape[1]
    step = 512 if width % 512 == 0 else 128
    for begin in range(0, width, step):
        lanes = slice(begin, begin + step)
        weight = [own_ref[rows_of(core, HD), lanes], own_ref[rows_of(1 - core, HD), lanes]]
        for mine_ref, theirs_ref in zip(mine_refs, theirs_refs):
            weight += [mine_ref[:, lanes], theirs_ref[:, lanes]]
        out_ref[:, lanes] = dot(normed, jnp.concatenate(weight, axis=0), NN).astype(BF16)


SMEM = pl.BlockSpec(memory_space=pltpu.SMEM)
VMEM = pl.BlockSpec(memory_space=pltpu.VMEM)


def call(kernel, name, outs, args, grant=16):
    return pl.pallas_call(
        kernel,
        name=name,
        out_shape=outs,
        in_specs=[SMEM] + [VMEM] * (len(args) - 1),
        out_specs=[VMEM] * len(outs),
        compiler_params=pltpu.CompilerParams(vmem_limit_bytes=grant * 2**20),
        cost_estimate=pl.CostEstimate(flops=1, bytes_accessed=1, transcendentals=0),
    )(*args)


def without_where(kernel):
    return lambda where_ref, *refs: kernel(*refs)


def after(values, *earlier):
    tied = lax.optimization_barrier((tuple(values), earlier))
    return list(tied[0])


def on_device(queries, keys, values, log_decay, norm_gain, out_weight, out_grad):
    length, columns = queries.shape
    seq = lax.axis_size("seq")
    tensor = lax.axis_size("tensor")
    chips = seq // 2
    model = out_weight.shape[1]
    width = model // tensor
    place = lax.axis_index("tensor")
    core = lax.rem(lax.axis_index("seq"), 2)
    side = lax.rem(lax.axis_index("seq") // 2, 2)
    where = jnp.stack([core, side]).astype(jnp.int32)
    gain = norm_gain.reshape(1, columns)

    def swap_tensor(value, k):
        return lax.ppermute(value, "tensor", [(i, i ^ k) for i in range(tensor)])

    def swap_core(value):
        return lax.ppermute(value, "seq", [(i, i ^ 1) for i in range(seq)])

    def swap_side(value):
        return lax.ppermute(value, "seq", [(i, i ^ 2) for i in range(seq)])

    def to_chip(value, step):
        return lax.ppermute(
            value, "seq", [(i, i + 2 * step) for i in range(seq) if 0 <= i + 2 * step < seq]
        )

    def shape(dtype, *dims):
        return jax.ShapeDtypeStruct(dims, dtype)

    others = range(1, tensor)
    message = shape(BF16, HD + TAIL, HD)
    pair16 = shape(BF16, 2, length, HD)
    pair32 = shape(F32, 2, length, HD)
    one16 = shape(BF16, length, HD)
    both16 = shape(BF16, length, columns)

    far = [step for step in others if step & (step - 1)]
    near = [step for step in others if not step & (step - 1)]
    order = far + near
    plan = [(step, step in far) for step in order]

    def slice_for(step, halves):
        rows = HD // 2 if halves else HD
        begin = core * HD + side * rows if halves else core * HD
        return lax.dynamic_slice(out_weight, (begin, (place ^ step) * width), (rows, width))

    slices = [slice_for(step, halves) for step, halves in plan]
    got = [swap_core(rows) for rows in (queries, keys, values, log_decay)]
    (weight,) = after([out_weight], *slices)
    weight_own = lax.dynamic_slice(weight, (0, place * width), (columns, width))
    got = after(got, weight_own)
    q, k, v, col, row, first, fresh = call(
        fresh_kernel,
        "fresh",
        [pair16, pair16, pair16, shape(F32, length, 2), shape(F32, 2, length), shape(F32, HD, HD), message],
        [where, queries, keys, values, *got[:3], log_decay, got[3]],
    )
    arrived = [to_chip(fresh, step) for step in range(1, chips)]
    slices = after(slices, *arrived)
    arriving = [swap_tensor(piece, step) for piece, step in zip(slices, order)]
    (grad,) = after([out_grad], *arrived)
    grad_got = swap_core(grad)
    (inner,) = call(without_where(inner_kernel), "inner", [pair32], [where, q, k, v, col, row, first])
    mixed, normed, states = call(
        mixed_kernel,
        "mixed",
        [pair32, pair16, shape(F32, 2, HD, HD)],
        [where, q, col, inner, gain, first, *arrived],
    )
    pieces = [("own", [weight_own])]
    for (step, halves), piece in zip(plan, arriving):
        if halves:
            (piece,) = after([piece], mixed)
        pieces.append(("halves", [piece, swap_side(piece)]) if halves else ("whole", [piece]))
    partials, mine, theirs = [], [], []
    for number in range(0, tensor, 2):
        kinds, sources = zip(*pieces[number : number + 2])
        sources = after(sum(sources, []), mixed, *partials)
        *outs, weight = call(
            functools.partial(partial_kernel, kinds),
            "partial",
            [pair16 if number else pair32, pair16, shape(BF16, 2 * HD if number else HD, width)],
            [where, out_grad, grad_got, *sources],
        )
        partials += outs
        mine.append(weight)
        if number == 0:
            theirs.append(swap_core(weight))
    own_partial, *partials = partials
    sent = [swap_tensor(partial, step) for partial, step in zip(partials, order)]
    normed_all = [normed] + [swap_tensor(normed, step) for step in order]
    grad_mixed, second, upward = call(
        grad_mixed_kernel,
        "grad_mixed",
        [pair32, shape(F32, HD, HD), message],
        [where, q, col, gain, mixed, own_partial, *sent],
    )
    (upward,) = after([upward], *normed_all)
    returned = [to_chip(upward, -step) for step in range(1, chips)]
    theirs += [swap_core(weight) for weight in after(mine[1:], upward)]
    inner_keep, inner_send, cross = call(
        inner_grad_kernel,
        "inner_grad",
        [shape(F32, length, 4 * HD)] * 2 + [shape(BF16, tensor, length, HD)],
        [where, q, k, v, col, row, grad_mixed, states, second, *normed_all],
    )
    cross_got = swap_core(cross)
    inner_got = swap_core(*after([inner_send], *returned))
    (layer_out,) = call(
        functools.partial(layer_kernel, tensor // 2),
        "layer",
        [shape(BF16, length, width)],
        [where, weight_own, *mine, *theirs, *normed_all, cross_got],
    )
    returned_got = after([swap_core(rows) for rows in returned], layer_out)
    query_grad, key_grad, value_grad = call(
        functools.partial(outer_grad_kernel, chips - 1),
        "outer_grad",
        [both16] * 3,
        [where, keys, values, inner_keep, inner_got, *returned, *returned_got],
    )
    return layer_out, query_grad, key_grad, value_grad


def solution(mesh):
    in_specs = (
        P("seq", "tensor"),
        P("seq", "tensor"),
        P("seq", "tensor"),
        P("tensor", "seq"),
        P("tensor"),
        P("tensor", None),
        P("seq", "tensor"),
    )
    out_specs = (P("seq", "tensor"), P("seq", "tensor"), P("seq", "tensor"), P("seq", "tensor"))
    return jax.shard_map(
        on_device, mesh=mesh, in_specs=in_specs, out_specs=out_specs, check_vma=False
    )
```

```python
import functools

import jax
import jax.numpy as jnp
from jax import lax
from jax.experimental import pallas as pl
from jax.experimental.pallas import tpu as pltpu
from jax.sharding import PartitionSpec as P

EXACT = lax.Precision.HIGHEST
EPSILON = 1e-05
F32 = jnp.float32
BF16 = jnp.bfloat16
TAIL = 16
HD = 128

NN = (((1,), (0,)), ((), ()))
NT = (((1,), (1,)), ((), ()))
TN = (((0,), (0,)), ((), ()))


def dot(a, b, dims):
    return lax.dot_general(a, b, dims, preferred_element_type=F32)


def split(x):
    high = x.astype(BF16)
    return high, (x - high.astype(F32)).astype(BF16)


def dot_fb(a, b, dims):
    high, low = split(a)
    return dot(high, b, dims) + dot(low, b, dims)


def dot_bf(a, b, dims):
    high, low = split(b)
    return dot(a, high, dims) + dot(a, low, dims)


def dot_ff(a, b, dims):
    ah, al = split(a)
    bh, bl = split(b)
    return dot(ah, bh, dims) + (dot(ah, bl, dims) + dot(al, bh, dims))


def triangle(length):
    rows = lax.broadcasted_iota(jnp.int32, (length, length), 0)
    cols = lax.broadcasted_iota(jnp.int32, (length, length), 1)
    return rows >= cols


def running_columns(decay, lower):
    return lax.dot_general(lower.astype(F32), decay, NT, precision=EXACT, preferred_element_type=F32)


def running_rows(decay, lower):
    return lax.dot_general(decay, lower.astype(F32), NT, precision=EXACT, preferred_element_type=F32)


def put_total(ref, base, total):
    first = total.astype(BF16).astype(F32)
    second = (total - first).astype(BF16).astype(F32)
    third = total - first - second
    at = lax.broadcasted_iota(jnp.int32, (TAIL, 128), 0)
    tail = jnp.where(at == 0, first, jnp.where(at == 1, second, jnp.where(at == 2, third, 0.0)))
    ref[base : base + TAIL, :] = tail.astype(BF16)


def get_total(ref, base):
    tail = ref[base : base + TAIL, :].astype(F32)
    return tail[0:1] + tail[1:2] + tail[2:3]


def total_of(columns, block):
    length = columns.shape[0]
    return jnp.broadcast_to(columns[length - 1 : length, block : block + 1], (1, HD))


def chip_sum(refs):
    summed = jnp.zeros((HD, HD), F32)
    passed = jnp.zeros((1, HD), F32)
    for ref in refs:
        summed = summed + jnp.exp(passed) * ref[0:HD, :].astype(F32)
        passed = passed + get_total(ref, HD)
    return summed


def put_message(ref, state, total):
    ref[0:HD, :] = state.astype(BF16)
    put_total(ref, HD, total)


def join_kernel(own_ref, got_ref, out_ref):
    total = get_total(own_ref, HD)
    state = own_ref[0:HD, :].astype(F32) + jnp.exp(total) * got_ref[0:HD, :].astype(F32)
    put_message(out_ref, state, total + get_total(got_ref, HD))


def cross_kernel(where_ref, *refs):
    *normed_refs, cross_ref = refs
    for number, ref in enumerate(normed_refs):
        cross_ref[number] = ref[1 - where_ref[0]]


def lanes_of(number):
    return pl.ds(pl.multiple_of(number * HD, HD), HD)


def rows_of(number, count):
    return pl.ds(pl.multiple_of(number * count, count), count)


def fresh_kernel(
    where_ref, q_ref, k_ref, v_ref, q_got, k_got, v_got, decay_ref, decay_got, q_out, k_out, v_out, col_ref, row_ref, first_ref, message_ref
):
    core = where_ref[0]
    length = q_ref.shape[0]
    for out, ref, got in ((q_out, q_ref, q_got), (k_out, k_ref, k_got), (v_out, v_ref, v_got)):
        out[core] = ref[:, lanes_of(core)]
        out[1 - core] = got[:, lanes_of(core)]
    mine = jnp.where(core == 0, decay_ref[0:1, :], decay_ref[1:2, :])
    theirs = jnp.where(core == 0, decay_got[0:1, :], decay_got[1:2, :])
    block = lax.broadcasted_iota(jnp.int32, (2, length), 0)
    decay = jnp.where(block == core, mine, theirs)
    lower = triangle(length)
    columns = running_columns(decay, lower)
    col_ref[...] = columns
    row_ref[...] = running_rows(decay, lower)
    states = []
    for b in range(2):
        fade = jnp.exp(columns[length - 1 : length, b : b + 1] - columns[:, b : b + 1])
        states.append(dot_bf(k_out[b], fade * v_out[b].astype(F32), TN))
    totals = [total_of(columns, b) for b in range(2)]
    first_ref[...] = states[0]
    put_message(message_ref, jnp.exp(totals[1]) * states[0] + states[1], totals[0] + totals[1])


def weights(columns, across, lower, b):
    return jnp.exp(jnp.where(lower, columns[:, b : b + 1] - across[b : b + 1, :], -1e30))


def inner_kernel(q_ref, k_ref, v_ref, col_ref, row_ref, first_ref, inner_ref):
    columns, across = col_ref[...], row_ref[...]
    lower = triangle(columns.shape[0])
    for b in range(2):
        scores = dot(q_ref[b], k_ref[b], NT) * weights(columns, across, lower, b)
        inner = dot_fb(scores, v_ref[b], NN)
        if b == 1:
            inner = inner + jnp.exp(columns[:, 1:2]) * dot_bf(q_ref[b], first_ref[...], NN)
        inner_ref[b] = inner


def scale_of(mixed):
    return lax.rsqrt(jnp.mean(mixed * mixed, axis=-1, keepdims=True) + EPSILON)


def mixed_kernel(where_ref, q_ref, col_ref, inner_ref, gain_ref, first_ref, *refs):
    chip_refs, (mixed_ref, normed_ref, state_ref) = refs[:-3], refs[-3:]
    core = where_ref[0]
    columns = col_ref[...]
    gain = gain_ref[:, lanes_of(core)]
    state = chip_sum(chip_refs)
    high, low = split(state)
    shrink = jnp.exp(total_of(columns, 0))
    state_ref[0] = state
    state_ref[1] = shrink * state + first_ref[...]
    for b in range(2):
        grow = jnp.exp(columns[:, b : b + 1])
        if b == 1:
            grow = grow * shrink
        mixed = inner_ref[b] + grow * (dot(q_ref[b], high, NN) + dot(q_ref[b], low, NN))
        mixed_ref[b] = mixed
        normed_ref[b] = (mixed * scale_of(mixed) * gain).astype(BF16)


def partial_kernel(kinds, where_ref, grad_ref, got_ref, *refs):
    core, side = where_ref[0], where_ref[1]
    refs = list(refs)
    inputs = [[refs.pop(0) for _ in range(2 if kind == "halves" else 1)] for kind in kinds]
    *products, weight_out = refs
    weights = []
    for kind, sources in zip(kinds, inputs):
        if kind == "own":
            weights.append(sources[0][rows_of(core, HD), :])
        elif kind == "halves":
            mine, theirs = sources[0][...], sources[1][...]
            weights += [jnp.where(side == 0, mine, theirs), jnp.where(side == 0, theirs, mine)]
        else:
            weights.append(sources[0][...])
    weight = jnp.concatenate(weights, axis=0)
    weight_out[...] = weight[2 * HD - weight_out.shape[0] :]
    for block, ref in ((core, grad_ref), (1 - core, got_ref)):
        product = dot(ref[...], weight, NT)
        for number, out in enumerate(products):
            out[block] = product[:, number * HD : (number + 1) * HD].astype(out.dtype)


def grad_mixed_kernel(where_ref, q_ref, col_ref, gain_ref, mixed_ref, own_ref, *refs):
    part_refs, (grad_ref, second_ref, message_ref) = refs[:-3], refs[-3:]
    columns = col_ref[...]
    gain = gain_ref[:, lanes_of(where_ref[0])]
    ups = []
    for b in range(2):
        normed = own_ref[b]
        for ref in part_refs:
            normed = normed + ref[b].astype(F32)
        lifted = normed * gain
        mixed = mixed_ref[b]
        scale = scale_of(mixed)
        unit = mixed * scale
        grad = scale * (lifted - unit * jnp.mean(unit * lifted, axis=-1, keepdims=True))
        grad_ref[b] = grad
        ups.append(dot_bf(q_ref[b], jnp.exp(columns[:, b : b + 1]) * grad, TN))
    second_ref[...] = ups[1]
    totals = [total_of(columns, b) for b in range(2)]
    put_message(message_ref, ups[0] + jnp.exp(totals[0]) * ups[1], totals[0] + totals[1])


def inner_grad_kernel(
    where_ref, q_ref, k_ref, v_ref, col_ref, row_ref, grad_ref, state_ref, second_ref, keep_ref, send_ref
):
    core = where_ref[0]
    columns, across = col_ref[...], row_ref[...]
    length = columns.shape[0]
    lower = triangle(length)
    parts = []
    ends = [columns[length - 1 : length, b : b + 1] for b in range(2)]
    for b in range(2):
        q, k, v, grad = q_ref[b], k_ref[b], v_ref[b], grad_ref[b]
        weight = weights(columns, across, lower, b)
        scores = dot(q, k, NT) * weight
        grad_scores = dot_fb(grad, v, NT) * weight
        carried = jnp.exp(columns[:, b : b + 1]) * dot_ff(grad, state_ref[b], NT)
        dq = dot_fb(grad_scores, k, NN) + carried
        dk = dot_fb(grad_scores, q, TN)
        dv = dot_ff(scores, grad, TN)
        fade = jnp.exp(ends[b] - columns[:, b : b + 1])
        if b == 0:
            dk = dk + fade * dot_bf(v, second_ref[...], NT)
            dv = dv + fade * dot_bf(k, second_ref[...], NN)
            fade = fade * jnp.exp(ends[1])
        parts.append((dq, dk, dv, jnp.broadcast_to(fade, (length, HD))))
    for number, (early, late) in enumerate(zip(*parts)):
        part = slice(number * HD, (number + 1) * HD)
        keep_ref[:, part] = jnp.where(core == 0, early, late)
        send_ref[:, part] = jnp.where(core == 0, late, early)


def outer_grad_kernel(count, where_ref, k_ref, v_ref, inner_ref, inner_got_ref, *refs):
    core = where_ref[0]
    outs = refs[2 * count :]
    for head, inner, chip_refs in (
        (core, inner_ref, refs[:count]),
        (1 - core, inner_got_ref, refs[count : 2 * count]),
    ):
        high, low = split(chip_sum(chip_refs))
        fade = inner[:, 3 * HD : 4 * HD]
        k, v = k_ref[:, lanes_of(head)], v_ref[:, lanes_of(head)]
        outs[0][:, lanes_of(head)] = inner[:, 0:HD].astype(BF16)
        key = inner[:, HD : 2 * HD] + fade * (dot(v, high, NT) + dot(v, low, NT))
        outs[1][:, lanes_of(head)] = key.astype(BF16)
        value = inner[:, 2 * HD : 3 * HD] + fade * (dot(k, high, NN) + dot(k, low, NN))
        outs[2][:, lanes_of(head)] = value.astype(BF16)


def layer_kernel(pairs, where_ref, own_ref, *refs):
    mine_refs, theirs_refs = refs[:pairs], refs[pairs : 2 * pairs]
    *normed_refs, got_ref, out_ref = refs[2 * pairs :]
    core = where_ref[0]
    mine = [ref[core] for ref in normed_refs]
    theirs = [got_ref[number] for number in range(got_ref.shape[0])]
    normed = [mine[0], theirs[0], mine[1], theirs[1]]
    for begin in range(2, len(mine), 2):
        normed += mine[begin : begin + 2] + theirs[begin : begin + 2]
    normed = jnp.concatenate(normed, axis=1)
    width = own_ref.shape[1]
    step = 512 if width % 512 == 0 else 128
    for begin in range(0, width, step):
        lanes = slice(begin, begin + step)
        weight = [own_ref[rows_of(core, HD), lanes], own_ref[rows_of(1 - core, HD), lanes]]
        for mine_ref, theirs_ref in zip(mine_refs, theirs_refs):
            weight += [mine_ref[:, lanes], theirs_ref[:, lanes]]
        out_ref[:, lanes] = dot(normed, jnp.concatenate(weight, axis=0), NN).astype(BF16)


SMEM = pl.BlockSpec(memory_space=pltpu.SMEM)
VMEM = pl.BlockSpec(memory_space=pltpu.VMEM)


def call(kernel, name, outs, args, grant=16):
    return pl.pallas_call(
        kernel,
        name=name,
        out_shape=outs,
        in_specs=[SMEM] + [VMEM] * (len(args) - 1),
        out_specs=[VMEM] * len(outs),
        compiler_params=pltpu.CompilerParams(vmem_limit_bytes=grant * 2**20),
        cost_estimate=pl.CostEstimate(flops=1, bytes_accessed=1, transcendentals=0),
    )(*args)


def without_where(kernel):
    return lambda where_ref, *refs: kernel(*refs)


def after(values, *earlier):
    tied = lax.optimization_barrier((tuple(values), earlier))
    return list(tied[0])


def on_device(queries, keys, values, log_decay, norm_gain, out_weight, out_grad):
    length, columns = queries.shape
    seq = lax.axis_size("seq")
    tensor = lax.axis_size("tensor")
    chips = seq // 2
    model = out_weight.shape[1]
    width = model // tensor
    place = lax.axis_index("tensor")
    core = lax.rem(lax.axis_index("seq"), 2)
    side = lax.rem(lax.axis_index("seq") // 2, 2)
    where = jnp.stack([core, side]).astype(jnp.int32)
    gain = norm_gain.reshape(1, columns)

    def swap_tensor(value, k):
        return lax.ppermute(value, "tensor", [(i, i ^ k) for i in range(tensor)])

    def swap_core(value):
        return lax.ppermute(value, "seq", [(i, i ^ 1) for i in range(seq)])

    def swap_side(value):
        return lax.ppermute(value, "seq", [(i, i ^ 2) for i in range(seq)])

    def to_chip(value, step):
        return lax.ppermute(
            value, "seq", [(i, i + 2 * step) for i in range(seq) if 0 <= i + 2 * step < seq]
        )

    def shape(dtype, *dims):
        return jax.ShapeDtypeStruct(dims, dtype)

    others = range(1, tensor)
    message = shape(BF16, HD + TAIL, HD)
    pair16 = shape(BF16, 2, length, HD)
    pair32 = shape(F32, 2, length, HD)
    one16 = shape(BF16, length, HD)
    both16 = shape(BF16, length, columns)

    far = [step for step in others if step & (step - 1)]
    near = [step for step in others if not step & (step - 1)]
    order = far + near
    plan = [(step, step in far) for step in order]

    def slice_for(step, halves):
        rows = HD // 2 if halves else HD
        begin = core * HD + side * rows if halves else core * HD
        return lax.dynamic_slice(out_weight, (begin, (place ^ step) * width), (rows, width))

    slices = [slice_for(step, halves) for step, halves in plan]
    arriving = [swap_tensor(piece, step) for piece, step in zip(slices, order)]
    got = [swap_core(rows) for rows in (queries, keys, values)]
    got.append(swap_core(log_decay))
    (weight,) = after([out_weight], *slices)
    weight_own = lax.dynamic_slice(weight, (0, place * width), (columns, width))
    got = after(got, weight_own)
    (grad,) = after([out_grad], *got)
    grad_got = swap_core(grad)
    q, k, v, col, row, first, fresh = call(
        fresh_kernel,
        "fresh",
        [pair16, pair16, pair16, shape(F32, length, 2), shape(F32, 2, length), shape(F32, HD, HD), message],
        [where, queries, keys, values, *got[:3], log_decay, got[3]],
    )
    (fresh,) = after([fresh], grad_got)
    arrived, window, step = [], fresh, 1
    while step < chips:
        if arrived:
            (window,) = call(without_where(join_kernel), "join", [message], [where, window, arrived[-1]])
        arrived.append(to_chip(window, step))
        step *= 2
    (inner,) = call(without_where(inner_kernel), "inner", [pair32], [where, q, k, v, col, row, first])
    pieces = [("own", [weight_own])]
    for (step, halves), piece in zip(plan, arriving):
        if halves:
            (piece,) = after([piece], arrived[0])
        pieces.append(("halves", [piece, swap_side(piece)]) if halves else ("whole", [piece]))
    partials, mine, theirs = [], [], []
    for number in range(0, tensor, 2):
        kinds, sources = zip(*pieces[number : number + 2])
        sources = after(sum(sources, []), arrived[0], inner, *partials)
        *outs, weight = call(
            functools.partial(partial_kernel, kinds),
            "partial",
            [pair16 if number else pair32, pair16, shape(BF16, 2 * HD if number else HD, width)],
            [where, out_grad, grad_got, *sources],
        )
        partials += outs
        mine.append(weight)
        if number == 0:
            theirs.append(swap_core(weight))
    own_partial, *partials = partials
    sent = [swap_tensor(partial, step) for partial, step in zip(partials, order)]
    mixed, normed, states = call(
        mixed_kernel,
        "mixed",
        [pair32, pair16, shape(F32, 2, HD, HD)],
        [where, q, col, inner, gain, first, *after(arrived, *partials)],
    )
    normed_all = [normed] + [swap_tensor(normed, step) for step in order]
    grad_mixed, second, upward = call(
        grad_mixed_kernel,
        "grad_mixed",
        [pair32, shape(F32, HD, HD), message],
        [where, q, col, gain, mixed, own_partial, *sent],
    )
    (upward,) = after([upward], *normed_all)
    (cross,) = call(cross_kernel, "cross", [shape(BF16, tensor, length, HD)], [where, *normed_all])
    cross_got = swap_core(cross)
    returned = [to_chip(upward, -step) for step in reversed(range(1, chips))][::-1]
    theirs += [swap_core(weight) for weight in after(mine[1:], upward)]
    inner_keep, inner_send = call(
        inner_grad_kernel,
        "inner_grad",
        [shape(F32, length, 4 * HD)] * 2,
        [where, q, k, v, col, row, grad_mixed, states, second],
    )
    (layer_out,) = call(
        functools.partial(layer_kernel, tensor // 2),
        "layer",
        [shape(BF16, length, width)],
        [where, weight_own, *mine, *theirs, *normed_all, cross_got],
    )
    returned = after(returned, layer_out)
    inner_got = swap_core(*after([inner_send], *returned))
    returned_got = [swap_core(rows) for rows in returned]
    query_grad, key_grad, value_grad = call(
        functools.partial(outer_grad_kernel, chips - 1),
        "outer_grad",
        [both16] * 3,
        [where, keys, values, inner_keep, inner_got, *returned, *returned_got],
    )
    return layer_out, query_grad, key_grad, value_grad


def solution(mesh):
    in_specs = (
        P("seq", "tensor"),
        P("seq", "tensor"),
        P("seq", "tensor"),
        P("tensor", "seq"),
        P("tensor"),
        P("tensor", None),
        P("seq", "tensor"),
    )
    out_specs = (P("seq", "tensor"), P("seq", "tensor"), P("seq", "tensor"), P("seq", "tensor"))
    return jax.shard_map(
        on_device, mesh=mesh, in_specs=in_specs, out_specs=out_specs, check_vma=False
    )
```

```python
import functools

import jax
import jax.numpy as jnp
from jax import lax
from jax.experimental import pallas as pl
from jax.experimental.pallas import tpu as pltpu
from jax.sharding import PartitionSpec as P

EXACT = lax.Precision.HIGHEST
EPSILON = 1e-05
F32 = jnp.float32
BF16 = jnp.bfloat16
TAIL = 16
HD = 128

NN = (((1,), (0,)), ((), ()))
NT = (((1,), (1,)), ((), ()))
TN = (((0,), (0,)), ((), ()))


def dot(a, b, dims):
    return lax.dot_general(a, b, dims, preferred_element_type=F32)


def split(x):
    high = x.astype(BF16)
    return high, (x - high.astype(F32)).astype(BF16)


def dot_fb(a, b, dims):
    high, low = split(a)
    return dot(high, b, dims) + dot(low, b, dims)


def dot_bf(a, b, dims):
    high, low = split(b)
    return dot(a, high, dims) + dot(a, low, dims)


def dot_ff(a, b, dims):
    ah, al = split(a)
    bh, bl = split(b)
    return dot(ah, bh, dims) + (dot(ah, bl, dims) + dot(al, bh, dims))


def triangle(length):
    rows = lax.broadcasted_iota(jnp.int32, (length, length), 0)
    cols = lax.broadcasted_iota(jnp.int32, (length, length), 1)
    return rows >= cols


def running_columns(decay, lower):
    return lax.dot_general(lower.astype(F32), decay, NT, precision=EXACT, preferred_element_type=F32)


def running_rows(decay, lower):
    return lax.dot_general(decay, lower.astype(F32), NT, precision=EXACT, preferred_element_type=F32)


def put_total(ref, base, total):
    first = total.astype(BF16).astype(F32)
    second = (total - first).astype(BF16).astype(F32)
    third = total - first - second
    at = lax.broadcasted_iota(jnp.int32, (TAIL, 128), 0)
    tail = jnp.where(at == 0, first, jnp.where(at == 1, second, jnp.where(at == 2, third, 0.0)))
    ref[base : base + TAIL, :] = tail.astype(BF16)


def get_total(ref, base):
    tail = ref[base : base + TAIL, :].astype(F32)
    return tail[0:1] + tail[1:2] + tail[2:3]


def total_of(columns, block):
    length = columns.shape[0]
    return jnp.broadcast_to(columns[length - 1 : length, block : block + 1], (1, HD))


def chip_sum(refs):
    summed = jnp.zeros((HD, HD), F32)
    passed = jnp.zeros((1, HD), F32)
    for ref in refs:
        summed = summed + jnp.exp(passed) * ref[0:HD, :].astype(F32)
        passed = passed + get_total(ref, HD)
    return summed


def put_message(ref, state, total):
    ref[0:HD, :] = state.astype(BF16)
    put_total(ref, HD, total)


def join_kernel(own_ref, got_ref, out_ref):
    total = get_total(own_ref, HD)
    state = own_ref[0:HD, :].astype(F32) + jnp.exp(total) * got_ref[0:HD, :].astype(F32)
    put_message(out_ref, state, total + get_total(got_ref, HD))


def cross_kernel(where_ref, *refs):
    *normed_refs, cross_ref = refs
    for number, ref in enumerate(normed_refs):
        cross_ref[number] = ref[1 - where_ref[0]]


def lanes_of(number):
    return pl.ds(pl.multiple_of(number * HD, HD), HD)


def rows_of(number, count):
    return pl.ds(pl.multiple_of(number * count, count), count)


def fresh_kernel(
    where_ref, q_ref, k_ref, v_ref, q_got, k_got, v_got, decay_ref, decay_got, q_out, k_out, v_out, col_ref, row_ref, first_ref, message_ref
):
    core = where_ref[0]
    length = q_ref.shape[0]
    for out, ref, got in ((q_out, q_ref, q_got), (k_out, k_ref, k_got), (v_out, v_ref, v_got)):
        out[core] = ref[:, lanes_of(core)]
        out[1 - core] = got[:, lanes_of(core)]
    mine = jnp.where(core == 0, decay_ref[0:1, :], decay_ref[1:2, :])
    theirs = jnp.where(core == 0, decay_got[0:1, :], decay_got[1:2, :])
    block = lax.broadcasted_iota(jnp.int32, (2, length), 0)
    decay = jnp.where(block == core, mine, theirs)
    lower = triangle(length)
    columns = running_columns(decay, lower)
    col_ref[...] = columns
    row_ref[...] = running_rows(decay, lower)
    states = []
    for b in range(2):
        fade = jnp.exp(columns[length - 1 : length, b : b + 1] - columns[:, b : b + 1])
        states.append(dot_bf(k_out[b], fade * v_out[b].astype(F32), TN))
    totals = [total_of(columns, b) for b in range(2)]
    first_ref[...] = states[0]
    put_message(message_ref, jnp.exp(totals[1]) * states[0] + states[1], totals[0] + totals[1])


def weights(columns, across, lower, b):
    return jnp.exp(jnp.where(lower, columns[:, b : b + 1] - across[b : b + 1, :], -1e30))


def inner_kernel(q_ref, k_ref, v_ref, col_ref, row_ref, first_ref, inner_ref):
    columns, across = col_ref[...], row_ref[...]
    lower = triangle(columns.shape[0])
    for b in range(2):
        scores = dot(q_ref[b], k_ref[b], NT) * weights(columns, across, lower, b)
        inner = dot_fb(scores, v_ref[b], NN)
        if b == 1:
            inner = inner + jnp.exp(columns[:, 1:2]) * dot_bf(q_ref[b], first_ref[...], NN)
        inner_ref[b] = inner


def scale_of(mixed):
    return lax.rsqrt(jnp.mean(mixed * mixed, axis=-1, keepdims=True) + EPSILON)


def mixed_kernel(where_ref, q_ref, col_ref, inner_ref, gain_ref, first_ref, *refs):
    chip_refs, (mixed_ref, normed_ref, state_ref) = refs[:-3], refs[-3:]
    core = where_ref[0]
    columns = col_ref[...]
    gain = gain_ref[:, lanes_of(core)]
    state = chip_sum(chip_refs)
    high, low = split(state)
    shrink = jnp.exp(total_of(columns, 0))
    state_ref[0] = state
    state_ref[1] = shrink * state + first_ref[...]
    for b in range(2):
        grow = jnp.exp(columns[:, b : b + 1])
        if b == 1:
            grow = grow * shrink
        mixed = inner_ref[b] + grow * (dot(q_ref[b], high, NN) + dot(q_ref[b], low, NN))
        mixed_ref[b] = mixed
        normed_ref[b] = (mixed * scale_of(mixed) * gain).astype(BF16)


def partial_kernel(kinds, where_ref, grad_ref, got_ref, *refs):
    core, side = where_ref[0], where_ref[1]
    refs = list(refs)
    inputs = [[refs.pop(0) for _ in range(2 if kind == "halves" else 1)] for kind in kinds]
    *products, weight_out = refs
    weights = []
    for kind, sources in zip(kinds, inputs):
        if kind == "own":
            weights.append(sources[0][rows_of(core, HD), :])
        elif kind == "halves":
            mine, theirs = sources[0][...], sources[1][...]
            weights += [jnp.where(side == 0, mine, theirs), jnp.where(side == 0, theirs, mine)]
        else:
            weights.append(sources[0][...])
    weight = jnp.concatenate(weights, axis=0)
    weight_out[...] = weight[2 * HD - weight_out.shape[0] :]
    for block, ref in ((core, grad_ref), (1 - core, got_ref)):
        product = dot(ref[...], weight, NT)
        for number, out in enumerate(products):
            out[block] = product[:, number * HD : (number + 1) * HD].astype(out.dtype)


def grad_mixed_kernel(where_ref, q_ref, col_ref, gain_ref, mixed_ref, own_ref, *refs):
    part_refs, (grad_ref, second_ref, message_ref) = refs[:-3], refs[-3:]
    columns = col_ref[...]
    gain = gain_ref[:, lanes_of(where_ref[0])]
    ups = []
    for b in range(2):
        normed = own_ref[b]
        for ref in part_refs:
            normed = normed + ref[b].astype(F32)
        lifted = normed * gain
        mixed = mixed_ref[b]
        scale = scale_of(mixed)
        unit = mixed * scale
        grad = scale * (lifted - unit * jnp.mean(unit * lifted, axis=-1, keepdims=True))
        grad_ref[b] = grad
        ups.append(dot_bf(q_ref[b], jnp.exp(columns[:, b : b + 1]) * grad, TN))
    second_ref[...] = ups[1]
    totals = [total_of(columns, b) for b in range(2)]
    put_message(message_ref, ups[0] + jnp.exp(totals[0]) * ups[1], totals[0] + totals[1])


def inner_grad_kernel(
    where_ref, q_ref, k_ref, v_ref, col_ref, row_ref, grad_ref, state_ref, second_ref, keep_ref, send_ref
):
    core = where_ref[0]
    columns, across = col_ref[...], row_ref[...]
    length = columns.shape[0]
    lower = triangle(length)
    parts = []
    ends = [columns[length - 1 : length, b : b + 1] for b in range(2)]
    for b in range(2):
        q, k, v, grad = q_ref[b], k_ref[b], v_ref[b], grad_ref[b]
        weight = weights(columns, across, lower, b)
        scores = dot(q, k, NT) * weight
        grad_scores = dot_fb(grad, v, NT) * weight
        carried = jnp.exp(columns[:, b : b + 1]) * dot_ff(grad, state_ref[b], NT)
        dq = dot_fb(grad_scores, k, NN) + carried
        dk = dot_fb(grad_scores, q, TN)
        dv = dot_ff(scores, grad, TN)
        fade = jnp.exp(ends[b] - columns[:, b : b + 1])
        if b == 0:
            dk = dk + fade * dot_bf(v, second_ref[...], NT)
            dv = dv + fade * dot_bf(k, second_ref[...], NN)
            fade = fade * jnp.exp(ends[1])
        parts.append((dq, dk, dv, jnp.broadcast_to(fade, (length, HD))))
    for number, (early, late) in enumerate(zip(*parts)):
        part = slice(number * HD, (number + 1) * HD)
        keep_ref[:, part] = jnp.where(core == 0, early, late)
        send_ref[:, part] = jnp.where(core == 0, late, early)


def outer_grad_kernel(count, where_ref, k_ref, v_ref, inner_ref, inner_got_ref, *refs):
    core = where_ref[0]
    outs = refs[2 * count :]
    for head, inner, chip_refs in (
        (core, inner_ref, refs[:count][::-1]),
        (1 - core, inner_got_ref, refs[count : 2 * count][::-1]),
    ):
        high, low = split(chip_sum(chip_refs))
        fade = inner[:, 3 * HD : 4 * HD]
        k, v = k_ref[:, lanes_of(head)], v_ref[:, lanes_of(head)]
        outs[0][:, lanes_of(head)] = inner[:, 0:HD].astype(BF16)
        key = inner[:, HD : 2 * HD] + fade * (dot(v, high, NT) + dot(v, low, NT))
        outs[1][:, lanes_of(head)] = key.astype(BF16)
        value = inner[:, 2 * HD : 3 * HD] + fade * (dot(k, high, NN) + dot(k, low, NN))
        outs[2][:, lanes_of(head)] = value.astype(BF16)


def layer_kernel(pairs, where_ref, own_ref, *refs):
    mine_refs, theirs_refs = refs[:pairs], refs[pairs : 2 * pairs]
    *normed_refs, got_ref, out_ref = refs[2 * pairs :]
    core = where_ref[0]
    mine = [ref[core] for ref in normed_refs]
    theirs = [got_ref[number] for number in range(got_ref.shape[0])]
    normed = [mine[0], theirs[0], mine[1], theirs[1]]
    for begin in range(2, len(mine), 2):
        normed += mine[begin : begin + 2] + theirs[begin : begin + 2]
    normed = jnp.concatenate(normed, axis=1)
    width = own_ref.shape[1]
    step = 512 if width % 512 == 0 else 128
    for begin in range(0, width, step):
        lanes = slice(begin, begin + step)
        weight = [own_ref[rows_of(core, HD), lanes], own_ref[rows_of(1 - core, HD), lanes]]
        for mine_ref, theirs_ref in zip(mine_refs, theirs_refs):
            weight += [mine_ref[:, lanes], theirs_ref[:, lanes]]
        out_ref[:, lanes] = dot(normed, jnp.concatenate(weight, axis=0), NN).astype(BF16)


SMEM = pl.BlockSpec(memory_space=pltpu.SMEM)
VMEM = pl.BlockSpec(memory_space=pltpu.VMEM)


def call(kernel, name, outs, args, grant=16):
    return pl.pallas_call(
        kernel,
        name=name,
        out_shape=outs,
        in_specs=[SMEM] + [VMEM] * (len(args) - 1),
        out_specs=[VMEM] * len(outs),
        compiler_params=pltpu.CompilerParams(vmem_limit_bytes=grant * 2**20),
        cost_estimate=pl.CostEstimate(flops=1, bytes_accessed=1, transcendentals=0),
    )(*args)


def without_where(kernel):
    return lambda where_ref, *refs: kernel(*refs)


def after(values, *earlier):
    tied = lax.optimization_barrier((tuple(values), earlier))
    return list(tied[0])


def on_device(queries, keys, values, log_decay, norm_gain, out_weight, out_grad):
    length, columns = queries.shape
    seq = lax.axis_size("seq")
    tensor = lax.axis_size("tensor")
    chips = seq // 2
    model = out_weight.shape[1]
    width = model // tensor
    place = lax.axis_index("tensor")
    core = lax.rem(lax.axis_index("seq"), 2)
    side = lax.rem(lax.axis_index("seq") // 2, 2)
    where = jnp.stack([core, side]).astype(jnp.int32)
    gain = norm_gain.reshape(1, columns)

    def swap_tensor(value, k):
        return lax.ppermute(value, "tensor", [(i, i ^ k) for i in range(tensor)])

    def swap_core(value):
        return lax.ppermute(value, "seq", [(i, i ^ 1) for i in range(seq)])

    def swap_side(value):
        return lax.ppermute(value, "seq", [(i, i ^ 2) for i in range(seq)])

    def to_chip(value, step):
        return lax.ppermute(
            value, "seq", [(i, i + 2 * step) for i in range(seq) if 0 <= i + 2 * step < seq]
        )

    def shape(dtype, *dims):
        return jax.ShapeDtypeStruct(dims, dtype)

    others = range(1, tensor)
    message = shape(BF16, HD + TAIL, HD)
    pair16 = shape(BF16, 2, length, HD)
    pair32 = shape(F32, 2, length, HD)
    one16 = shape(BF16, length, HD)
    both16 = shape(BF16, length, columns)

    far = [step for step in others if step & (step - 1)]
    near = [step for step in others if not step & (step - 1)]
    order = far + near
    plan = [(step, step in far) for step in order]

    def slice_for(step, halves):
        rows = HD // 2 if halves else HD
        begin = core * HD + side * rows if halves else core * HD
        return lax.dynamic_slice(out_weight, (begin, (place ^ step) * width), (rows, width))

    slices = [slice_for(step, halves) for step, halves in plan]
    arriving = [swap_tensor(piece, step) for piece, step in zip(slices, order)]
    got = [swap_core(rows) for rows in (queries, keys, values)]
    got.append(swap_core(log_decay))
    (weight,) = after([out_weight], *slices)
    weight_own = lax.dynamic_slice(weight, (0, place * width), (columns, width))
    got = after(got, weight_own)
    (grad,) = after([out_grad], *got)
    grad_got = swap_core(grad)
    q, k, v, col, row, first, fresh = call(
        fresh_kernel,
        "fresh",
        [pair16, pair16, pair16, shape(F32, length, 2), shape(F32, 2, length), shape(F32, HD, HD), message],
        [where, queries, keys, values, *got[:3], log_decay, got[3]],
    )
    (fresh,) = after([fresh], grad_got)
    arrived, window, step = [], fresh, 1
    while step < chips:
        if arrived:
            (window,) = call(without_where(join_kernel), "join", [message], [where, window, arrived[-1]])
        arrived.append(to_chip(window, step))
        step *= 2
    (inner,) = call(without_where(inner_kernel), "inner", [pair32], [where, q, k, v, col, row, first])
    pieces = [("own", [weight_own])]
    for (step, halves), piece in zip(plan, arriving):
        if halves:
            (piece,) = after([piece], arrived[0])
        pieces.append(("halves", [piece, swap_side(piece)]) if halves else ("whole", [piece]))
    partials, mine, theirs = [], [], []
    for number in range(0, tensor, 2):
        kinds, sources = zip(*pieces[number : number + 2])
        sources = after(sum(sources, []), *arrived, inner, *partials)
        *outs, weight = call(
            functools.partial(partial_kernel, kinds),
            "partial",
            [pair16 if number else pair32, pair16, shape(BF16, 2 * HD if number else HD, width)],
            [where, out_grad, grad_got, *sources],
        )
        partials += outs
        mine.append(weight)
        if number == 0:
            theirs.append(swap_core(weight))
    own_partial, *partials = partials
    sent = [swap_tensor(partial, step) for partial, step in zip(partials, order)]
    mixed, normed, states = call(
        mixed_kernel,
        "mixed",
        [pair32, pair16, shape(F32, 2, HD, HD)],
        [where, q, col, inner, gain, first, *after(arrived, *partials)],
    )
    normed_all = [normed] + [swap_tensor(normed, step) for step in order]
    grad_mixed, second, upward = call(
        grad_mixed_kernel,
        "grad_mixed",
        [pair32, shape(F32, HD, HD), message],
        [where, q, col, gain, mixed, own_partial, *sent],
    )
    (upward,) = after([upward], *normed_all)
    (cross,) = call(cross_kernel, "cross", [shape(BF16, tensor, length, HD)], [where, *normed_all])
    cross_got = swap_core(cross)
    returned = [to_chip(upward, -step) for step in reversed(range(1, chips))]
    theirs += [swap_core(weight) for weight in after(mine[1:], upward)]
    inner_keep, inner_send = call(
        inner_grad_kernel,
        "inner_grad",
        [shape(F32, length, 4 * HD)] * 2,
        [where, q, k, v, col, row, grad_mixed, states, second],
    )
    (layer_out,) = call(
        functools.partial(layer_kernel, tensor // 2),
        "layer",
        [shape(BF16, length, width)],
        [where, weight_own, *mine, *theirs, *normed_all, cross_got],
    )
    returned = after(returned, layer_out)
    inner_got = swap_core(*after([inner_send], *returned))
    returned_got = [swap_core(rows) for rows in returned]
    query_grad, key_grad, value_grad = call(
        functools.partial(outer_grad_kernel, chips - 1),
        "outer_grad",
        [both16] * 3,
        [where, keys, values, inner_keep, inner_got, *returned, *returned_got],
    )
    return layer_out, query_grad, key_grad, value_grad


def solution(mesh):
    in_specs = (
        P("seq", "tensor"),
        P("seq", "tensor"),
        P("seq", "tensor"),
        P("tensor", "seq"),
        P("tensor"),
        P("tensor", None),
        P("seq", "tensor"),
    )
    out_specs = (P("seq", "tensor"), P("seq", "tensor"), P("seq", "tensor"), P("seq", "tensor"))
    return jax.shard_map(
        on_device, mesh=mesh, in_specs=in_specs, out_specs=out_specs, check_vma=False
    )
```

```python
import functools

import jax
import jax.numpy as jnp
from jax import lax
from jax.experimental import pallas as pl
from jax.experimental.pallas import tpu as pltpu
from jax.sharding import PartitionSpec as P

EXACT = lax.Precision.HIGHEST
EPSILON = 1e-05
F32 = jnp.float32
BF16 = jnp.bfloat16
TAIL = 16
HD = 128

NN = (((1,), (0,)), ((), ()))
NT = (((1,), (1,)), ((), ()))
TN = (((0,), (0,)), ((), ()))


def dot(a, b, dims):
    return lax.dot_general(a, b, dims, preferred_element_type=F32)


def split(x):
    high = x.astype(BF16)
    return high, (x - high.astype(F32)).astype(BF16)


def dot_fb(a, b, dims):
    high, low = split(a)
    return dot(high, b, dims) + dot(low, b, dims)


def dot_bf(a, b, dims):
    high, low = split(b)
    return dot(a, high, dims) + dot(a, low, dims)


def dot_ff(a, b, dims):
    ah, al = split(a)
    bh, bl = split(b)
    return dot(ah, bh, dims) + (dot(ah, bl, dims) + dot(al, bh, dims))


def triangle(length):
    rows = lax.broadcasted_iota(jnp.int32, (length, length), 0)
    cols = lax.broadcasted_iota(jnp.int32, (length, length), 1)
    return rows >= cols


def running_columns(decay, lower):
    return lax.dot_general(lower.astype(F32), decay, NT, precision=EXACT, preferred_element_type=F32)


def running_rows(decay, lower):
    return lax.dot_general(decay, lower.astype(F32), NT, precision=EXACT, preferred_element_type=F32)


def put_total(ref, base, total):
    first = total.astype(BF16).astype(F32)
    second = (total - first).astype(BF16).astype(F32)
    third = total - first - second
    at = lax.broadcasted_iota(jnp.int32, (TAIL, 128), 0)
    tail = jnp.where(at == 0, first, jnp.where(at == 1, second, jnp.where(at == 2, third, 0.0)))
    ref[base : base + TAIL, :] = tail.astype(BF16)


def get_total(ref, base):
    tail = ref[base : base + TAIL, :].astype(F32)
    return tail[0:1] + tail[1:2] + tail[2:3]


def total_of(columns, block):
    length = columns.shape[0]
    return jnp.broadcast_to(columns[length - 1 : length, block : block + 1], (1, HD))


def chip_sum(refs):
    summed = jnp.zeros((HD, HD), F32)
    passed = jnp.zeros((1, HD), F32)
    for ref in refs:
        summed = summed + jnp.exp(passed) * ref[0:HD, :].astype(F32)
        passed = passed + get_total(ref, HD)
    return summed


def put_message(ref, state, total):
    ref[0:HD, :] = state.astype(BF16)
    put_total(ref, HD, total)


def join_kernel(own_ref, got_ref, out_ref):
    total = get_total(own_ref, HD)
    state = own_ref[0:HD, :].astype(F32) + jnp.exp(total) * got_ref[0:HD, :].astype(F32)
    put_message(out_ref, state, total + get_total(got_ref, HD))


def cross_kernel(where_ref, *refs):
    *normed_refs, cross_ref = refs
    for number, ref in enumerate(normed_refs):
        cross_ref[number] = ref[1 - where_ref[0]]


def lanes_of(number):
    return pl.ds(pl.multiple_of(number * HD, HD), HD)


def rows_of(number, count):
    return pl.ds(pl.multiple_of(number * count, count), count)


def fresh_kernel(
    where_ref, q_ref, k_ref, v_ref, q_got, k_got, v_got, decay_ref, decay_got, q_out, k_out, v_out, col_ref, row_ref, first_ref, message_ref
):
    core = where_ref[0]
    length = q_ref.shape[0]
    for out, ref, got in ((q_out, q_ref, q_got), (k_out, k_ref, k_got), (v_out, v_ref, v_got)):
        out[core] = ref[:, lanes_of(core)]
        out[1 - core] = got[:, lanes_of(core)]
    mine = jnp.where(core == 0, decay_ref[0:1, :], decay_ref[1:2, :])
    theirs = jnp.where(core == 0, decay_got[0:1, :], decay_got[1:2, :])
    block = lax.broadcasted_iota(jnp.int32, (2, length), 0)
    decay = jnp.where(block == core, mine, theirs)
    lower = triangle(length)
    columns = running_columns(decay, lower)
    col_ref[...] = columns
    row_ref[...] = running_rows(decay, lower)
    states = []
    for b in range(2):
        fade = jnp.exp(columns[length - 1 : length, b : b + 1] - columns[:, b : b + 1])
        states.append(dot_bf(k_out[b], fade * v_out[b].astype(F32), TN))
    totals = [total_of(columns, b) for b in range(2)]
    first_ref[...] = states[0]
    put_message(message_ref, jnp.exp(totals[1]) * states[0] + states[1], totals[0] + totals[1])


def weights(columns, across, lower, b):
    return jnp.exp(jnp.where(lower, columns[:, b : b + 1] - across[b : b + 1, :], -1e30))


def inner_kernel(q_ref, k_ref, v_ref, col_ref, row_ref, first_ref, inner_ref):
    columns, across = col_ref[...], row_ref[...]
    lower = triangle(columns.shape[0])
    for b in range(2):
        scores = dot(q_ref[b], k_ref[b], NT) * weights(columns, across, lower, b)
        inner = dot_fb(scores, v_ref[b], NN)
        if b == 1:
            inner = inner + jnp.exp(columns[:, 1:2]) * dot_bf(q_ref[b], first_ref[...], NN)
        inner_ref[b] = inner


def scale_of(mixed):
    return lax.rsqrt(jnp.mean(mixed * mixed, axis=-1, keepdims=True) + EPSILON)


def mixed_kernel(where_ref, q_ref, col_ref, inner_ref, gain_ref, first_ref, *refs):
    chip_refs, (mixed_ref, normed_ref, state_ref) = refs[:-3], refs[-3:]
    core = where_ref[0]
    columns = col_ref[...]
    gain = gain_ref[:, lanes_of(core)]
    state = chip_sum(chip_refs)
    high, low = split(state)
    shrink = jnp.exp(total_of(columns, 0))
    state_ref[0] = state
    state_ref[1] = shrink * state + first_ref[...]
    for b in range(2):
        grow = jnp.exp(columns[:, b : b + 1])
        if b == 1:
            grow = grow * shrink
        mixed = inner_ref[b] + grow * (dot(q_ref[b], high, NN) + dot(q_ref[b], low, NN))
        mixed_ref[b] = mixed
        normed_ref[b] = (mixed * scale_of(mixed) * gain).astype(BF16)


def partial_kernel(kinds, where_ref, grad_ref, got_ref, *refs):
    core, side = where_ref[0], where_ref[1]
    refs = list(refs)
    inputs = [[refs.pop(0) for _ in range(2 if kind == "halves" else 1)] for kind in kinds]
    *products, weight_out = refs
    weights = []
    for kind, sources in zip(kinds, inputs):
        if kind == "own":
            weights.append(sources[0][rows_of(core, HD), :])
        elif kind == "halves":
            mine, theirs = sources[0][...], sources[1][...]
            weights += [jnp.where(side == 0, mine, theirs), jnp.where(side == 0, theirs, mine)]
        else:
            weights.append(sources[0][...])
    weight = jnp.concatenate(weights, axis=0)
    weight_out[...] = weight[2 * HD - weight_out.shape[0] :]
    for block, ref in ((core, grad_ref), (1 - core, got_ref)):
        product = dot(ref[...], weight, NT)
        for number, out in enumerate(products):
            out[block] = product[:, number * HD : (number + 1) * HD].astype(out.dtype)


def grad_mixed_kernel(where_ref, q_ref, col_ref, gain_ref, mixed_ref, own_ref, *refs):
    part_refs, (grad_ref, second_ref, message_ref) = refs[:-3], refs[-3:]
    columns = col_ref[...]
    gain = gain_ref[:, lanes_of(where_ref[0])]
    ups = []
    for b in range(2):
        normed = own_ref[b]
        for ref in part_refs:
            normed = normed + ref[b].astype(F32)
        lifted = normed * gain
        mixed = mixed_ref[b]
        scale = scale_of(mixed)
        unit = mixed * scale
        grad = scale * (lifted - unit * jnp.mean(unit * lifted, axis=-1, keepdims=True))
        grad_ref[b] = grad
        ups.append(dot_bf(q_ref[b], jnp.exp(columns[:, b : b + 1]) * grad, TN))
    second_ref[...] = ups[1]
    totals = [total_of(columns, b) for b in range(2)]
    put_message(message_ref, ups[0] + jnp.exp(totals[0]) * ups[1], totals[0] + totals[1])


def inner_grad_kernel(
    where_ref, q_ref, k_ref, v_ref, col_ref, row_ref, grad_ref, state_ref, second_ref, keep_ref, send_ref
):
    core = where_ref[0]
    columns, across = col_ref[...], row_ref[...]
    length = columns.shape[0]
    lower = triangle(length)
    parts = []
    ends = [columns[length - 1 : length, b : b + 1] for b in range(2)]
    for b in range(2):
        q, k, v, grad = q_ref[b], k_ref[b], v_ref[b], grad_ref[b]
        weight = weights(columns, across, lower, b)
        scores = dot(q, k, NT) * weight
        grad_scores = dot_fb(grad, v, NT) * weight
        carried = jnp.exp(columns[:, b : b + 1]) * dot_ff(grad, state_ref[b], NT)
        dq = dot_fb(grad_scores, k, NN) + carried
        dk = dot_fb(grad_scores, q, TN)
        dv = dot_ff(scores, grad, TN)
        fade = jnp.exp(ends[b] - columns[:, b : b + 1])
        if b == 0:
            dk = dk + fade * dot_bf(v, second_ref[...], NT)
            dv = dv + fade * dot_bf(k, second_ref[...], NN)
            fade = fade * jnp.exp(ends[1])
        parts.append((dq, dk, dv, jnp.broadcast_to(fade, (length, HD))))
    for number, (early, late) in enumerate(zip(*parts)):
        part = slice(number * HD, (number + 1) * HD)
        keep_ref[:, part] = jnp.where(core == 0, early, late)
        send_ref[:, part] = jnp.where(core == 0, late, early)


def outer_grad_kernel(count, where_ref, k_ref, v_ref, inner_ref, inner_got_ref, *refs):
    core = where_ref[0]
    outs = refs[2 * count :]
    for head, inner, chip_refs in (
        (core, inner_ref, refs[:count][::-1]),
        (1 - core, inner_got_ref, refs[count : 2 * count][::-1]),
    ):
        high, low = split(chip_sum(chip_refs))
        fade = inner[:, 3 * HD : 4 * HD]
        k, v = k_ref[:, lanes_of(head)], v_ref[:, lanes_of(head)]
        outs[0][:, lanes_of(head)] = inner[:, 0:HD].astype(BF16)
        key = inner[:, HD : 2 * HD] + fade * (dot(v, high, NT) + dot(v, low, NT))
        outs[1][:, lanes_of(head)] = key.astype(BF16)
        value = inner[:, 2 * HD : 3 * HD] + fade * (dot(k, high, NN) + dot(k, low, NN))
        outs[2][:, lanes_of(head)] = value.astype(BF16)


def layer_kernel(pairs, where_ref, own_ref, *refs):
    mine_refs, theirs_refs = refs[:pairs], refs[pairs : 2 * pairs]
    *normed_refs, got_ref, out_ref = refs[2 * pairs :]
    core = where_ref[0]
    mine = [ref[core] for ref in normed_refs]
    theirs = [got_ref[number] for number in range(got_ref.shape[0])]
    normed = [mine[0], theirs[0], mine[1], theirs[1]]
    for begin in range(2, len(mine), 2):
        normed += mine[begin : begin + 2] + theirs[begin : begin + 2]
    normed = jnp.concatenate(normed, axis=1)
    width = own_ref.shape[1]
    step = 512 if width % 512 == 0 else 128
    for begin in range(0, width, step):
        lanes = slice(begin, begin + step)
        weight = [own_ref[rows_of(core, HD), lanes], own_ref[rows_of(1 - core, HD), lanes]]
        for mine_ref, theirs_ref in zip(mine_refs, theirs_refs):
            weight += [mine_ref[:, lanes], theirs_ref[:, lanes]]
        out_ref[:, lanes] = dot(normed, jnp.concatenate(weight, axis=0), NN).astype(BF16)


SMEM = pl.BlockSpec(memory_space=pltpu.SMEM)
VMEM = pl.BlockSpec(memory_space=pltpu.VMEM)


def call(kernel, name, outs, args, grant=16):
    return pl.pallas_call(
        kernel,
        name=name,
        out_shape=outs,
        in_specs=[SMEM] + [VMEM] * (len(args) - 1),
        out_specs=[VMEM] * len(outs),
        compiler_params=pltpu.CompilerParams(vmem_limit_bytes=grant * 2**20),
        cost_estimate=pl.CostEstimate(flops=1, bytes_accessed=1, transcendentals=0),
    )(*args)


def without_where(kernel):
    return lambda where_ref, *refs: kernel(*refs)


def after(values, *earlier):
    tied = lax.optimization_barrier((tuple(values), earlier))
    return list(tied[0])


def on_device(queries, keys, values, log_decay, norm_gain, out_weight, out_grad):
    length, columns = queries.shape
    seq = lax.axis_size("seq")
    tensor = lax.axis_size("tensor")
    chips = seq // 2
    model = out_weight.shape[1]
    width = model // tensor
    place = lax.axis_index("tensor")
    core = lax.rem(lax.axis_index("seq"), 2)
    side = lax.rem(lax.axis_index("seq") // 2, 2)
    where = jnp.stack([core, side]).astype(jnp.int32)
    gain = norm_gain.reshape(1, columns)

    def swap_tensor(value, k):
        return lax.ppermute(value, "tensor", [(i, i ^ k) for i in range(tensor)])

    def swap_core(value):
        return lax.ppermute(value, "seq", [(i, i ^ 1) for i in range(seq)])

    def swap_side(value):
        return lax.ppermute(value, "seq", [(i, i ^ 2) for i in range(seq)])

    def to_chip(value, step):
        return lax.ppermute(
            value, "seq", [(i, i + 2 * step) for i in range(seq) if 0 <= i + 2 * step < seq]
        )

    def shape(dtype, *dims):
        return jax.ShapeDtypeStruct(dims, dtype)

    others = range(1, tensor)
    message = shape(BF16, HD + TAIL, HD)
    pair16 = shape(BF16, 2, length, HD)
    pair32 = shape(F32, 2, length, HD)
    one16 = shape(BF16, length, HD)
    both16 = shape(BF16, length, columns)

    far = [step for step in others if step & (step - 1)]
    near = [step for step in others if not step & (step - 1)]
    order = far + near
    plan = [(step, step in far) for step in order]

    def slice_for(step, halves):
        rows = HD // 2 if halves else HD
        begin = core * HD + side * rows if halves else core * HD
        return lax.dynamic_slice(out_weight, (begin, (place ^ step) * width), (rows, width))

    slices = [slice_for(step, halves) for step, halves in plan]
    arriving = [swap_tensor(piece, step) for piece, step in zip(slices, order)]
    got = [swap_core(rows) for rows in (queries, keys, values)]
    got.append(swap_core(log_decay))
    (weight,) = after([out_weight], *slices)
    weight_own = lax.dynamic_slice(weight, (0, place * width), (columns, width))
    got = after(got, weight_own)
    (grad,) = after([out_grad], *got)
    grad_got = swap_core(grad)
    q, k, v, col, row, first, fresh = call(
        fresh_kernel,
        "fresh",
        [pair16, pair16, pair16, shape(F32, length, 2), shape(F32, 2, length), shape(F32, HD, HD), message],
        [where, queries, keys, values, *got[:3], log_decay, got[3]],
    )
    (fresh,) = after([fresh], grad_got)
    arrived, window, step = [], fresh, 1
    while step < chips:
        if arrived:
            (window,) = call(without_where(join_kernel), "join", [message], [where, window, arrived[-1]])
        arrived.append(to_chip(window, step))
        step *= 2
    (inner,) = call(without_where(inner_kernel), "inner", [pair32], [where, q, k, v, col, row, first])
    pieces = [("own", [weight_own])]
    for (step, halves), piece in zip(plan, arriving):
        if halves:
            (piece,) = after([piece], arrived[0])
        pieces.append(("halves", [piece, swap_side(piece)]) if halves else ("whole", [piece]))
    partials, mine, theirs = [], [], []
    for number in range(0, tensor, 2):
        kinds, sources = zip(*pieces[number : number + 2])
        sources = after(sum(sources, []), *arrived, inner, *partials)
        *outs, weight = call(
            functools.partial(partial_kernel, kinds),
            "partial",
            [pair16 if number else pair32, pair16, shape(BF16, 2 * HD if number else HD, width)],
            [where, out_grad, grad_got, *sources],
        )
        partials += outs
        mine.append(weight)
        if number == 0:
            theirs.append(swap_core(weight))
    own_partial, *partials = partials
    sent = [swap_tensor(partial, step) for partial, step in zip(partials, order)]
    mixed, normed, states = call(
        mixed_kernel,
        "mixed",
        [pair32, pair16, shape(F32, 2, HD, HD)],
        [where, q, col, inner, gain, first, *after(arrived, *partials)],
    )
    theirs += [swap_core(weight) for weight in mine[1:]]
    sent = after(sent, *theirs)
    (normed_sent,) = after([normed], *sent)
    normed_all = [normed] + [swap_tensor(normed_sent, step) for step in order]
    grad_mixed, second, upward = call(
        grad_mixed_kernel,
        "grad_mixed",
        [pair32, shape(F32, HD, HD), message],
        [where, q, col, gain, mixed, own_partial, *sent],
    )
    (cross,) = call(cross_kernel, "cross", [shape(BF16, tensor, length, HD)], [where, *normed_all])
    cross_got = swap_core(cross)
    (upward,) = after([upward], normed_all[-1])
    returned = [to_chip(upward, -step) for step in reversed(range(1, chips))]
    inner_keep, inner_send = call(
        inner_grad_kernel,
        "inner_grad",
        [shape(F32, length, 4 * HD)] * 2,
        [where, q, k, v, col, row, grad_mixed, states, second],
    )
    inner_got = swap_core(*after([inner_send], *returned, *normed_all))
    returned_got = [swap_core(rows) for rows in returned]
    query_grad, key_grad, value_grad = call(
        functools.partial(outer_grad_kernel, chips - 1),
        "outer_grad",
        [both16] * 3,
        [where, keys, values, inner_keep, inner_got, *returned, *returned_got],
    )
    (cross_got,) = after([cross_got], key_grad)
    (layer_out,) = call(
        functools.partial(layer_kernel, tensor // 2),
        "layer",
        [shape(BF16, length, width)],
        [where, weight_own, *mine, *theirs, *normed_all, cross_got],
    )
    return layer_out, query_grad, key_grad, value_grad


def solution(mesh):
    in_specs = (
        P("seq", "tensor"),
        P("seq", "tensor"),
        P("seq", "tensor"),
        P("tensor", "seq"),
        P("tensor"),
        P("tensor", None),
        P("seq", "tensor"),
    )
    out_specs = (P("seq", "tensor"), P("seq", "tensor"), P("seq", "tensor"), P("seq", "tensor"))
    return jax.shard_map(
        on_device, mesh=mesh, in_specs=in_specs, out_specs=out_specs, check_vma=False
    )
```

```python
import functools

import jax
import jax.numpy as jnp
from jax import lax
from jax.experimental import pallas as pl
from jax.experimental.pallas import tpu as pltpu
from jax.sharding import PartitionSpec as P

EXACT = lax.Precision.HIGHEST
EPSILON = 1e-05
F32 = jnp.float32
BF16 = jnp.bfloat16
TAIL = 16
HD = 128

NN = (((1,), (0,)), ((), ()))
NT = (((1,), (1,)), ((), ()))
TN = (((0,), (0,)), ((), ()))


def dot(a, b, dims):
    return lax.dot_general(a, b, dims, preferred_element_type=F32)


def split(x):
    high = x.astype(BF16)
    return high, (x - high.astype(F32)).astype(BF16)


def dot_fb(a, b, dims):
    high, low = split(a)
    return dot(high, b, dims) + dot(low, b, dims)


def dot_bf(a, b, dims):
    high, low = split(b)
    return dot(a, high, dims) + dot(a, low, dims)


def dot_ff(a, b, dims):
    ah, al = split(a)
    bh, bl = split(b)
    return dot(ah, bh, dims) + (dot(ah, bl, dims) + dot(al, bh, dims))


def triangle(length):
    rows = lax.broadcasted_iota(jnp.int32, (length, length), 0)
    cols = lax.broadcasted_iota(jnp.int32, (length, length), 1)
    return rows >= cols


def running_columns(decay, lower):
    return lax.dot_general(lower.astype(F32), decay, NT, precision=EXACT, preferred_element_type=F32)


def running_rows(decay, lower):
    return lax.dot_general(decay, lower.astype(F32), NT, precision=EXACT, preferred_element_type=F32)


def put_total(ref, base, total):
    first = total.astype(BF16).astype(F32)
    second = (total - first).astype(BF16).astype(F32)
    third = total - first - second
    at = lax.broadcasted_iota(jnp.int32, (TAIL, 128), 0)
    tail = jnp.where(at == 0, first, jnp.where(at == 1, second, jnp.where(at == 2, third, 0.0)))
    ref[base : base + TAIL, :] = tail.astype(BF16)


def get_total(ref, base):
    tail = ref[base : base + TAIL, :].astype(F32)
    return tail[0:1] + tail[1:2] + tail[2:3]


def total_of(columns, block):
    length = columns.shape[0]
    return jnp.broadcast_to(columns[length - 1 : length, block : block + 1], (1, HD))


def chip_sum(refs):
    summed = jnp.zeros((HD, HD), F32)
    passed = jnp.zeros((1, HD), F32)
    for ref in refs:
        summed = summed + jnp.exp(passed) * ref[0:HD, :].astype(F32)
        passed = passed + get_total(ref, HD)
    return summed


def put_message(ref, state, total):
    ref[0:HD, :] = state.astype(BF16)
    put_total(ref, HD, total)


def join_kernel(own_ref, got_ref, out_ref):
    total = get_total(own_ref, HD)
    state = own_ref[0:HD, :].astype(F32) + jnp.exp(total) * got_ref[0:HD, :].astype(F32)
    put_message(out_ref, state, total + get_total(got_ref, HD))


def cross_kernel(where_ref, *refs):
    *normed_refs, cross_ref = refs
    for number, ref in enumerate(normed_refs):
        cross_ref[number] = ref[1 - where_ref[0]]


def lanes_of(number):
    return pl.ds(pl.multiple_of(number * HD, HD), HD)


def rows_of(number, count):
    return pl.ds(pl.multiple_of(number * count, count), count)


def fresh_kernel(
    where_ref, q_ref, k_ref, v_ref, q_got, k_got, v_got, decay_ref, decay_got, q_out, k_out, v_out, col_ref, row_ref, first_ref, message_ref
):
    core = where_ref[0]
    length = q_ref.shape[0]
    for out, ref, got in ((q_out, q_ref, q_got), (k_out, k_ref, k_got), (v_out, v_ref, v_got)):
        out[core] = ref[:, lanes_of(core)]
        out[1 - core] = got[:, lanes_of(core)]
    mine = jnp.where(core == 0, decay_ref[0:1, :], decay_ref[1:2, :])
    theirs = jnp.where(core == 0, decay_got[0:1, :], decay_got[1:2, :])
    block = lax.broadcasted_iota(jnp.int32, (2, length), 0)
    decay = jnp.where(block == core, mine, theirs)
    lower = triangle(length)
    columns = running_columns(decay, lower)
    col_ref[...] = columns
    row_ref[...] = running_rows(decay, lower)
    states = []
    for b in range(2):
        fade = jnp.exp(columns[length - 1 : length, b : b + 1] - columns[:, b : b + 1])
        states.append(dot_bf(k_out[b], fade * v_out[b].astype(F32), TN))
    totals = [total_of(columns, b) for b in range(2)]
    first_ref[...] = states[0]
    put_message(message_ref, jnp.exp(totals[1]) * states[0] + states[1], totals[0] + totals[1])


def weights(columns, across, lower, b):
    return jnp.exp(jnp.where(lower, columns[:, b : b + 1] - across[b : b + 1, :], -1e30))


def inner_kernel(q_ref, k_ref, v_ref, col_ref, row_ref, first_ref, inner_ref):
    columns, across = col_ref[...], row_ref[...]
    lower = triangle(columns.shape[0])
    for b in range(2):
        scores = dot(q_ref[b], k_ref[b], NT) * weights(columns, across, lower, b)
        inner = dot_fb(scores, v_ref[b], NN)
        if b == 1:
            inner = inner + jnp.exp(columns[:, 1:2]) * dot_bf(q_ref[b], first_ref[...], NN)
        inner_ref[b] = inner


def scale_of(mixed):
    return lax.rsqrt(jnp.mean(mixed * mixed, axis=-1, keepdims=True) + EPSILON)


def mixed_kernel(where_ref, q_ref, col_ref, inner_ref, gain_ref, first_ref, *refs):
    chip_refs, (mixed_ref, normed_ref, state_ref) = refs[:-3], refs[-3:]
    core = where_ref[0]
    columns = col_ref[...]
    gain = gain_ref[:, lanes_of(core)]
    state = chip_sum(chip_refs)
    high, low = split(state)
    shrink = jnp.exp(total_of(columns, 0))
    state_ref[0] = state
    state_ref[1] = shrink * state + first_ref[...]
    for b in range(2):
        grow = jnp.exp(columns[:, b : b + 1])
        if b == 1:
            grow = grow * shrink
        mixed = inner_ref[b] + grow * (dot(q_ref[b], high, NN) + dot(q_ref[b], low, NN))
        mixed_ref[b] = mixed
        normed_ref[b] = (mixed * scale_of(mixed) * gain).astype(BF16)


def partial_kernel(kinds, where_ref, grad_ref, got_ref, *refs):
    core, side = where_ref[0], where_ref[1]
    refs = list(refs)
    inputs = [[refs.pop(0) for _ in range(2 if kind == "halves" else 1)] for kind in kinds]
    *products, weight_out = refs
    weights = []
    for kind, sources in zip(kinds, inputs):
        if kind == "own":
            weights.append(sources[0][rows_of(core, HD), :])
        elif kind == "halves":
            mine, theirs = sources[0][...], sources[1][...]
            weights += [jnp.where(side == 0, mine, theirs), jnp.where(side == 0, theirs, mine)]
        else:
            weights.append(sources[0][...])
    weight = jnp.concatenate(weights, axis=0)
    weight_out[...] = weight[2 * HD - weight_out.shape[0] :]
    for block, ref in ((core, grad_ref), (1 - core, got_ref)):
        product = dot(ref[...], weight, NT)
        for number, out in enumerate(products):
            out[block] = product[:, number * HD : (number + 1) * HD].astype(out.dtype)


def grad_mixed_kernel(where_ref, q_ref, col_ref, gain_ref, mixed_ref, own_ref, *refs):
    part_refs, (grad_ref, second_ref, message_ref) = refs[:-3], refs[-3:]
    columns = col_ref[...]
    gain = gain_ref[:, lanes_of(where_ref[0])]
    ups = []
    for b in range(2):
        normed = own_ref[b]
        for ref in part_refs:
            normed = normed + ref[b].astype(F32)
        lifted = normed * gain
        mixed = mixed_ref[b]
        scale = scale_of(mixed)
        unit = mixed * scale
        grad = scale * (lifted - unit * jnp.mean(unit * lifted, axis=-1, keepdims=True))
        grad_ref[b] = grad
        ups.append(dot_bf(q_ref[b], jnp.exp(columns[:, b : b + 1]) * grad, TN))
    second_ref[...] = ups[1]
    totals = [total_of(columns, b) for b in range(2)]
    put_message(message_ref, ups[0] + jnp.exp(totals[0]) * ups[1], totals[0] + totals[1])


def inner_grad_kernel(
    where_ref, q_ref, k_ref, v_ref, col_ref, row_ref, grad_ref, state_ref, second_ref, keep_ref, send_ref
):
    core = where_ref[0]
    columns, across = col_ref[...], row_ref[...]
    length = columns.shape[0]
    lower = triangle(length)
    parts = []
    ends = [columns[length - 1 : length, b : b + 1] for b in range(2)]
    for b in range(2):
        q, k, v, grad = q_ref[b], k_ref[b], v_ref[b], grad_ref[b]
        weight = weights(columns, across, lower, b)
        scores = dot(q, k, NT) * weight
        grad_scores = dot_fb(grad, v, NT) * weight
        carried = jnp.exp(columns[:, b : b + 1]) * dot_ff(grad, state_ref[b], NT)
        dq = dot_fb(grad_scores, k, NN) + carried
        dk = dot_fb(grad_scores, q, TN)
        dv = dot_ff(scores, grad, TN)
        fade = jnp.exp(ends[b] - columns[:, b : b + 1])
        if b == 0:
            dk = dk + fade * dot_bf(v, second_ref[...], NT)
            dv = dv + fade * dot_bf(k, second_ref[...], NN)
            fade = fade * jnp.exp(ends[1])
        parts.append((dq, dk, dv, jnp.broadcast_to(fade, (length, HD))))
    for number, (early, late) in enumerate(zip(*parts)):
        part = slice(number * HD, (number + 1) * HD)
        keep_ref[:, part] = jnp.where(core == 0, early, late)
        send_ref[:, part] = jnp.where(core == 0, late, early)


def outer_grad_kernel(count, where_ref, k_ref, v_ref, inner_ref, inner_got_ref, *refs):
    core = where_ref[0]
    outs = refs[2 * count :]
    for head, inner, chip_refs in (
        (core, inner_ref, refs[:count][::-1]),
        (1 - core, inner_got_ref, refs[count : 2 * count][::-1]),
    ):
        high, low = split(chip_sum(chip_refs))
        fade = inner[:, 3 * HD : 4 * HD]
        k, v = k_ref[:, lanes_of(head)], v_ref[:, lanes_of(head)]
        outs[0][:, lanes_of(head)] = inner[:, 0:HD].astype(BF16)
        key = inner[:, HD : 2 * HD] + fade * (dot(v, high, NT) + dot(v, low, NT))
        outs[1][:, lanes_of(head)] = key.astype(BF16)
        value = inner[:, 2 * HD : 3 * HD] + fade * (dot(k, high, NN) + dot(k, low, NN))
        outs[2][:, lanes_of(head)] = value.astype(BF16)


def layer_kernel(pairs, where_ref, own_ref, *refs):
    mine_refs, theirs_refs = refs[:pairs], refs[pairs : 2 * pairs]
    *normed_refs, got_ref, out_ref = refs[2 * pairs :]
    core = where_ref[0]
    mine = [ref[core] for ref in normed_refs]
    theirs = [got_ref[number] for number in range(got_ref.shape[0])]
    normed = [mine[0], theirs[0], mine[1], theirs[1]]
    for begin in range(2, len(mine), 2):
        normed += mine[begin : begin + 2] + theirs[begin : begin + 2]
    normed = jnp.concatenate(normed, axis=1)
    width = own_ref.shape[1]
    step = 512 if width % 512 == 0 else 128
    for begin in range(0, width, step):
        lanes = slice(begin, begin + step)
        weight = [own_ref[rows_of(core, HD), lanes], own_ref[rows_of(1 - core, HD), lanes]]
        for mine_ref, theirs_ref in zip(mine_refs, theirs_refs):
            weight += [mine_ref[:, lanes], theirs_ref[:, lanes]]
        out_ref[:, lanes] = dot(normed, jnp.concatenate(weight, axis=0), NN).astype(BF16)


SMEM = pl.BlockSpec(memory_space=pltpu.SMEM)
VMEM = pl.BlockSpec(memory_space=pltpu.VMEM)


def call(kernel, name, outs, args, grant=16):
    return pl.pallas_call(
        kernel,
        name=name,
        out_shape=outs,
        in_specs=[SMEM] + [VMEM] * (len(args) - 1),
        out_specs=[VMEM] * len(outs),
        compiler_params=pltpu.CompilerParams(vmem_limit_bytes=grant * 2**20),
        cost_estimate=pl.CostEstimate(flops=1, bytes_accessed=1, transcendentals=0),
    )(*args)


def without_where(kernel):
    return lambda where_ref, *refs: kernel(*refs)


def after(values, *earlier):
    tied = lax.optimization_barrier((earlier, tuple(values)))
    return list(tied[1])


def on_device(queries, keys, values, log_decay, norm_gain, out_weight, out_grad):
    length, columns = queries.shape
    seq = lax.axis_size("seq")
    tensor = lax.axis_size("tensor")
    chips = seq // 2
    model = out_weight.shape[1]
    width = model // tensor
    place = lax.axis_index("tensor")
    core = lax.rem(lax.axis_index("seq"), 2)
    side = lax.rem(lax.axis_index("seq") // 2, 2)
    where = jnp.stack([core, side]).astype(jnp.int32)
    gain = norm_gain.reshape(1, columns)

    def swap_tensor(value, k):
        return lax.ppermute(value, "tensor", [(i, i ^ k) for i in range(tensor)])

    def swap_core(value):
        return lax.ppermute(value, "seq", [(i, i ^ 1) for i in range(seq)])

    def swap_side(value):
        return lax.ppermute(value, "seq", [(i, i ^ 2) for i in range(seq)])

    def to_chip(value, step):
        return lax.ppermute(
            value, "seq", [(i, i + 2 * step) for i in range(seq) if 0 <= i + 2 * step < seq]
        )

    def shape(dtype, *dims):
        return jax.ShapeDtypeStruct(dims, dtype)

    others = range(1, tensor)
    message = shape(BF16, HD + TAIL, HD)
    pair16 = shape(BF16, 2, length, HD)
    pair32 = shape(F32, 2, length, HD)
    one16 = shape(BF16, length, HD)
    both16 = shape(BF16, length, columns)

    far = [step for step in others if step & (step - 1)]
    near = [step for step in others if not step & (step - 1)]
    order = far + near
    plan = [(step, step in far) for step in order]

    def slice_for(step, halves):
        rows = HD // 2 if halves else HD
        begin = core * HD + side * rows if halves else core * HD
        return lax.dynamic_slice(out_weight, (begin, (place ^ step) * width), (rows, width))

    slices = [slice_for(step, halves) for step, halves in plan]
    arriving = [swap_tensor(piece, step) for piece, step in zip(slices, order)]
    got = [swap_core(rows) for rows in (queries, keys, values)]
    got.append(swap_core(log_decay))
    (weight,) = after([out_weight], *slices)
    weight_own = lax.dynamic_slice(weight, (0, place * width), (columns, width))
    got = after(got, weight_own)
    (grad,) = after([out_grad], *got)
    grad_got = swap_core(grad)
    q, k, v, col, row, first, fresh = call(
        fresh_kernel,
        "fresh",
        [pair16, pair16, pair16, shape(F32, length, 2), shape(F32, 2, length), shape(F32, HD, HD), message],
        [where, queries, keys, values, *got[:3], log_decay, got[3]],
    )
    (fresh,) = after([fresh], grad_got)
    arrived, window, step = [], fresh, 1
    while step < chips:
        if arrived:
            (window,) = call(without_where(join_kernel), "join", [message], [where, window, arrived[-1]])
        arrived.append(to_chip(window, step))
        step *= 2
    pieces = [("own", [weight_own])]
    for (step, halves), piece in zip(plan, arriving):
        if halves:
            (piece,) = after([piece], window)
        pieces.append(("halves", [piece, swap_side(piece)]) if halves else ("whole", [piece]))
    partials, mine, theirs = [], [], []
    for number in range(0, tensor, 2):
        kinds, sources = zip(*pieces[number : number + 2])
        sources = after(sum(sources, []), *arrived, *partials)
        *outs, weight = call(
            functools.partial(partial_kernel, kinds),
            "partial",
            [pair16 if number else pair32, pair16, shape(BF16, 2 * HD if number else HD, width)],
            [where, out_grad, grad_got, *sources],
        )
        partials += outs
        mine.append(weight)
        if number == 0:
            theirs.append(swap_core(weight))
    own_partial, *partials = partials
    sent = [swap_tensor(partial, step) for partial, step in zip(partials, order)]
    (inner,) = call(without_where(inner_kernel), "inner", [pair32], [where, q, k, v, col, row, *after([first], *partials)])
    mixed, normed, states = call(
        mixed_kernel,
        "mixed",
        [pair32, pair16, shape(F32, 2, HD, HD)],
        [where, q, col, inner, gain, first, *after(arrived, *partials)],
    )
    normed_all = [normed] + [swap_tensor(normed, step) for step in order]
    grad_mixed, second, upward = call(
        grad_mixed_kernel,
        "grad_mixed",
        [pair32, shape(F32, HD, HD), message],
        [where, q, col, gain, mixed, own_partial, *sent],
    )
    (upward,) = after([upward], *normed_all)
    (cross,) = call(cross_kernel, "cross", [shape(BF16, tensor, length, HD)], [where, *normed_all])
    cross_got = swap_core(cross)
    returned = [to_chip(upward, -step) for step in reversed(range(1, chips))]
    theirs += [swap_core(weight) for weight in after(mine[1:], upward)]
    inner_keep, inner_send = call(
        inner_grad_kernel,
        "inner_grad",
        [shape(F32, length, 4 * HD)] * 2,
        [where, q, k, v, col, row, grad_mixed, states, second],
    )
    (layer_out,) = call(
        functools.partial(layer_kernel, tensor // 2),
        "layer",
        [shape(BF16, length, width)],
        [where, weight_own, *mine, *theirs, *normed_all, cross_got],
    )
    returned = after(returned, layer_out)
    inner_got = swap_core(*after([inner_send], *returned))
    returned_got = [swap_core(rows) for rows in returned]
    query_grad, key_grad, value_grad = call(
        functools.partial(outer_grad_kernel, chips - 1),
        "outer_grad",
        [both16] * 3,
        [where, keys, values, inner_keep, inner_got, *returned, *returned_got],
    )
    return layer_out, query_grad, key_grad, value_grad


def solution(mesh):
    in_specs = (
        P("seq", "tensor"),
        P("seq", "tensor"),
        P("seq", "tensor"),
        P("tensor", "seq"),
        P("tensor"),
        P("tensor", None),
        P("seq", "tensor"),
    )
    out_specs = (P("seq", "tensor"), P("seq", "tensor"), P("seq", "tensor"), P("seq", "tensor"))
    return jax.shard_map(
        on_device, mesh=mesh, in_specs=in_specs, out_specs=out_specs, check_vma=False
    )
```

```python
import functools

import jax
import jax.numpy as jnp
from jax import lax
from jax.experimental import pallas as pl
from jax.experimental.pallas import tpu as pltpu
from jax.sharding import PartitionSpec as P

EXACT = lax.Precision.HIGHEST
EPSILON = 1e-05
F32 = jnp.float32
BF16 = jnp.bfloat16
TAIL = 16
HD = 128

NN = (((1,), (0,)), ((), ()))
NT = (((1,), (1,)), ((), ()))
TN = (((0,), (0,)), ((), ()))


def dot(a, b, dims):
    return lax.dot_general(a, b, dims, preferred_element_type=F32)


def split(x):
    high = x.astype(BF16)
    return high, (x - high.astype(F32)).astype(BF16)


def dot_fb(a, b, dims):
    high, low = split(a)
    return dot(high, b, dims) + dot(low, b, dims)


def dot_bf(a, b, dims):
    high, low = split(b)
    return dot(a, high, dims) + dot(a, low, dims)


def triangle(length):
    rows = lax.broadcasted_iota(jnp.int32, (length, length), 0)
    cols = lax.broadcasted_iota(jnp.int32, (length, length), 1)
    return rows >= cols


def running_columns(decay, lower):
    return lax.dot_general(lower.astype(F32), decay, NT, precision=EXACT, preferred_element_type=F32)


def running_rows(decay, lower):
    return lax.dot_general(decay, lower.astype(F32), NT, precision=EXACT, preferred_element_type=F32)


def put_total(ref, base, total):
    first = total.astype(BF16).astype(F32)
    second = (total - first).astype(BF16).astype(F32)
    third = total - first - second
    at = lax.broadcasted_iota(jnp.int32, (TAIL, 128), 0)
    tail = jnp.where(at == 0, first, jnp.where(at == 1, second, jnp.where(at == 2, third, 0.0)))
    ref[base : base + TAIL, :] = tail.astype(BF16)


def get_total(ref, base):
    tail = ref[base : base + TAIL, :].astype(F32)
    return tail[0:1] + tail[1:2] + tail[2:3]


def total_of(columns, block):
    length = columns.shape[0]
    return jnp.broadcast_to(columns[length - 1 : length, block : block + 1], (1, HD))


def chip_sum(refs):
    summed = jnp.zeros((HD, HD), F32)
    passed = jnp.zeros((1, HD), F32)
    for ref in refs:
        summed = summed + jnp.exp(passed) * ref[0:HD, :].astype(F32)
        passed = passed + get_total(ref, HD)
    return summed


def put_message(ref, state, total):
    ref[0:HD, :] = state.astype(BF16)
    put_total(ref, HD, total)


def join_kernel(own_ref, got_ref, out_ref):
    total = get_total(own_ref, HD)
    state = own_ref[0:HD, :].astype(F32) + jnp.exp(total) * got_ref[0:HD, :].astype(F32)
    put_message(out_ref, state, total + get_total(got_ref, HD))


def cross_kernel(where_ref, *refs):
    *normed_refs, cross_ref = refs
    for number, ref in enumerate(normed_refs):
        cross_ref[number] = ref[1 - where_ref[0]]


def lanes_of(number):
    return pl.ds(pl.multiple_of(number * HD, HD), HD)


def rows_of(number, count):
    return pl.ds(pl.multiple_of(number * count, count), count)


def fresh_kernel(
    where_ref, q_ref, k_ref, v_ref, q_got, k_got, v_got, decay_ref, decay_got, q_out, k_out, v_out, col_ref, row_ref, first_ref, message_ref
):
    core = where_ref[0]
    length = q_ref.shape[0]
    for out, ref, got in ((q_out, q_ref, q_got), (k_out, k_ref, k_got), (v_out, v_ref, v_got)):
        out[core] = ref[:, lanes_of(core)]
        out[1 - core] = got[:, lanes_of(core)]
    mine = jnp.where(core == 0, decay_ref[0:1, :], decay_ref[1:2, :])
    theirs = jnp.where(core == 0, decay_got[0:1, :], decay_got[1:2, :])
    block = lax.broadcasted_iota(jnp.int32, (2, length), 0)
    decay = jnp.where(block == core, mine, theirs)
    lower = triangle(length)
    columns = running_columns(decay, lower)
    col_ref[...] = columns
    row_ref[...] = running_rows(decay, lower)
    states = []
    for b in range(2):
        fade = jnp.exp(columns[length - 1 : length, b : b + 1] - columns[:, b : b + 1])
        states.append(dot(k_out[b], (fade * v_out[b].astype(F32)).astype(BF16), TN))
    totals = [total_of(columns, b) for b in range(2)]
    first_ref[...] = states[0]
    put_message(message_ref, jnp.exp(totals[1]) * states[0] + states[1], totals[0] + totals[1])


def weights(columns, across, lower, b):
    return jnp.exp(jnp.where(lower, columns[:, b : b + 1] - across[b : b + 1, :], -1e30))


def inner_kernel(q_ref, k_ref, v_ref, col_ref, row_ref, first_ref, inner_ref):
    columns, across = col_ref[...], row_ref[...]
    lower = triangle(columns.shape[0])
    for b in range(2):
        scores = dot(q_ref[b], k_ref[b], NT) * weights(columns, across, lower, b)
        inner = dot_fb(scores, v_ref[b], NN)
        if b == 1:
            inner = inner + jnp.exp(columns[:, 1:2]) * dot_bf(q_ref[b], first_ref[...], NN)
        inner_ref[b] = inner


def scale_of(mixed):
    return lax.rsqrt(jnp.mean(mixed * mixed, axis=-1, keepdims=True) + EPSILON)


def mixed_kernel(where_ref, q_ref, col_ref, inner_ref, gain_ref, first_ref, *refs):
    chip_refs, (mixed_ref, normed_ref, state_ref) = refs[:-3], refs[-3:]
    core = where_ref[0]
    columns = col_ref[...]
    gain = gain_ref[:, lanes_of(core)]
    state = chip_sum(chip_refs)
    high, low = split(state)
    shrink = jnp.exp(total_of(columns, 0))
    state_ref[0] = state
    state_ref[1] = shrink * state + first_ref[...]
    for b in range(2):
        grow = jnp.exp(columns[:, b : b + 1])
        if b == 1:
            grow = grow * shrink
        mixed = inner_ref[b] + grow * (dot(q_ref[b], high, NN) + dot(q_ref[b], low, NN))
        mixed_ref[b] = mixed
        normed_ref[b] = (mixed * scale_of(mixed) * gain).astype(BF16)


def partial_kernel(kinds, where_ref, grad_ref, got_ref, *refs):
    core, side = where_ref[0], where_ref[1]
    refs = list(refs)
    inputs = [[refs.pop(0) for _ in range(2 if kind == "halves" else 1)] for kind in kinds]
    *products, weight_out = refs
    weights = []
    for kind, sources in zip(kinds, inputs):
        if kind == "own":
            weights.append(sources[0][rows_of(core, HD), :])
        elif kind == "halves":
            mine, theirs = sources[0][...], sources[1][...]
            weights += [jnp.where(side == 0, mine, theirs), jnp.where(side == 0, theirs, mine)]
        else:
            weights.append(sources[0][...])
    weight = jnp.concatenate(weights, axis=0)
    weight_out[...] = weight[2 * HD - weight_out.shape[0] :]
    length = grad_ref.shape[0]
    product = dot(jnp.concatenate([grad_ref[...], got_ref[...]], axis=0), weight, NT)
    for begin, block in ((0, core), (length, 1 - core)):
        for number, out in enumerate(products):
            part = product[begin : begin + length, number * HD : (number + 1) * HD]
            out[block] = part.astype(out.dtype)


def grad_mixed_kernel(where_ref, q_ref, col_ref, gain_ref, mixed_ref, own_ref, *refs):
    part_refs, (grad_ref, second_ref, message_ref) = refs[:-3], refs[-3:]
    columns = col_ref[...]
    gain = gain_ref[:, lanes_of(where_ref[0])]
    ups = []
    for b in range(2):
        normed = own_ref[b]
        for ref in part_refs:
            normed = normed + ref[b].astype(F32)
        lifted = normed * gain
        mixed = mixed_ref[b]
        scale = scale_of(mixed)
        unit = mixed * scale
        grad = scale * (lifted - unit * jnp.mean(unit * lifted, axis=-1, keepdims=True))
        grad_ref[b] = grad
        ups.append(dot(q_ref[b], (jnp.exp(columns[:, b : b + 1]) * grad).astype(BF16), TN))
    second_ref[...] = ups[1]
    totals = [total_of(columns, b) for b in range(2)]
    put_message(message_ref, ups[0] + jnp.exp(totals[0]) * ups[1], totals[0] + totals[1])


def inner_grad_kernel(
    where_ref, q_ref, k_ref, v_ref, col_ref, row_ref, grad_ref, state_ref, second_ref, keep_ref, send_ref
):
    core = where_ref[0]
    columns, across = col_ref[...], row_ref[...]
    length = columns.shape[0]
    lower = triangle(length)
    parts = []
    ends = [columns[length - 1 : length, b : b + 1] for b in range(2)]
    for b in range(2):
        q, k, v, grad = q_ref[b], k_ref[b], v_ref[b], grad_ref[b]
        weight = weights(columns, across, lower, b)
        narrow = grad.astype(BF16)
        scores = (dot(q, k, NT) * weight).astype(BF16)
        grad_scores = (dot(narrow, v, NT) * weight).astype(BF16)
        carried = jnp.exp(columns[:, b : b + 1]) * dot(narrow, state_ref[b].astype(BF16), NT)
        dq = dot(grad_scores, k, NN) + carried
        dk = dot(grad_scores, q, TN)
        dv = dot(scores, narrow, TN)
        fade = jnp.exp(ends[b] - columns[:, b : b + 1])
        if b == 0:
            second = second_ref[...].astype(BF16)
            dk = dk + fade * dot(v, second, NT)
            dv = dv + fade * dot(k, second, NN)
            fade = fade * jnp.exp(ends[1])
        parts.append((dq, dk, dv, jnp.broadcast_to(fade, (length, HD))))
    for number, (early, late) in enumerate(zip(*parts)):
        part = slice(number * HD, (number + 1) * HD)
        keep_ref[:, part] = jnp.where(core == 0, early, late)
        send_ref[:, part] = jnp.where(core == 0, late, early)


def outer_grad_kernel(count, where_ref, k_ref, v_ref, inner_ref, inner_got_ref, *refs):
    core = where_ref[0]
    outs = refs[2 * count :]
    for head, inner, chip_refs in (
        (core, inner_ref, refs[:count][::-1]),
        (1 - core, inner_got_ref, refs[count : 2 * count][::-1]),
    ):
        state = chip_sum(chip_refs).astype(BF16)
        fade = inner[:, 3 * HD : 4 * HD]
        k, v = k_ref[:, lanes_of(head)], v_ref[:, lanes_of(head)]
        outs[0][:, lanes_of(head)] = inner[:, 0:HD].astype(BF16)
        key = inner[:, HD : 2 * HD] + fade * dot(v, state, NT)
        outs[1][:, lanes_of(head)] = key.astype(BF16)
        value = inner[:, 2 * HD : 3 * HD] + fade * dot(k, state, NN)
        outs[2][:, lanes_of(head)] = value.astype(BF16)


def layer_kernel(pairs, where_ref, own_ref, *refs):
    mine_refs, theirs_refs = refs[:pairs], refs[pairs : 2 * pairs]
    *normed_refs, got_ref, out_ref = refs[2 * pairs :]
    core = where_ref[0]
    mine = [ref[core] for ref in normed_refs]
    theirs = [got_ref[number] for number in range(got_ref.shape[0])]
    normed = [mine[0], theirs[0], mine[1], theirs[1]]
    for begin in range(2, len(mine), 2):
        normed += mine[begin : begin + 2] + theirs[begin : begin + 2]
    normed = jnp.concatenate(normed, axis=1)
    width = own_ref.shape[1]
    step = 512 if width % 512 == 0 else 128
    for begin in range(0, width, step):
        lanes = slice(begin, begin + step)
        weight = [own_ref[rows_of(core, HD), lanes], own_ref[rows_of(1 - core, HD), lanes]]
        for mine_ref, theirs_ref in zip(mine_refs, theirs_refs):
            weight += [mine_ref[:, lanes], theirs_ref[:, lanes]]
        out_ref[:, lanes] = dot(normed, jnp.concatenate(weight, axis=0), NN).astype(BF16)


SMEM = pl.BlockSpec(memory_space=pltpu.SMEM)
VMEM = pl.BlockSpec(memory_space=pltpu.VMEM)


def call(kernel, name, outs, args, grant=16):
    return pl.pallas_call(
        kernel,
        name=name,
        out_shape=outs,
        in_specs=[SMEM] + [VMEM] * (len(args) - 1),
        out_specs=[VMEM] * len(outs),
        compiler_params=pltpu.CompilerParams(vmem_limit_bytes=grant * 2**20),
        cost_estimate=pl.CostEstimate(flops=1, bytes_accessed=1, transcendentals=0),
    )(*args)


def without_where(kernel):
    return lambda where_ref, *refs: kernel(*refs)


def after(values, *earlier):
    tied = lax.optimization_barrier((tuple(values), earlier))
    return list(tied[0])


def on_device(queries, keys, values, log_decay, norm_gain, out_weight, out_grad):
    length, columns = queries.shape
    seq = lax.axis_size("seq")
    tensor = lax.axis_size("tensor")
    chips = seq // 2
    model = out_weight.shape[1]
    width = model // tensor
    place = lax.axis_index("tensor")
    core = lax.rem(lax.axis_index("seq"), 2)
    side = lax.rem(lax.axis_index("seq") // 2, 2)
    where = jnp.stack([core, side]).astype(jnp.int32)
    gain = norm_gain.reshape(1, columns)

    def swap_tensor(value, k):
        return lax.ppermute(value, "tensor", [(i, i ^ k) for i in range(tensor)])

    def swap_core(value):
        return lax.ppermute(value, "seq", [(i, i ^ 1) for i in range(seq)])

    def swap_side(value):
        return lax.ppermute(value, "seq", [(i, i ^ 2) for i in range(seq)])

    def to_chip(value, step):
        return lax.ppermute(
            value, "seq", [(i, i + 2 * step) for i in range(seq) if 0 <= i + 2 * step < seq]
        )

    def shape(dtype, *dims):
        return jax.ShapeDtypeStruct(dims, dtype)

    others = range(1, tensor)
    message = shape(BF16, HD + TAIL, HD)
    pair16 = shape(BF16, 2, length, HD)
    pair32 = shape(F32, 2, length, HD)
    one16 = shape(BF16, length, HD)
    both16 = shape(BF16, length, columns)

    far = [step for step in others if step & (step - 1)]
    near = [step for step in others if not step & (step - 1)]
    order = far + near
    plan = [(step, step in far) for step in order]

    def slice_for(step, halves):
        rows = HD // 2 if halves else HD
        begin = core * HD + side * rows if halves else core * HD
        return lax.dynamic_slice(out_weight, (begin, (place ^ step) * width), (rows, width))

    slices = [slice_for(step, halves) for step, halves in plan]
    arriving = [swap_tensor(piece, step) for piece, step in zip(slices, order)]
    got = [swap_core(rows) for rows in (queries, keys, values)]
    got.append(swap_core(log_decay))
    (weight,) = after([out_weight], *slices)
    weight_own = lax.dynamic_slice(weight, (0, place * width), (columns, width))
    got = after(got, weight_own)
    (grad,) = after([out_grad], *got)
    grad_got = swap_core(grad)
    q, k, v, col, row, first, fresh = call(
        fresh_kernel,
        "fresh",
        [pair16, pair16, pair16, shape(F32, length, 2), shape(F32, 2, length), shape(F32, HD, HD), message],
        [where, queries, keys, values, *got[:3], log_decay, got[3]],
    )
    (fresh,) = after([fresh], grad_got)
    arrived, window, step = [], fresh, 1
    while step < chips:
        if arrived:
            (window,) = call(without_where(join_kernel), "join", [message], [where, window, arrived[-1]])
        arrived.append(to_chip(window, step))
        step *= 2
    (inner,) = call(without_where(inner_kernel), "inner", [pair32], [where, q, k, v, col, row, first])
    pieces = [("own", [weight_own])]
    for (step, halves), piece in zip(plan, arriving):
        if halves:
            (piece,) = after([piece], arrived[0])
        pieces.append(("halves", [piece, swap_side(piece)]) if halves else ("whole", [piece]))
    partials, mine, theirs = [], [], []
    for number in range(0, tensor, 2):
        kinds, sources = zip(*pieces[number : number + 2])
        sources = after(sum(sources, []), *arrived, inner, *partials)
        *outs, weight = call(
            functools.partial(partial_kernel, kinds),
            "partial",
            [pair16 if number else pair32, pair16, shape(BF16, 2 * HD if number else HD, width)],
            [where, out_grad, grad_got, *sources],
        )
        partials += outs
        mine.append(weight)
        if number == 0:
            theirs.append(swap_core(weight))
    own_partial, *partials = partials
    sent = [swap_tensor(partial, step) for partial, step in zip(partials, order)]
    mixed, normed, states = call(
        mixed_kernel,
        "mixed",
        [pair32, pair16, shape(F32, 2, HD, HD)],
        [where, q, col, inner, gain, first, *after(arrived, *partials)],
    )
    normed_all = [normed] + [swap_tensor(normed, step) for step in order]
    grad_mixed, second, upward = call(
        grad_mixed_kernel,
        "grad_mixed",
        [pair32, shape(F32, HD, HD), message],
        [where, q, col, gain, mixed, own_partial, *sent],
    )
    (upward,) = after([upward], *normed_all)
    (cross,) = call(cross_kernel, "cross", [shape(BF16, tensor, length, HD)], [where, *normed_all])
    cross_got = swap_core(cross)
    returned = [to_chip(upward, -step) for step in reversed(range(1, chips))]
    theirs += [swap_core(weight) for weight in after(mine[1:], upward)]
    inner_keep, inner_send = call(
        inner_grad_kernel,
        "inner_grad",
        [shape(F32, length, 4 * HD)] * 2,
        [where, q, k, v, col, row, grad_mixed, states, second],
    )
    (layer_out,) = call(
        functools.partial(layer_kernel, tensor // 2),
        "layer",
        [shape(BF16, length, width)],
        [where, weight_own, *mine, *theirs, *normed_all, cross_got],
    )
    returned = after(returned, layer_out)
    inner_got = swap_core(*after([inner_send], *returned))
    returned_got = [swap_core(rows) for rows in returned]
    query_grad, key_grad, value_grad = call(
        functools.partial(outer_grad_kernel, chips - 1),
        "outer_grad",
        [both16] * 3,
        [where, keys, values, inner_keep, inner_got, *returned, *returned_got],
    )
    return layer_out, query_grad, key_grad, value_grad


def solution(mesh):
    in_specs = (
        P("seq", "tensor"),
        P("seq", "tensor"),
        P("seq", "tensor"),
        P("tensor", "seq"),
        P("tensor"),
        P("tensor", None),
        P("seq", "tensor"),
    )
    out_specs = (P("seq", "tensor"), P("seq", "tensor"), P("seq", "tensor"), P("seq", "tensor"))
    return jax.shard_map(
        on_device, mesh=mesh, in_specs=in_specs, out_specs=out_specs, check_vma=False
    )
```

```python
import functools

import jax
import jax.numpy as jnp
from jax import lax
from jax.experimental import pallas as pl
from jax.experimental.pallas import tpu as pltpu
from jax.sharding import PartitionSpec as P

EPSILON = 1e-05
F32 = jnp.float32
BF16 = jnp.bfloat16
TAIL = 16
HD = 128

NN = (((1,), (0,)), ((), ()))
NT = (((1,), (1,)), ((), ()))
TN = (((0,), (0,)), ((), ()))


def dot(a, b, dims):
    return lax.dot_general(a, b, dims, preferred_element_type=F32)


def split(x):
    high = x.astype(BF16)
    return high, (x - high.astype(F32)).astype(BF16)


def dot_fb(a, b, dims):
    high, low = split(a)
    return dot(high, b, dims) + dot(low, b, dims)


def dot_bf(a, b, dims):
    high, low = split(b)
    return dot(a, high, dims) + dot(a, low, dims)


def triangle(length):
    rows = lax.broadcasted_iota(jnp.int32, (length, length), 0)
    cols = lax.broadcasted_iota(jnp.int32, (length, length), 1)
    return rows >= cols


def running_sums(decay, lower):
    ones = lower.astype(BF16)
    columns = rows = 0.0
    for _ in range(3):
        part = decay.astype(BF16)
        decay = decay - part.astype(F32)
        columns = columns + dot(ones, part, NT)
        rows = rows + dot(part, ones, NT)
    return columns, rows


def put_total(ref, base, total):
    first = total.astype(BF16).astype(F32)
    second = (total - first).astype(BF16).astype(F32)
    third = total - first - second
    at = lax.broadcasted_iota(jnp.int32, (TAIL, 128), 0)
    tail = jnp.where(at == 0, first, jnp.where(at == 1, second, jnp.where(at == 2, third, 0.0)))
    ref[base : base + TAIL, :] = tail.astype(BF16)


def get_total(ref, base):
    tail = ref[base : base + TAIL, :].astype(F32)
    return tail[0:1] + tail[1:2] + tail[2:3]


def total_of(columns, block):
    length = columns.shape[0]
    return jnp.broadcast_to(columns[length - 1 : length, block : block + 1], (1, HD))


def chip_sum(refs):
    summed = jnp.zeros((HD, HD), F32)
    passed = jnp.zeros((1, HD), F32)
    for ref in refs:
        summed = summed + jnp.exp(passed) * ref[0:HD, :].astype(F32)
        passed = passed + get_total(ref, HD)
    return summed


def put_message(ref, state, total):
    ref[0:HD, :] = state.astype(BF16)
    put_total(ref, HD, total)


def join_kernel(own_ref, got_ref, out_ref):
    total = get_total(own_ref, HD)
    state = own_ref[0:HD, :].astype(F32) + jnp.exp(total) * got_ref[0:HD, :].astype(F32)
    put_message(out_ref, state, total + get_total(got_ref, HD))


def cross_kernel(where_ref, *refs):
    *normed_refs, cross_ref = refs
    for number, ref in enumerate(normed_refs):
        cross_ref[number] = ref[1 - where_ref[0]]


def lanes_of(number):
    return pl.ds(pl.multiple_of(number * HD, HD), HD)


def rows_of(number, count):
    return pl.ds(pl.multiple_of(number * count, count), count)


def fresh_kernel(
    where_ref, q_ref, k_ref, v_ref, q_got, k_got, v_got, decay_ref, decay_got, q_out, k_out, v_out, col_ref, row_ref, first_ref, message_ref
):
    core = where_ref[0]
    length = q_ref.shape[0]
    for out, ref, got in ((q_out, q_ref, q_got), (k_out, k_ref, k_got), (v_out, v_ref, v_got)):
        out[core] = ref[:, lanes_of(core)]
        out[1 - core] = got[:, lanes_of(core)]
    mine = jnp.where(core == 0, decay_ref[0:1, :], decay_ref[1:2, :])
    theirs = jnp.where(core == 0, decay_got[0:1, :], decay_got[1:2, :])
    block = lax.broadcasted_iota(jnp.int32, (2, length), 0)
    decay = jnp.where(block == core, mine, theirs)
    lower = triangle(length)
    columns, rows = running_sums(decay, lower)
    col_ref[...] = columns
    row_ref[...] = rows
    states = []
    for b in range(2):
        fade = jnp.exp(columns[length - 1 : length, b : b + 1] - columns[:, b : b + 1])
        states.append(dot(k_out[b], (fade * v_out[b].astype(F32)).astype(BF16), TN))
    totals = [total_of(columns, b) for b in range(2)]
    first_ref[...] = states[0]
    put_message(message_ref, jnp.exp(totals[1]) * states[0] + states[1], totals[0] + totals[1])


def weights(columns, across, lower, b):
    return jnp.exp(jnp.where(lower, columns[:, b : b + 1] - across[b : b + 1, :], -1e30))


def inner_kernel(q_ref, k_ref, v_ref, col_ref, row_ref, first_ref, inner_ref):
    columns, across = col_ref[...], row_ref[...]
    lower = triangle(columns.shape[0])
    for b in range(2):
        scores = dot(q_ref[b], k_ref[b], NT) * weights(columns, across, lower, b)
        inner = dot_fb(scores, v_ref[b], NN)
        if b == 1:
            inner = inner + jnp.exp(columns[:, 1:2]) * dot_bf(q_ref[b], first_ref[...], NN)
        inner_ref[b] = inner


def scale_of(mixed):
    return lax.rsqrt(jnp.mean(mixed * mixed, axis=-1, keepdims=True) + EPSILON)


def mixed_kernel(where_ref, q_ref, col_ref, inner_ref, gain_ref, first_ref, *refs):
    chip_refs, (mixed_ref, normed_ref, state_ref) = refs[:-3], refs[-3:]
    core = where_ref[0]
    columns = col_ref[...]
    gain = gain_ref[:, lanes_of(core)]
    state = chip_sum(chip_refs)
    high, low = split(state)
    shrink = jnp.exp(total_of(columns, 0))
    state_ref[0] = state
    state_ref[1] = shrink * state + first_ref[...]
    for b in range(2):
        grow = jnp.exp(columns[:, b : b + 1])
        if b == 1:
            grow = grow * shrink
        mixed = inner_ref[b] + grow * (dot(q_ref[b], high, NN) + dot(q_ref[b], low, NN))
        mixed_ref[b] = mixed
        normed_ref[b] = (mixed * scale_of(mixed) * gain).astype(BF16)


def partial_kernel(kinds, where_ref, grad_ref, got_ref, *refs):
    core, side = where_ref[0], where_ref[1]
    refs = list(refs)
    inputs = [[refs.pop(0) for _ in range(2 if kind == "halves" else 1)] for kind in kinds]
    *products, weight_out = refs
    weights = []
    for kind, sources in zip(kinds, inputs):
        if kind == "own":
            weights.append(sources[0][rows_of(core, HD), :])
        elif kind == "halves":
            mine, theirs = sources[0][...], sources[1][...]
            weights += [jnp.where(side == 0, mine, theirs), jnp.where(side == 0, theirs, mine)]
        else:
            weights.append(sources[0][...])
    weight = jnp.concatenate(weights, axis=0)
    weight_out[...] = weight[2 * HD - weight_out.shape[0] :]
    length = grad_ref.shape[0]
    product = dot(jnp.concatenate([grad_ref[...], got_ref[...]], axis=0), weight, NT)
    for begin, block in ((0, core), (length, 1 - core)):
        for number, out in enumerate(products):
            part = product[begin : begin + length, number * HD : (number + 1) * HD]
            out[block] = part.astype(out.dtype)


def grad_mixed_kernel(where_ref, q_ref, col_ref, gain_ref, mixed_ref, own_ref, *refs):
    part_refs, (grad_ref, second_ref, message_ref) = refs[:-3], refs[-3:]
    columns = col_ref[...]
    gain = gain_ref[:, lanes_of(where_ref[0])]
    ups = []
    for b in range(2):
        normed = own_ref[b]
        for ref in part_refs:
            normed = normed + ref[b].astype(F32)
        lifted = normed * gain
        mixed = mixed_ref[b]
        scale = scale_of(mixed)
        unit = mixed * scale
        grad = scale * (lifted - unit * jnp.mean(unit * lifted, axis=-1, keepdims=True))
        grad_ref[b] = grad
        ups.append(dot(q_ref[b], (jnp.exp(columns[:, b : b + 1]) * grad).astype(BF16), TN))
    second_ref[...] = ups[1]
    totals = [total_of(columns, b) for b in range(2)]
    put_message(message_ref, ups[0] + jnp.exp(totals[0]) * ups[1], totals[0] + totals[1])


def inner_grad_kernel(
    where_ref, q_ref, k_ref, v_ref, col_ref, row_ref, grad_ref, state_ref, second_ref, keep_ref, send_ref
):
    core = where_ref[0]
    columns, across = col_ref[...], row_ref[...]
    length = columns.shape[0]
    lower = triangle(length)
    parts = []
    ends = [columns[length - 1 : length, b : b + 1] for b in range(2)]
    for b in range(2):
        q, k, v, grad = q_ref[b], k_ref[b], v_ref[b], grad_ref[b]
        weight = weights(columns, across, lower, b)
        narrow = grad.astype(BF16)
        scores = (dot(q, k, NT) * weight).astype(BF16)
        grad_scores = (dot(narrow, v, NT) * weight).astype(BF16)
        carried = jnp.exp(columns[:, b : b + 1]) * dot(narrow, state_ref[b].astype(BF16), NT)
        dq = dot(grad_scores, k, NN) + carried
        dk = dot(grad_scores, q, TN)
        dv = dot(scores, narrow, TN)
        fade = jnp.exp(ends[b] - columns[:, b : b + 1])
        if b == 0:
            second = second_ref[...].astype(BF16)
            dk = dk + fade * dot(v, second, NT)
            dv = dv + fade * dot(k, second, NN)
            fade = fade * jnp.exp(ends[1])
        parts.append((dq, dk, dv, jnp.broadcast_to(fade, (length, HD))))
    for number, (early, late) in enumerate(zip(*parts)):
        part = slice(number * HD, (number + 1) * HD)
        keep_ref[:, part] = jnp.where(core == 0, early, late)
        send_ref[:, part] = jnp.where(core == 0, late, early)


def outer_grad_kernel(count, where_ref, k_ref, v_ref, inner_ref, inner_got_ref, *refs):
    core = where_ref[0]
    outs = refs[2 * count :]
    for head, inner, chip_refs in (
        (core, inner_ref, refs[:count][::-1]),
        (1 - core, inner_got_ref, refs[count : 2 * count][::-1]),
    ):
        state = chip_sum(chip_refs).astype(BF16)
        fade = inner[:, 3 * HD : 4 * HD]
        k, v = k_ref[:, lanes_of(head)], v_ref[:, lanes_of(head)]
        outs[0][:, lanes_of(head)] = inner[:, 0:HD].astype(BF16)
        key = inner[:, HD : 2 * HD] + fade * dot(v, state, NT)
        outs[1][:, lanes_of(head)] = key.astype(BF16)
        value = inner[:, 2 * HD : 3 * HD] + fade * dot(k, state, NN)
        outs[2][:, lanes_of(head)] = value.astype(BF16)


def layer_kernel(pairs, where_ref, own_ref, *refs):
    mine_refs, theirs_refs = refs[:pairs], refs[pairs : 2 * pairs]
    *normed_refs, got_ref, out_ref = refs[2 * pairs :]
    core = where_ref[0]
    mine = [ref[core] for ref in normed_refs]
    theirs = [got_ref[number] for number in range(got_ref.shape[0])]
    normed = [mine[0], theirs[0], mine[1], theirs[1]]
    for begin in range(2, len(mine), 2):
        normed += mine[begin : begin + 2] + theirs[begin : begin + 2]
    normed = jnp.concatenate(normed, axis=1)
    width = own_ref.shape[1]
    step = 512 if width % 512 == 0 else 128
    for begin in range(0, width, step):
        lanes = slice(begin, begin + step)
        weight = [own_ref[rows_of(core, HD), lanes], own_ref[rows_of(1 - core, HD), lanes]]
        for mine_ref, theirs_ref in zip(mine_refs, theirs_refs):
            weight += [mine_ref[:, lanes], theirs_ref[:, lanes]]
        out_ref[:, lanes] = dot(normed, jnp.concatenate(weight, axis=0), NN).astype(BF16)


SMEM = pl.BlockSpec(memory_space=pltpu.SMEM)
VMEM = pl.BlockSpec(memory_space=pltpu.VMEM)


def call(kernel, name, outs, args, grant=16):
    return pl.pallas_call(
        kernel,
        name=name,
        out_shape=outs,
        in_specs=[SMEM] + [VMEM] * (len(args) - 1),
        out_specs=[VMEM] * len(outs),
        compiler_params=pltpu.CompilerParams(vmem_limit_bytes=grant * 2**20),
        cost_estimate=pl.CostEstimate(flops=1, bytes_accessed=1, transcendentals=0),
    )(*args)


def without_where(kernel):
    return lambda where_ref, *refs: kernel(*refs)


def after(values, *earlier):
    tied = lax.optimization_barrier((tuple(values), earlier))
    return list(tied[0])


def on_device(queries, keys, values, log_decay, norm_gain, out_weight, out_grad):
    length, columns = queries.shape
    seq = lax.axis_size("seq")
    tensor = lax.axis_size("tensor")
    chips = seq // 2
    model = out_weight.shape[1]
    width = model // tensor
    place = lax.axis_index("tensor")
    core = lax.rem(lax.axis_index("seq"), 2)
    side = lax.rem(lax.axis_index("seq") // 2, 2)
    where = jnp.stack([core, side]).astype(jnp.int32)
    gain = norm_gain.reshape(1, columns)

    def swap_tensor(value, k):
        return lax.ppermute(value, "tensor", [(i, i ^ k) for i in range(tensor)])

    def swap_core(value):
        return lax.ppermute(value, "seq", [(i, i ^ 1) for i in range(seq)])

    def swap_side(value):
        return lax.ppermute(value, "seq", [(i, i ^ 2) for i in range(seq)])

    def to_chip(value, step):
        return lax.ppermute(
            value, "seq", [(i, i + 2 * step) for i in range(seq) if 0 <= i + 2 * step < seq]
        )

    def shape(dtype, *dims):
        return jax.ShapeDtypeStruct(dims, dtype)

    others = range(1, tensor)
    message = shape(BF16, HD + TAIL, HD)
    pair16 = shape(BF16, 2, length, HD)
    pair32 = shape(F32, 2, length, HD)
    one16 = shape(BF16, length, HD)
    both16 = shape(BF16, length, columns)

    far = [step for step in others if step & (step - 1)]
    near = [step for step in others if not step & (step - 1)]
    order = far + near
    plan = [(step, step in far) for step in order]

    def slice_for(step, halves):
        rows = HD // 2 if halves else HD
        begin = core * HD + side * rows if halves else core * HD
        return lax.dynamic_slice(out_weight, (begin, (place ^ step) * width), (rows, width))

    slices = [slice_for(step, halves) for step, halves in plan]
    arriving = [swap_tensor(piece, step) for piece, step in zip(slices, order)]
    got = [swap_core(rows) for rows in (queries, keys, values)]
    got.append(swap_core(log_decay))
    (weight,) = after([out_weight], *slices)
    weight_own = lax.dynamic_slice(weight, (0, place * width), (columns, width))
    got = after(got, weight_own)
    (grad,) = after([out_grad], *got)
    grad_got = swap_core(grad)
    q, k, v, col, row, first, fresh = call(
        fresh_kernel,
        "fresh",
        [pair16, pair16, pair16, shape(F32, length, 2), shape(F32, 2, length), shape(F32, HD, HD), message],
        [where, queries, keys, values, *got[:3], log_decay, got[3]],
    )
    (fresh,) = after([fresh], grad_got)
    arrived, window, step = [], fresh, 1
    while step < chips:
        if arrived:
            (window,) = call(without_where(join_kernel), "join", [message], [where, window, arrived[-1]])
        arrived.append(to_chip(window, step))
        step *= 2
    (inner,) = call(without_where(inner_kernel), "inner", [pair32], [where, q, k, v, col, row, first])
    pieces = [("own", [weight_own])]
    for (step, halves), piece in zip(plan, arriving):
        if halves:
            (piece,) = after([piece], arrived[0])
        pieces.append(("halves", [piece, swap_side(piece)]) if halves else ("whole", [piece]))
    partials, mine, theirs = [], [], []
    for number in range(0, tensor, 2):
        kinds, sources = zip(*pieces[number : number + 2])
        sources = after(sum(sources, []), *arrived, inner, *partials)
        *outs, weight = call(
            functools.partial(partial_kernel, kinds),
            "partial",
            [pair16 if number else pair32, pair16, shape(BF16, 2 * HD if number else HD, width)],
            [where, out_grad, grad_got, *sources],
        )
        partials += outs
        mine.append(weight)
        if number == 0:
            theirs.append(swap_core(weight))
    own_partial, *partials = partials
    sent = [swap_tensor(partial, step) for partial, step in zip(partials, order)]
    mixed, normed, states = call(
        mixed_kernel,
        "mixed",
        [pair32, pair16, shape(F32, 2, HD, HD)],
        [where, q, col, inner, gain, first, *after(arrived, *partials)],
    )
    normed_all = [normed] + [swap_tensor(normed, step) for step in order]
    grad_mixed, second, upward = call(
        grad_mixed_kernel,
        "grad_mixed",
        [pair32, shape(F32, HD, HD), message],
        [where, q, col, gain, mixed, own_partial, *sent],
    )
    (upward,) = after([upward], *normed_all)
    (cross,) = call(cross_kernel, "cross", [shape(BF16, tensor, length, HD)], [where, *normed_all])
    cross_got = swap_core(cross)
    returned = [to_chip(upward, -step) for step in reversed(range(1, chips))]
    theirs += [swap_core(weight) for weight in after(mine[1:], upward)]
    inner_keep, inner_send = call(
        inner_grad_kernel,
        "inner_grad",
        [shape(F32, length, 4 * HD)] * 2,
        [where, q, k, v, col, row, grad_mixed, states, second],
    )
    (layer_out,) = call(
        functools.partial(layer_kernel, tensor // 2),
        "layer",
        [shape(BF16, length, width)],
        [where, weight_own, *mine, *theirs, *normed_all, cross_got],
    )
    returned = after(returned, layer_out)
    inner_got = swap_core(*after([inner_send], *returned))
    returned_got = [swap_core(rows) for rows in returned]
    query_grad, key_grad, value_grad = call(
        functools.partial(outer_grad_kernel, chips - 1),
        "outer_grad",
        [both16] * 3,
        [where, keys, values, inner_keep, inner_got, *returned, *returned_got],
    )
    return layer_out, query_grad, key_grad, value_grad


def solution(mesh):
    in_specs = (
        P("seq", "tensor"),
        P("seq", "tensor"),
        P("seq", "tensor"),
        P("tensor", "seq"),
        P("tensor"),
        P("tensor", None),
        P("seq", "tensor"),
    )
    out_specs = (P("seq", "tensor"), P("seq", "tensor"), P("seq", "tensor"), P("seq", "tensor"))
    return jax.shard_map(
        on_device, mesh=mesh, in_specs=in_specs, out_specs=out_specs, check_vma=False
    )
```

```python
import functools

import jax
import jax.numpy as jnp
from jax import lax
from jax.experimental import pallas as pl
from jax.experimental.pallas import tpu as pltpu
from jax.sharding import PartitionSpec as P

EPSILON = 1e-05
F32 = jnp.float32
BF16 = jnp.bfloat16
TAIL = 16
HD = 128

NN = (((1,), (0,)), ((), ()))
NT = (((1,), (1,)), ((), ()))
TN = (((0,), (0,)), ((), ()))


def dot(a, b, dims):
    return lax.dot_general(a, b, dims, preferred_element_type=F32)


def split(x):
    high = x.astype(BF16)
    return high, (x - high.astype(F32)).astype(BF16)


def dot_fb(a, b, dims):
    high, low = split(a)
    return dot(high, b, dims) + dot(low, b, dims)


def dot_bf(a, b, dims):
    high, low = split(b)
    return dot(a, high, dims) + dot(a, low, dims)


def triangle(length):
    rows = lax.broadcasted_iota(jnp.int32, (length, length), 0)
    cols = lax.broadcasted_iota(jnp.int32, (length, length), 1)
    return rows >= cols


def running_sums(decay, lower):
    ones = lower.astype(BF16)
    columns = rows = 0.0
    for _ in range(3):
        part = decay.astype(BF16)
        decay = decay - part.astype(F32)
        columns = columns + dot(ones, part, NT)
        rows = rows + dot(part, ones, NT)
    return columns, rows


def put_total(ref, base, total):
    first = total.astype(BF16).astype(F32)
    second = (total - first).astype(BF16).astype(F32)
    third = total - first - second
    at = lax.broadcasted_iota(jnp.int32, (TAIL, 128), 0)
    tail = jnp.where(at == 0, first, jnp.where(at == 1, second, jnp.where(at == 2, third, 0.0)))
    ref[base : base + TAIL, :] = tail.astype(BF16)


def get_total(ref, base):
    tail = ref[base : base + TAIL, :].astype(F32)
    return tail[0:1] + tail[1:2] + tail[2:3]


def total_of(columns, block):
    length = columns.shape[0]
    return jnp.broadcast_to(columns[length - 1 : length, block : block + 1], (1, HD))


def chip_sum(refs):
    summed = jnp.zeros((HD, HD), F32)
    passed = jnp.zeros((1, HD), F32)
    for ref in refs:
        summed = summed + jnp.exp(passed) * ref[0:HD, :].astype(F32)
        passed = passed + get_total(ref, HD)
    return summed


def put_message(ref, state, total):
    ref[0:HD, :] = state.astype(BF16)
    put_total(ref, HD, total)


def join_kernel(own_ref, got_ref, out_ref):
    total = get_total(own_ref, HD)
    state = own_ref[0:HD, :].astype(F32) + jnp.exp(total) * got_ref[0:HD, :].astype(F32)
    put_message(out_ref, state, total + get_total(got_ref, HD))


def cross_kernel(where_ref, *refs):
    *normed_refs, cross_ref = refs
    for number, ref in enumerate(normed_refs):
        cross_ref[number] = ref[1 - where_ref[0]]


def lanes_of(number):
    return pl.ds(pl.multiple_of(number * HD, HD), HD)


def rows_of(number, count):
    return pl.ds(pl.multiple_of(number * count, count), count)


def fresh_kernel(
    where_ref, q_ref, k_ref, v_ref, q_got, k_got, v_got, decay_ref, decay_got, q_out, k_out, v_out, col_ref, row_ref, first_ref, message_ref
):
    core = where_ref[0]
    length = q_ref.shape[0]
    for out, ref, got in ((q_out, q_ref, q_got), (k_out, k_ref, k_got), (v_out, v_ref, v_got)):
        out[core] = ref[:, lanes_of(core)]
        out[1 - core] = got[:, lanes_of(core)]
    mine = jnp.where(core == 0, decay_ref[0:1, :], decay_ref[1:2, :])
    theirs = jnp.where(core == 0, decay_got[0:1, :], decay_got[1:2, :])
    block = lax.broadcasted_iota(jnp.int32, (2, length), 0)
    decay = jnp.where(block == core, mine, theirs)
    lower = triangle(length)
    columns, rows = running_sums(decay, lower)
    col_ref[...] = columns
    row_ref[...] = rows
    states = []
    for b in range(2):
        fade = jnp.exp(columns[length - 1 : length, b : b + 1] - columns[:, b : b + 1])
        states.append(dot(k_out[b], (fade * v_out[b].astype(F32)).astype(BF16), TN))
    totals = [total_of(columns, b) for b in range(2)]
    first_ref[...] = states[0]
    put_message(message_ref, jnp.exp(totals[1]) * states[0] + states[1], totals[0] + totals[1])


def weights(columns, across, lower, b):
    return jnp.exp(jnp.where(lower, columns[:, b : b + 1] - across[b : b + 1, :], -1e30))


def inner_kernel(q_ref, k_ref, v_ref, col_ref, row_ref, first_ref, inner_ref):
    columns, across = col_ref[...], row_ref[...]
    lower = triangle(columns.shape[0])
    for b in range(2):
        scores = dot(q_ref[b], k_ref[b], NT) * weights(columns, across, lower, b)
        inner = dot_fb(scores, v_ref[b], NN)
        if b == 1:
            inner = inner + jnp.exp(columns[:, 1:2]) * dot_bf(q_ref[b], first_ref[...], NN)
        inner_ref[b] = inner


def scale_of(mixed):
    return lax.rsqrt(jnp.mean(mixed * mixed, axis=-1, keepdims=True) + EPSILON)


def mixed_kernel(where_ref, q_ref, col_ref, inner_ref, gain_ref, first_ref, *refs):
    chip_refs, (mixed_ref, normed_ref, state_ref) = refs[:-3], refs[-3:]
    core = where_ref[0]
    columns = col_ref[...]
    gain = gain_ref[:, lanes_of(core)]
    state = chip_sum(chip_refs)
    high, low = split(state)
    shrink = jnp.exp(total_of(columns, 0))
    state_ref[0] = state
    state_ref[1] = shrink * state + first_ref[...]
    for b in range(2):
        grow = jnp.exp(columns[:, b : b + 1])
        if b == 1:
            grow = grow * shrink
        mixed = inner_ref[b] + grow * (dot(q_ref[b], high, NN) + dot(q_ref[b], low, NN))
        mixed_ref[b] = mixed
        normed_ref[b] = (mixed * scale_of(mixed) * gain).astype(BF16)


def partial_kernel(kinds, where_ref, grad_ref, got_ref, *refs):
    core, side = where_ref[0], where_ref[1]
    refs = list(refs)
    inputs = [[refs.pop(0) for _ in range(2 if kind == "halves" else 1)] for kind in kinds]
    *products, weight_out = refs
    weights = []
    for kind, sources in zip(kinds, inputs):
        if kind == "own":
            weights.append(sources[0][rows_of(core, HD), :])
        elif kind == "halves":
            mine, theirs = sources[0][...], sources[1][...]
            weights += [jnp.where(side == 0, mine, theirs), jnp.where(side == 0, theirs, mine)]
        else:
            weights.append(sources[0][...])
    weight = jnp.concatenate(weights, axis=0)
    weight_out[...] = weight[2 * HD - weight_out.shape[0] :]
    length = grad_ref.shape[0]
    product = dot(jnp.concatenate([grad_ref[...], got_ref[...]], axis=0), weight, NT)
    for begin, block in ((0, core), (length, 1 - core)):
        for number, out in enumerate(products):
            part = product[begin : begin + length, number * HD : (number + 1) * HD]
            out[block] = part.astype(out.dtype)


def grad_mixed_kernel(where_ref, q_ref, col_ref, gain_ref, mixed_ref, own_ref, *refs):
    part_refs, (grad_ref, second_ref, message_ref) = refs[:-3], refs[-3:]
    columns = col_ref[...]
    gain = gain_ref[:, lanes_of(where_ref[0])]
    ups = []
    for b in range(2):
        normed = own_ref[b]
        for ref in part_refs:
            normed = normed + ref[b].astype(F32)
        lifted = normed * gain
        mixed = mixed_ref[b]
        scale = scale_of(mixed)
        unit = mixed * scale
        grad = scale * (lifted - unit * jnp.mean(unit * lifted, axis=-1, keepdims=True))
        grad_ref[b] = grad
        ups.append(dot(q_ref[b], (jnp.exp(columns[:, b : b + 1]) * grad).astype(BF16), TN))
    second_ref[...] = ups[1]
    totals = [total_of(columns, b) for b in range(2)]
    put_message(message_ref, ups[0] + jnp.exp(totals[0]) * ups[1], totals[0] + totals[1])


def inner_grad_kernel(
    where_ref, q_ref, k_ref, v_ref, col_ref, row_ref, grad_ref, state_ref, second_ref, keep_ref, send_ref
):
    core = where_ref[0]
    columns, across = col_ref[...], row_ref[...]
    length = columns.shape[0]
    lower = triangle(length)
    parts = []
    ends = [columns[length - 1 : length, b : b + 1] for b in range(2)]
    for b in range(2):
        q, k, v, grad = q_ref[b], k_ref[b], v_ref[b], grad_ref[b]
        weight = weights(columns, across, lower, b)
        narrow = grad.astype(BF16)
        scores = (dot(q, k, NT) * weight).astype(BF16)
        grad_scores = (dot(narrow, v, NT) * weight).astype(BF16)
        carried = jnp.exp(columns[:, b : b + 1]) * dot(narrow, state_ref[b].astype(BF16), NT)
        dq = dot(grad_scores, k, NN) + carried
        dk = dot(grad_scores, q, TN)
        dv = dot(scores, narrow, TN)
        fade = jnp.exp(ends[b] - columns[:, b : b + 1])
        if b == 0:
            second = second_ref[...].astype(BF16)
            dk = dk + fade * dot(v, second, NT)
            dv = dv + fade * dot(k, second, NN)
            fade = fade * jnp.exp(ends[1])
        parts.append((dq, dk, dv, jnp.broadcast_to(fade, (length, HD))))
    for number, (early, late) in enumerate(zip(*parts)):
        part = slice(number * HD, (number + 1) * HD)
        keep_ref[:, part] = jnp.where(core == 0, early, late)
        send_ref[:, part] = jnp.where(core == 0, late, early)


def outer_grad_kernel(count, where_ref, k_ref, v_ref, inner_ref, inner_got_ref, *refs):
    core = where_ref[0]
    outs = refs[2 * count :]
    for head, inner, chip_refs in (
        (core, inner_ref, refs[:count][::-1]),
        (1 - core, inner_got_ref, refs[count : 2 * count][::-1]),
    ):
        state = chip_sum(chip_refs).astype(BF16)
        fade = inner[:, 3 * HD : 4 * HD]
        k, v = k_ref[:, lanes_of(head)], v_ref[:, lanes_of(head)]
        outs[0][:, lanes_of(head)] = inner[:, 0:HD].astype(BF16)
        key = inner[:, HD : 2 * HD] + fade * dot(v, state, NT)
        outs[1][:, lanes_of(head)] = key.astype(BF16)
        value = inner[:, 2 * HD : 3 * HD] + fade * dot(k, state, NN)
        outs[2][:, lanes_of(head)] = value.astype(BF16)


def layer_kernel(pairs, where_ref, own_ref, *refs):
    mine_refs, theirs_refs = refs[:pairs], refs[pairs : 2 * pairs]
    *normed_refs, got_ref, out_ref = refs[2 * pairs :]
    core = where_ref[0]
    mine = [ref[core] for ref in normed_refs]
    theirs = [got_ref[number] for number in range(got_ref.shape[0])]
    first = core == 0
    own = jnp.concatenate([jnp.where(first, mine[0], theirs[0]), jnp.where(first, theirs[0], mine[0])], axis=1)
    pieces = [(own, own_ref), (mine[1], mine_refs[0]), (theirs[1], theirs_refs[0])]
    for pair in range(1, pairs):
        for rows, refs in ((mine, mine_refs), (theirs, theirs_refs)):
            pieces.append((jnp.concatenate(rows[2 * pair : 2 * pair + 2], axis=1), refs[pair]))
    width = own_ref.shape[1]
    step = 512 if width % 512 == 0 else 128
    for begin in range(0, width, step):
        lanes = slice(begin, begin + step)
        out_ref[:, lanes] = sum(dot(rows, ref[:, lanes], NN) for rows, ref in pieces).astype(BF16)


SMEM = pl.BlockSpec(memory_space=pltpu.SMEM)
VMEM = pl.BlockSpec(memory_space=pltpu.VMEM)


def call(kernel, name, outs, args, grant=16):
    return pl.pallas_call(
        kernel,
        name=name,
        out_shape=outs,
        in_specs=[SMEM] + [VMEM] * (len(args) - 1),
        out_specs=[VMEM] * len(outs),
        compiler_params=pltpu.CompilerParams(vmem_limit_bytes=grant * 2**20),
        cost_estimate=pl.CostEstimate(flops=1, bytes_accessed=1, transcendentals=0),
    )(*args)


def without_where(kernel):
    return lambda where_ref, *refs: kernel(*refs)


def after(values, *earlier):
    tied = lax.optimization_barrier((tuple(values), earlier))
    return list(tied[0])


def on_device(queries, keys, values, log_decay, norm_gain, out_weight, out_grad):
    length, columns = queries.shape
    seq = lax.axis_size("seq")
    tensor = lax.axis_size("tensor")
    chips = seq // 2
    model = out_weight.shape[1]
    width = model // tensor
    place = lax.axis_index("tensor")
    core = lax.rem(lax.axis_index("seq"), 2)
    side = lax.rem(lax.axis_index("seq") // 2, 2)
    where = jnp.stack([core, side]).astype(jnp.int32)
    gain = norm_gain.reshape(1, columns)

    def swap_tensor(value, k):
        return lax.ppermute(value, "tensor", [(i, i ^ k) for i in range(tensor)])

    def swap_core(value):
        return lax.ppermute(value, "seq", [(i, i ^ 1) for i in range(seq)])

    def swap_side(value):
        return lax.ppermute(value, "seq", [(i, i ^ 2) for i in range(seq)])

    def to_chip(value, step):
        return lax.ppermute(
            value, "seq", [(i, i + 2 * step) for i in range(seq) if 0 <= i + 2 * step < seq]
        )

    def shape(dtype, *dims):
        return jax.ShapeDtypeStruct(dims, dtype)

    others = range(1, tensor)
    message = shape(BF16, HD + TAIL, HD)
    pair16 = shape(BF16, 2, length, HD)
    pair32 = shape(F32, 2, length, HD)
    one16 = shape(BF16, length, HD)
    both16 = shape(BF16, length, columns)

    far = [step for step in others if step & (step - 1)]
    near = [step for step in others if not step & (step - 1)]
    order = far + near
    plan = [(step, step in far) for step in order]

    def slice_for(step, halves):
        rows = HD // 2 if halves else HD
        begin = core * HD + side * rows if halves else core * HD
        return lax.dynamic_slice(out_weight, (begin, (place ^ step) * width), (rows, width))

    slices = [slice_for(step, halves) for step, halves in plan]
    arriving = [swap_tensor(piece, step) for piece, step in zip(slices, order)]
    got = [swap_core(rows) for rows in (queries, keys, values)]
    got.append(swap_core(log_decay))
    (weight,) = after([out_weight], *slices)
    weight_own = lax.dynamic_slice(weight, (0, place * width), (columns, width))
    got = after(got, weight_own)
    (grad,) = after([out_grad], *got)
    grad_got = swap_core(grad)
    q, k, v, col, row, first, fresh = call(
        fresh_kernel,
        "fresh",
        [pair16, pair16, pair16, shape(F32, length, 2), shape(F32, 2, length), shape(F32, HD, HD), message],
        [where, queries, keys, values, *got[:3], log_decay, got[3]],
    )
    (fresh,) = after([fresh], grad_got)
    arrived, window, step = [], fresh, 1
    while step < chips:
        if arrived:
            (window,) = call(without_where(join_kernel), "join", [message], [where, window, arrived[-1]])
        arrived.append(to_chip(window, step))
        step *= 2
    (inner,) = call(without_where(inner_kernel), "inner", [pair32], [where, q, k, v, col, row, first])
    pieces = [("own", [weight_own])]
    for (step, halves), piece in zip(plan, arriving):
        if halves:
            (piece,) = after([piece], arrived[0])
        pieces.append(("halves", [piece, swap_side(piece)]) if halves else ("whole", [piece]))
    partials, mine, theirs = [], [], []
    for number in range(0, tensor, 2):
        kinds, sources = zip(*pieces[number : number + 2])
        sources = after(sum(sources, []), *arrived, inner, *partials)
        *outs, weight = call(
            functools.partial(partial_kernel, kinds),
            "partial",
            [pair16 if number else pair32, pair16, shape(BF16, 2 * HD if number else HD, width)],
            [where, out_grad, grad_got, *sources],
        )
        partials += outs
        mine.append(weight)
        if number == 0:
            theirs.append(swap_core(weight))
    own_partial, *partials = partials
    sent = [swap_tensor(partial, step) for partial, step in zip(partials, order)]
    mixed, normed, states = call(
        mixed_kernel,
        "mixed",
        [pair32, pair16, shape(F32, 2, HD, HD)],
        [where, q, col, inner, gain, first, *after(arrived, *partials)],
    )
    normed_all = [normed] + [swap_tensor(normed, step) for step in order]
    grad_mixed, second, upward = call(
        grad_mixed_kernel,
        "grad_mixed",
        [pair32, shape(F32, HD, HD), message],
        [where, q, col, gain, mixed, own_partial, *sent],
    )
    (upward,) = after([upward], *normed_all)
    (cross,) = call(cross_kernel, "cross", [shape(BF16, tensor, length, HD)], [where, *normed_all])
    cross_got = swap_core(cross)
    returned = [to_chip(upward, -step) for step in reversed(range(1, chips))]
    theirs += [swap_core(weight) for weight in after(mine[1:], upward)]
    inner_keep, inner_send = call(
        inner_grad_kernel,
        "inner_grad",
        [shape(F32, length, 4 * HD)] * 2,
        [where, q, k, v, col, row, grad_mixed, states, second],
    )
    (layer_out,) = call(
        functools.partial(layer_kernel, tensor // 2),
        "layer",
        [shape(BF16, length, width)],
        [where, weight_own, *mine, *theirs, *normed_all, cross_got],
    )
    returned = after(returned, layer_out)
    inner_got = swap_core(*after([inner_send], *returned))
    returned_got = [swap_core(rows) for rows in returned]
    query_grad, key_grad, value_grad = call(
        functools.partial(outer_grad_kernel, chips - 1),
        "outer_grad",
        [both16] * 3,
        [where, keys, values, inner_keep, inner_got, *returned, *returned_got],
    )
    return layer_out, query_grad, key_grad, value_grad


def solution(mesh):
    in_specs = (
        P("seq", "tensor"),
        P("seq", "tensor"),
        P("seq", "tensor"),
        P("tensor", "seq"),
        P("tensor"),
        P("tensor", None),
        P("seq", "tensor"),
    )
    out_specs = (P("seq", "tensor"), P("seq", "tensor"), P("seq", "tensor"), P("seq", "tensor"))
    return jax.shard_map(
        on_device, mesh=mesh, in_specs=in_specs, out_specs=out_specs, check_vma=False
    )
```

```python
import functools

import jax
import jax.numpy as jnp
from jax import lax
from jax.experimental import pallas as pl
from jax.experimental.pallas import tpu as pltpu
from jax.sharding import PartitionSpec as P

EPSILON = 1e-05
F32 = jnp.float32
BF16 = jnp.bfloat16
TAIL = 16
HD = 128

NN = (((1,), (0,)), ((), ()))
NT = (((1,), (1,)), ((), ()))
TN = (((0,), (0,)), ((), ()))


def dot(a, b, dims):
    return lax.dot_general(a, b, dims, preferred_element_type=F32)


def split(x):
    high = x.astype(BF16)
    return high, (x - high.astype(F32)).astype(BF16)


def dot_fb(a, b, dims):
    high, low = split(a)
    return dot(high, b, dims) + dot(low, b, dims)


def dot_bf(a, b, dims):
    high, low = split(b)
    return dot(a, high, dims) + dot(a, low, dims)


def triangle(length):
    rows = lax.broadcasted_iota(jnp.int32, (length, length), 0)
    cols = lax.broadcasted_iota(jnp.int32, (length, length), 1)
    return rows >= cols


def running_sums(decay, lower):
    ones = lower.astype(BF16)
    columns = rows = 0.0
    for _ in range(3):
        part = decay.astype(BF16)
        decay = decay - part.astype(F32)
        columns = columns + dot(ones, part, NT)
        rows = rows + dot(part, ones, NT)
    return columns, rows


def put_total(ref, base, total):
    first = total.astype(BF16).astype(F32)
    second = (total - first).astype(BF16).astype(F32)
    third = total - first - second
    at = lax.broadcasted_iota(jnp.int32, (TAIL, 128), 0)
    tail = jnp.where(at == 0, first, jnp.where(at == 1, second, jnp.where(at == 2, third, 0.0)))
    ref[base : base + TAIL, :] = tail.astype(BF16)


def get_total(ref, base):
    tail = ref[base : base + TAIL, :].astype(F32)
    return tail[0:1] + tail[1:2] + tail[2:3]


def total_of(columns, block):
    length = columns.shape[0]
    return jnp.broadcast_to(columns[length - 1 : length, block : block + 1], (1, HD))


def chip_sum(refs):
    summed = jnp.zeros((HD, HD), F32)
    passed = jnp.zeros((1, HD), F32)
    for ref in refs:
        summed = summed + jnp.exp(passed) * ref[0:HD, :].astype(F32)
        passed = passed + get_total(ref, HD)
    return summed


def put_message(ref, state, total):
    ref[0:HD, :] = state.astype(BF16)
    put_total(ref, HD, total)


def join_kernel(own_ref, got_ref, out_ref):
    total = get_total(own_ref, HD)
    state = own_ref[0:HD, :].astype(F32) + jnp.exp(total) * got_ref[0:HD, :].astype(F32)
    put_message(out_ref, state, total + get_total(got_ref, HD))


def cross_kernel(where_ref, *refs):
    *normed_refs, cross_ref = refs
    for number, ref in enumerate(normed_refs):
        cross_ref[number] = ref[1 - where_ref[0]]


def lanes_of(number):
    return pl.ds(pl.multiple_of(number * HD, HD), HD)


def rows_of(number, count):
    return pl.ds(pl.multiple_of(number * count, count), count)


def fresh_kernel(
    where_ref, q_ref, k_ref, v_ref, q_got, k_got, v_got, decay_ref, decay_got, q_out, k_out, v_out, col_ref, row_ref, first_ref, message_ref
):
    core = where_ref[0]
    length = q_ref.shape[0]
    for out, ref, got in ((q_out, q_ref, q_got), (k_out, k_ref, k_got), (v_out, v_ref, v_got)):
        out[core] = ref[:, lanes_of(core)]
        out[1 - core] = got[:, lanes_of(core)]
    mine = jnp.where(core == 0, decay_ref[0:1, :], decay_ref[1:2, :])
    theirs = jnp.where(core == 0, decay_got[0:1, :], decay_got[1:2, :])
    block = lax.broadcasted_iota(jnp.int32, (2, length), 0)
    decay = jnp.where(block == core, mine, theirs)
    lower = triangle(length)
    columns, rows = running_sums(decay, lower)
    col_ref[...] = columns
    row_ref[...] = rows
    states = []
    for b in range(2):
        fade = jnp.exp(columns[length - 1 : length, b : b + 1] - columns[:, b : b + 1])
        states.append(dot(k_out[b], (fade * v_out[b].astype(F32)).astype(BF16), TN))
    totals = [total_of(columns, b) for b in range(2)]
    first_ref[...] = states[0]
    put_message(message_ref, jnp.exp(totals[1]) * states[0] + states[1], totals[0] + totals[1])


def weights(columns, across, lower, b):
    return jnp.exp(jnp.where(lower, columns[:, b : b + 1] - across[b : b + 1, :], -1e30))


def inner_kernel(q_ref, k_ref, v_ref, col_ref, row_ref, first_ref, inner_ref):
    columns, across = col_ref[...], row_ref[...]
    lower = triangle(columns.shape[0])
    for b in range(2):
        scores = dot(q_ref[b], k_ref[b], NT) * weights(columns, across, lower, b)
        inner = dot_fb(scores, v_ref[b], NN)
        if b == 1:
            inner = inner + jnp.exp(columns[:, 1:2]) * dot_bf(q_ref[b], first_ref[...], NN)
        inner_ref[b] = inner


def scale_of(mixed):
    return lax.rsqrt(jnp.mean(mixed * mixed, axis=-1, keepdims=True) + EPSILON)


def mixed_kernel(where_ref, q_ref, col_ref, inner_ref, gain_ref, first_ref, *refs):
    chip_refs, (mixed_ref, normed_ref, state_ref) = refs[:-3], refs[-3:]
    core = where_ref[0]
    columns = col_ref[...]
    gain = gain_ref[:, lanes_of(core)]
    state = chip_sum(chip_refs)
    high, low = split(state)
    shrink = jnp.exp(total_of(columns, 0))
    state_ref[0] = state
    state_ref[1] = shrink * state + first_ref[...]
    for b in range(2):
        grow = jnp.exp(columns[:, b : b + 1])
        if b == 1:
            grow = grow * shrink
        mixed = inner_ref[b] + grow * (dot(q_ref[b], high, NN) + dot(q_ref[b], low, NN))
        mixed_ref[b] = mixed
        normed_ref[b] = (mixed * scale_of(mixed) * gain).astype(BF16)


def partial_kernel(kinds, where_ref, grad_ref, got_ref, *refs):
    core, side = where_ref[0], where_ref[1]
    refs = list(refs)
    inputs = [[refs.pop(0) for _ in range(2 if kind == "halves" else 1)] for kind in kinds]
    *products, weight_out = refs
    weights = []
    for kind, sources in zip(kinds, inputs):
        if kind == "own":
            weights.append(sources[0][rows_of(core, HD), :])
        elif kind == "halves":
            mine, theirs = sources[0][...], sources[1][...]
            weights += [jnp.where(side == 0, mine, theirs), jnp.where(side == 0, theirs, mine)]
        else:
            weights.append(sources[0][...])
    weight = jnp.concatenate(weights, axis=0)
    weight_out[...] = weight[2 * HD - weight_out.shape[0] :]
    length = grad_ref.shape[0]
    product = dot(jnp.concatenate([grad_ref[...], got_ref[...]], axis=0), weight, NT)
    for begin, block in ((0, core), (length, 1 - core)):
        for number, out in enumerate(products):
            part = product[begin : begin + length, number * HD : (number + 1) * HD]
            out[block] = part.astype(out.dtype)


def grad_mixed_kernel(where_ref, q_ref, col_ref, gain_ref, mixed_ref, own_ref, *refs):
    part_refs, (grad_ref, second_ref, message_ref) = refs[:-3], refs[-3:]
    columns = col_ref[...]
    gain = gain_ref[:, lanes_of(where_ref[0])]
    ups = []
    for b in range(2):
        normed = own_ref[b]
        for ref in part_refs:
            normed = normed + ref[b].astype(F32)
        lifted = normed * gain
        mixed = mixed_ref[b]
        scale = scale_of(mixed)
        unit = mixed * scale
        grad = scale * (lifted - unit * jnp.mean(unit * lifted, axis=-1, keepdims=True))
        grad_ref[b] = grad
        ups.append(dot(q_ref[b], (jnp.exp(columns[:, b : b + 1]) * grad).astype(BF16), TN))
    second_ref[...] = ups[1]
    totals = [total_of(columns, b) for b in range(2)]
    put_message(message_ref, ups[0] + jnp.exp(totals[0]) * ups[1], totals[0] + totals[1])


def inner_grad_kernel(
    where_ref, q_ref, k_ref, v_ref, col_ref, row_ref, grad_ref, state_ref, second_ref, keep_ref, send_ref
):
    core = where_ref[0]
    columns, across = col_ref[...], row_ref[...]
    length = columns.shape[0]
    lower = triangle(length)
    parts = []
    ends = [columns[length - 1 : length, b : b + 1] for b in range(2)]
    for b in range(2):
        q, k, v, grad = q_ref[b], k_ref[b], v_ref[b], grad_ref[b]
        weight = weights(columns, across, lower, b)
        narrow = grad.astype(BF16)
        scores = (dot(q, k, NT) * weight).astype(BF16)
        grad_scores = (dot(narrow, v, NT) * weight).astype(BF16)
        carried = jnp.exp(columns[:, b : b + 1]) * dot(narrow, state_ref[b].astype(BF16), NT)
        dq = dot(grad_scores, k, NN) + carried
        dk = dot(grad_scores, q, TN)
        dv = dot(scores, narrow, TN)
        fade = jnp.exp(ends[b] - columns[:, b : b + 1])
        if b == 0:
            second = second_ref[...].astype(BF16)
            dk = dk + fade * dot(v, second, NT)
            dv = dv + fade * dot(k, second, NN)
            fade = fade * jnp.exp(ends[1])
        parts.append((dq, dk, dv, jnp.broadcast_to(fade, (length, HD))))
    for number, (early, late) in enumerate(zip(*parts)):
        part = slice(number * HD, (number + 1) * HD)
        keep_ref[:, part] = jnp.where(core == 0, early, late)
        send_ref[:, part] = jnp.where(core == 0, late, early).astype(BF16)


def outer_grad_kernel(count, where_ref, k_ref, v_ref, inner_ref, inner_got_ref, *refs):
    core = where_ref[0]
    outs = refs[2 * count :]
    for head, inner, chip_refs in (
        (core, inner_ref, refs[:count][::-1]),
        (1 - core, inner_got_ref, refs[count : 2 * count][::-1]),
    ):
        state = chip_sum(chip_refs).astype(BF16)
        fade = inner[:, 3 * HD : 4 * HD].astype(F32)
        k, v = k_ref[:, lanes_of(head)], v_ref[:, lanes_of(head)]
        outs[0][:, lanes_of(head)] = inner[:, 0:HD].astype(BF16)
        key = inner[:, HD : 2 * HD].astype(F32) + fade * dot(v, state, NT)
        outs[1][:, lanes_of(head)] = key.astype(BF16)
        value = inner[:, 2 * HD : 3 * HD].astype(F32) + fade * dot(k, state, NN)
        outs[2][:, lanes_of(head)] = value.astype(BF16)


def layer_kernel(pairs, where_ref, own_ref, *refs):
    mine_refs, theirs_refs = refs[:pairs], refs[pairs : 2 * pairs]
    *normed_refs, got_ref, out_ref = refs[2 * pairs :]
    core = where_ref[0]
    mine = [ref[core] for ref in normed_refs]
    theirs = [got_ref[number] for number in range(got_ref.shape[0])]
    normed = [mine[0], theirs[0], mine[1], theirs[1]]
    for begin in range(2, len(mine), 2):
        normed += mine[begin : begin + 2] + theirs[begin : begin + 2]
    normed = jnp.concatenate(normed, axis=1)
    width = own_ref.shape[1]
    step = 512 if width % 512 == 0 else 128
    for begin in range(0, width, step):
        lanes = slice(begin, begin + step)
        weight = [own_ref[rows_of(core, HD), lanes], own_ref[rows_of(1 - core, HD), lanes]]
        for mine_ref, theirs_ref in zip(mine_refs, theirs_refs):
            weight += [mine_ref[:, lanes], theirs_ref[:, lanes]]
        out_ref[:, lanes] = dot(normed, jnp.concatenate(weight, axis=0), NN).astype(BF16)


SMEM = pl.BlockSpec(memory_space=pltpu.SMEM)
VMEM = pl.BlockSpec(memory_space=pltpu.VMEM)


def call(kernel, name, outs, args, grant=16):
    return pl.pallas_call(
        kernel,
        name=name,
        out_shape=outs,
        in_specs=[SMEM] + [VMEM] * (len(args) - 1),
        out_specs=[VMEM] * len(outs),
        compiler_params=pltpu.CompilerParams(vmem_limit_bytes=grant * 2**20),
        cost_estimate=pl.CostEstimate(flops=1, bytes_accessed=1, transcendentals=0),
    )(*args)


def without_where(kernel):
    return lambda where_ref, *refs: kernel(*refs)


def after(values, *earlier):
    tied = lax.optimization_barrier((tuple(values), earlier))
    return list(tied[0])


def on_device(queries, keys, values, log_decay, norm_gain, out_weight, out_grad):
    length, columns = queries.shape
    seq = lax.axis_size("seq")
    tensor = lax.axis_size("tensor")
    chips = seq // 2
    model = out_weight.shape[1]
    width = model // tensor
    place = lax.axis_index("tensor")
    core = lax.rem(lax.axis_index("seq"), 2)
    side = lax.rem(lax.axis_index("seq") // 2, 2)
    where = jnp.stack([core, side]).astype(jnp.int32)
    gain = norm_gain.reshape(1, columns)

    def swap_tensor(value, k):
        return lax.ppermute(value, "tensor", [(i, i ^ k) for i in range(tensor)])

    def swap_core(value):
        return lax.ppermute(value, "seq", [(i, i ^ 1) for i in range(seq)])

    def swap_side(value):
        return lax.ppermute(value, "seq", [(i, i ^ 2) for i in range(seq)])

    def to_chip(value, step):
        return lax.ppermute(
            value, "seq", [(i, i + 2 * step) for i in range(seq) if 0 <= i + 2 * step < seq]
        )

    def shape(dtype, *dims):
        return jax.ShapeDtypeStruct(dims, dtype)

    others = range(1, tensor)
    message = shape(BF16, HD + TAIL, HD)
    pair16 = shape(BF16, 2, length, HD)
    pair32 = shape(F32, 2, length, HD)
    one16 = shape(BF16, length, HD)
    both16 = shape(BF16, length, columns)

    far = [step for step in others if step & (step - 1)]
    near = [step for step in others if not step & (step - 1)]
    order = far + near
    plan = [(step, step in far) for step in order]

    def slice_for(step, halves):
        rows = HD // 2 if halves else HD
        begin = core * HD + side * rows if halves else core * HD
        return lax.dynamic_slice(out_weight, (begin, (place ^ step) * width), (rows, width))

    slices = [slice_for(step, halves) for step, halves in plan]
    arriving = [swap_tensor(piece, step) for piece, step in zip(slices, order)]
    got = [swap_core(rows) for rows in (queries, keys, values)]
    got.append(swap_core(log_decay))
    (weight,) = after([out_weight], *slices)
    weight_own = lax.dynamic_slice(weight, (0, place * width), (columns, width))
    got = after(got, weight_own)
    (grad,) = after([out_grad], *got)
    grad_got = swap_core(grad)
    q, k, v, col, row, first, fresh = call(
        fresh_kernel,
        "fresh",
        [pair16, pair16, pair16, shape(F32, length, 2), shape(F32, 2, length), shape(F32, HD, HD), message],
        [where, queries, keys, values, *got[:3], log_decay, got[3]],
    )
    (fresh,) = after([fresh], grad_got)
    arrived, window, step = [], fresh, 1
    while step < chips:
        if arrived:
            (window,) = call(without_where(join_kernel), "join", [message], [where, window, arrived[-1]])
        arrived.append(to_chip(window, step))
        step *= 2
    (inner,) = call(without_where(inner_kernel), "inner", [pair32], [where, q, k, v, col, row, first])
    pieces = [("own", [weight_own])]
    for (step, halves), piece in zip(plan, arriving):
        if halves:
            (piece,) = after([piece], arrived[0])
        pieces.append(("halves", [piece, swap_side(piece)]) if halves else ("whole", [piece]))
    partials, mine, theirs = [], [], []
    for number in range(0, tensor, 2):
        kinds, sources = zip(*pieces[number : number + 2])
        sources = after(sum(sources, []), *arrived, inner, *partials)
        *outs, weight = call(
            functools.partial(partial_kernel, kinds),
            "partial",
            [pair16 if number else pair32, pair16, shape(BF16, 2 * HD if number else HD, width)],
            [where, out_grad, grad_got, *sources],
        )
        partials += outs
        mine.append(weight)
        if number == 0:
            theirs.append(swap_core(weight))
    own_partial, *partials = partials
    sent = [swap_tensor(partial, step) for partial, step in zip(partials, order)]
    mixed, normed, states = call(
        mixed_kernel,
        "mixed",
        [pair32, pair16, shape(F32, 2, HD, HD)],
        [where, q, col, inner, gain, first, *after(arrived, *partials)],
    )
    normed_all = [normed] + [swap_tensor(normed, step) for step in order]
    grad_mixed, second, upward = call(
        grad_mixed_kernel,
        "grad_mixed",
        [pair32, shape(F32, HD, HD), message],
        [where, q, col, gain, mixed, own_partial, *sent],
    )
    (upward,) = after([upward], *normed_all)
    (cross,) = call(cross_kernel, "cross", [shape(BF16, tensor, length, HD)], [where, *normed_all])
    cross_got = swap_core(cross)
    returned = [to_chip(upward, -step) for step in reversed(range(1, chips))]
    theirs += [swap_core(weight) for weight in after(mine[1:], upward)]
    inner_keep, inner_send = call(
        inner_grad_kernel,
        "inner_grad",
        [shape(F32, length, 4 * HD), shape(BF16, length, 4 * HD)],
        [where, q, k, v, col, row, grad_mixed, states, second],
    )
    (layer_out,) = call(
        functools.partial(layer_kernel, tensor // 2),
        "layer",
        [shape(BF16, length, width)],
        [where, weight_own, *mine, *theirs, *normed_all, cross_got],
    )
    returned = after(returned, layer_out)
    inner_got = swap_core(*after([inner_send], *returned))
    returned_got = [swap_core(rows) for rows in returned]
    query_grad, key_grad, value_grad = call(
        functools.partial(outer_grad_kernel, chips - 1),
        "outer_grad",
        [both16] * 3,
        [where, keys, values, inner_keep, inner_got, *returned, *returned_got],
    )
    return layer_out, query_grad, key_grad, value_grad


def solution(mesh):
    in_specs = (
        P("seq", "tensor"),
        P("seq", "tensor"),
        P("seq", "tensor"),
        P("tensor", "seq"),
        P("tensor"),
        P("tensor", None),
        P("seq", "tensor"),
    )
    out_specs = (P("seq", "tensor"), P("seq", "tensor"), P("seq", "tensor"), P("seq", "tensor"))
    return jax.shard_map(
        on_device, mesh=mesh, in_specs=in_specs, out_specs=out_specs, check_vma=False
    )
```

```python
import functools

import jax
import jax.numpy as jnp
from jax import lax
from jax.experimental import pallas as pl
from jax.experimental.pallas import tpu as pltpu
from jax.sharding import PartitionSpec as P

EPSILON = 1e-05
F32 = jnp.float32
BF16 = jnp.bfloat16
TAIL = 16
HD = 128

NN = (((1,), (0,)), ((), ()))
NT = (((1,), (1,)), ((), ()))
TN = (((0,), (0,)), ((), ()))


def dot(a, b, dims):
    return lax.dot_general(a, b, dims, preferred_element_type=F32)


def split(x):
    high = x.astype(BF16)
    return high, (x - high.astype(F32)).astype(BF16)


def dot_fb(a, b, dims):
    high, low = split(a)
    return dot(high, b, dims) + dot(low, b, dims)


def dot_bf(a, b, dims):
    high, low = split(b)
    return dot(a, high, dims) + dot(a, low, dims)


def triangle(length):
    rows = lax.broadcasted_iota(jnp.int32, (length, length), 0)
    cols = lax.broadcasted_iota(jnp.int32, (length, length), 1)
    return rows >= cols


def running_sums(decay, lower):
    ones = lower.astype(BF16)
    columns = rows = 0.0
    for _ in range(3):
        part = decay.astype(BF16)
        decay = decay - part.astype(F32)
        columns = columns + dot(ones, part, NT)
        rows = rows + dot(part, ones, NT)
    return columns, rows


def put_total(ref, base, total):
    first = total.astype(BF16).astype(F32)
    second = (total - first).astype(BF16).astype(F32)
    third = total - first - second
    at = lax.broadcasted_iota(jnp.int32, (TAIL, 128), 0)
    tail = jnp.where(at == 0, first, jnp.where(at == 1, second, jnp.where(at == 2, third, 0.0)))
    ref[base : base + TAIL, :] = tail.astype(BF16)


def get_total(ref, base):
    tail = ref[base : base + TAIL, :].astype(F32)
    return tail[0:1] + tail[1:2] + tail[2:3]


def total_of(columns, block):
    length = columns.shape[0]
    return jnp.broadcast_to(columns[length - 1 : length, block : block + 1], (1, HD))


def chip_sum(refs):
    summed = jnp.zeros((HD, HD), F32)
    passed = jnp.zeros((1, HD), F32)
    for ref in refs:
        summed = summed + jnp.exp(passed) * ref[0:HD, :].astype(F32)
        passed = passed + get_total(ref, HD)
    return summed


def put_message(ref, state, total):
    ref[0:HD, :] = state.astype(BF16)
    put_total(ref, HD, total)


def join_kernel(own_ref, got_ref, out_ref):
    total = get_total(own_ref, HD)
    state = own_ref[0:HD, :].astype(F32) + jnp.exp(total) * got_ref[0:HD, :].astype(F32)
    put_message(out_ref, state, total + get_total(got_ref, HD))


def cross_kernel(where_ref, *refs):
    *normed_refs, cross_ref = refs
    for number, ref in enumerate(normed_refs):
        cross_ref[number] = ref[1 - where_ref[0]]


def lanes_of(number):
    return pl.ds(pl.multiple_of(number * HD, HD), HD)


def rows_of(number, count):
    return pl.ds(pl.multiple_of(number * count, count), count)


def fresh_kernel(
    where_ref, q_ref, k_ref, v_ref, q_got, k_got, v_got, decay_ref, decay_got, q_out, k_out, v_out, col_ref, row_ref, first_ref, message_ref
):
    core = where_ref[0]
    length = q_ref.shape[0]
    for out, ref, got in ((q_out, q_ref, q_got), (k_out, k_ref, k_got), (v_out, v_ref, v_got)):
        out[core] = ref[:, lanes_of(core)]
        out[1 - core] = got[:, lanes_of(core)]
    mine = jnp.where(core == 0, decay_ref[0:1, :], decay_ref[1:2, :])
    theirs = jnp.where(core == 0, decay_got[0:1, :], decay_got[1:2, :])
    block = lax.broadcasted_iota(jnp.int32, (2, length), 0)
    decay = jnp.where(block == core, mine, theirs)
    lower = triangle(length)
    columns, rows = running_sums(decay, lower)
    col_ref[...] = columns
    row_ref[...] = rows
    states = []
    for b in range(2):
        fade = jnp.exp(columns[length - 1 : length, b : b + 1] - columns[:, b : b + 1])
        states.append(dot(k_out[b], (fade * v_out[b].astype(F32)).astype(BF16), TN))
    totals = [total_of(columns, b) for b in range(2)]
    first_ref[...] = states[0]
    put_message(message_ref, jnp.exp(totals[1]) * states[0] + states[1], totals[0] + totals[1])


def weights(columns, across, lower, b):
    return jnp.exp(jnp.where(lower, columns[:, b : b + 1] - across[b : b + 1, :], -1e30))


def inner_kernel(q_ref, k_ref, v_ref, col_ref, row_ref, first_ref, inner_ref):
    columns, across = col_ref[...], row_ref[...]
    lower = triangle(columns.shape[0])
    for b in range(2):
        scores = dot(q_ref[b], k_ref[b], NT) * weights(columns, across, lower, b)
        inner = dot_fb(scores, v_ref[b], NN)
        if b == 1:
            inner = inner + jnp.exp(columns[:, 1:2]) * dot_bf(q_ref[b], first_ref[...], NN)
        inner_ref[b] = inner


def scale_of(mixed):
    return lax.rsqrt(jnp.mean(mixed * mixed, axis=-1, keepdims=True) + EPSILON)


def mixed_kernel(where_ref, q_ref, col_ref, inner_ref, gain_ref, first_ref, *refs):
    chip_refs, (mixed_ref, normed_ref, state_ref) = refs[:-3], refs[-3:]
    core = where_ref[0]
    columns = col_ref[...]
    gain = gain_ref[:, lanes_of(core)]
    state = chip_sum(chip_refs)
    high, low = split(state)
    shrink = jnp.exp(total_of(columns, 0))
    state_ref[0] = state
    state_ref[1] = shrink * state + first_ref[...]
    for b in range(2):
        grow = jnp.exp(columns[:, b : b + 1])
        if b == 1:
            grow = grow * shrink
        mixed = inner_ref[b] + grow * (dot(q_ref[b], high, NN) + dot(q_ref[b], low, NN))
        mixed_ref[b] = mixed
        normed_ref[b] = (mixed * scale_of(mixed) * gain).astype(BF16)


def partial_kernel(kinds, where_ref, grad_ref, got_ref, *refs):
    core, side = where_ref[0], where_ref[1]
    refs = list(refs)
    inputs = [[refs.pop(0) for _ in range(2 if kind == "halves" else 1)] for kind in kinds]
    *products, weight_out = refs
    weights = []
    for kind, sources in zip(kinds, inputs):
        if kind == "own":
            weights.append(sources[0][rows_of(core, HD), :])
        elif kind == "halves":
            mine, theirs = sources[0][...], sources[1][...]
            weights += [jnp.where(side == 0, mine, theirs), jnp.where(side == 0, theirs, mine)]
        else:
            weights.append(sources[0][...])
    weight = jnp.concatenate(weights, axis=0)
    weight_out[...] = weight[2 * HD - weight_out.shape[0] :]
    length = grad_ref.shape[0]
    product = dot(jnp.concatenate([grad_ref[...], got_ref[...]], axis=0), weight, NT)
    for begin, block in ((0, core), (length, 1 - core)):
        for number, out in enumerate(products):
            part = product[begin : begin + length, number * HD : (number + 1) * HD]
            out[block] = part.astype(out.dtype)


def grad_mixed_kernel(where_ref, q_ref, col_ref, gain_ref, mixed_ref, own_ref, *refs):
    part_refs, (grad_ref, second_ref, message_ref) = refs[:-3], refs[-3:]
    columns = col_ref[...]
    gain = gain_ref[:, lanes_of(where_ref[0])]
    ups = []
    for b in range(2):
        normed = own_ref[b]
        for ref in part_refs:
            normed = normed + ref[b].astype(F32)
        lifted = normed * gain
        mixed = mixed_ref[b]
        scale = scale_of(mixed)
        unit = mixed * scale
        grad = scale * (lifted - unit * jnp.mean(unit * lifted, axis=-1, keepdims=True))
        grad_ref[b] = grad
        ups.append(dot(q_ref[b], (jnp.exp(columns[:, b : b + 1]) * grad).astype(BF16), TN))
    second_ref[...] = ups[1]
    totals = [total_of(columns, b) for b in range(2)]
    put_message(message_ref, ups[0] + jnp.exp(totals[0]) * ups[1], totals[0] + totals[1])


def inner_grad_kernel(
    where_ref, q_ref, k_ref, v_ref, col_ref, row_ref, grad_ref, state_ref, second_ref, keep_ref, send_ref
):
    core = where_ref[0]
    columns, across = col_ref[...], row_ref[...]
    length = columns.shape[0]
    lower = triangle(length)
    parts = []
    ends = [columns[length - 1 : length, b : b + 1] for b in range(2)]
    for b in range(2):
        q, k, v, grad = q_ref[b], k_ref[b], v_ref[b], grad_ref[b]
        weight = weights(columns, across, lower, b)
        narrow = grad.astype(BF16)
        scores = (dot(q, k, NT) * weight).astype(BF16)
        grad_scores = (dot(narrow, v, NT) * weight).astype(BF16)
        carried = jnp.exp(columns[:, b : b + 1]) * dot(narrow, state_ref[b].astype(BF16), NT)
        dq = dot(grad_scores, k, NN) + carried
        dk = dot(grad_scores, q, TN)
        dv = dot(scores, narrow, TN)
        fade = jnp.exp(ends[b] - columns[:, b : b + 1])
        if b == 0:
            second = second_ref[...].astype(BF16)
            dk = dk + fade * dot(v, second, NT)
            dv = dv + fade * dot(k, second, NN)
            fade = fade * jnp.exp(ends[1])
        parts.append((dq, dk, dv, jnp.broadcast_to(fade, (length, HD))))
    for number, (early, late) in enumerate(zip(*parts)):
        part = slice(number * HD, (number + 1) * HD)
        keep_ref[:, part] = jnp.where(core == 0, early, late)
        send_ref[:, part] = jnp.where(core == 0, late, early)


def outer_grad_kernel(count, where_ref, k_ref, v_ref, inner_ref, inner_got_ref, *refs):
    core = where_ref[0]
    outs = refs[2 * count :]
    for head, inner, chip_refs in (
        (core, inner_ref, refs[:count][::-1]),
        (1 - core, inner_got_ref, refs[count : 2 * count][::-1]),
    ):
        state = chip_sum(chip_refs).astype(BF16)
        fade = inner[:, 3 * HD : 4 * HD]
        k, v = k_ref[:, lanes_of(head)], v_ref[:, lanes_of(head)]
        outs[0][:, lanes_of(head)] = inner[:, 0:HD].astype(BF16)
        key = inner[:, HD : 2 * HD] + fade * dot(v, state, NT)
        outs[1][:, lanes_of(head)] = key.astype(BF16)
        value = inner[:, 2 * HD : 3 * HD] + fade * dot(k, state, NN)
        outs[2][:, lanes_of(head)] = value.astype(BF16)


def layer_kernel(pairs, where_ref, own_ref, *refs):
    mine_refs, theirs_refs = refs[:pairs], refs[pairs : 2 * pairs]
    *normed_refs, got_ref, out_ref = refs[2 * pairs :]
    core = where_ref[0]
    mine = [ref[core] for ref in normed_refs]
    theirs = [got_ref[number] for number in range(got_ref.shape[0])]
    normed = [mine[0], theirs[0], mine[1], theirs[1]]
    for begin in range(2, len(mine), 2):
        normed += mine[begin : begin + 2] + theirs[begin : begin + 2]
    normed = jnp.concatenate(normed, axis=1)
    width = own_ref.shape[1]
    step = 768 if width % 768 == 0 else 128
    for begin in range(0, width, step):
        lanes = slice(begin, begin + step)
        weight = [own_ref[rows_of(core, HD), lanes], own_ref[rows_of(1 - core, HD), lanes]]
        for mine_ref, theirs_ref in zip(mine_refs, theirs_refs):
            weight += [mine_ref[:, lanes], theirs_ref[:, lanes]]
        out_ref[:, lanes] = dot(normed, jnp.concatenate(weight, axis=0), NN).astype(BF16)


SMEM = pl.BlockSpec(memory_space=pltpu.SMEM)
VMEM = pl.BlockSpec(memory_space=pltpu.VMEM)


def call(kernel, name, outs, args, grant=16):
    return pl.pallas_call(
        kernel,
        name=name,
        out_shape=outs,
        in_specs=[SMEM] + [VMEM] * (len(args) - 1),
        out_specs=[VMEM] * len(outs),
        compiler_params=pltpu.CompilerParams(vmem_limit_bytes=grant * 2**20),
        cost_estimate=pl.CostEstimate(flops=1, bytes_accessed=1, transcendentals=0),
    )(*args)


def without_where(kernel):
    return lambda where_ref, *refs: kernel(*refs)


def after(values, *earlier):
    tied = lax.optimization_barrier((tuple(values), earlier))
    return list(tied[0])


def on_device(queries, keys, values, log_decay, norm_gain, out_weight, out_grad):
    length, columns = queries.shape
    seq = lax.axis_size("seq")
    tensor = lax.axis_size("tensor")
    chips = seq // 2
    model = out_weight.shape[1]
    width = model // tensor
    place = lax.axis_index("tensor")
    core = lax.rem(lax.axis_index("seq"), 2)
    side = lax.rem(lax.axis_index("seq") // 2, 2)
    where = jnp.stack([core, side]).astype(jnp.int32)
    gain = norm_gain.reshape(1, columns)

    def swap_tensor(value, k):
        return lax.ppermute(value, "tensor", [(i, i ^ k) for i in range(tensor)])

    def swap_core(value):
        return lax.ppermute(value, "seq", [(i, i ^ 1) for i in range(seq)])

    def swap_side(value):
        return lax.ppermute(value, "seq", [(i, i ^ 2) for i in range(seq)])

    def to_chip(value, step):
        return lax.ppermute(
            value, "seq", [(i, i + 2 * step) for i in range(seq) if 0 <= i + 2 * step < seq]
        )

    def shape(dtype, *dims):
        return jax.ShapeDtypeStruct(dims, dtype)

    others = range(1, tensor)
    message = shape(BF16, HD + TAIL, HD)
    pair16 = shape(BF16, 2, length, HD)
    pair32 = shape(F32, 2, length, HD)
    one16 = shape(BF16, length, HD)
    both16 = shape(BF16, length, columns)

    far = [step for step in others if step & (step - 1)]
    near = [step for step in others if not step & (step - 1)]
    order = far + near
    plan = [(step, step in far) for step in order]

    def slice_for(step, halves):
        rows = HD // 2 if halves else HD
        begin = core * HD + side * rows if halves else core * HD
        return lax.dynamic_slice(out_weight, (begin, (place ^ step) * width), (rows, width))

    slices = [slice_for(step, halves) for step, halves in plan]
    arriving = [swap_tensor(piece, step) for piece, step in zip(slices, order)]
    got = [swap_core(rows) for rows in (queries, keys, values)]
    got.append(swap_core(log_decay))
    (weight,) = after([out_weight], *slices)
    weight_own = lax.dynamic_slice(weight, (0, place * width), (columns, width))
    got = after(got, weight_own)
    (grad,) = after([out_grad], *got)
    grad_got = swap_core(grad)
    q, k, v, col, row, first, fresh = call(
        fresh_kernel,
        "fresh",
        [pair16, pair16, pair16, shape(F32, length, 2), shape(F32, 2, length), shape(F32, HD, HD), message],
        [where, queries, keys, values, *got[:3], log_decay, got[3]],
    )
    (fresh,) = after([fresh], grad_got)
    arrived, window, step = [], fresh, 1
    while step < chips:
        if arrived:
            (window,) = call(without_where(join_kernel), "join", [message], [where, window, arrived[-1]])
        arrived.append(to_chip(window, step))
        step *= 2
    (inner,) = call(without_where(inner_kernel), "inner", [pair32], [where, q, k, v, col, row, first])
    pieces = [("own", [weight_own])]
    for (step, halves), piece in zip(plan, arriving):
        if halves:
            (piece,) = after([piece], arrived[0])
        pieces.append(("halves", [piece, swap_side(piece)]) if halves else ("whole", [piece]))
    partials, mine, theirs = [], [], []
    for number in range(0, tensor, 2):
        kinds, sources = zip(*pieces[number : number + 2])
        sources = after(sum(sources, []), *arrived, inner, *partials)
        *outs, weight = call(
            functools.partial(partial_kernel, kinds),
            "partial",
            [pair16 if number else pair32, pair16, shape(BF16, 2 * HD if number else HD, width)],
            [where, out_grad, grad_got, *sources],
        )
        partials += outs
        mine.append(weight)
        if number == 0:
            theirs.append(swap_core(weight))
    own_partial, *partials = partials
    sent = [swap_tensor(partial, step) for partial, step in zip(partials, order)]
    mixed, normed, states = call(
        mixed_kernel,
        "mixed",
        [pair32, pair16, shape(F32, 2, HD, HD)],
        [where, q, col, inner, gain, first, *after(arrived, *partials)],
    )
    normed_all = [normed] + [swap_tensor(normed, step) for step in order]
    grad_mixed, second, upward = call(
        grad_mixed_kernel,
        "grad_mixed",
        [pair32, shape(F32, HD, HD), message],
        [where, q, col, gain, mixed, own_partial, *sent],
    )
    (upward,) = after([upward], *normed_all)
    (cross,) = call(cross_kernel, "cross", [shape(BF16, tensor, length, HD)], [where, *normed_all])
    cross_got = swap_core(cross)
    returned = [to_chip(upward, -step) for step in reversed(range(1, chips))]
    theirs += [swap_core(weight) for weight in after(mine[1:], upward)]
    inner_keep, inner_send = call(
        inner_grad_kernel,
        "inner_grad",
        [shape(F32, length, 4 * HD)] * 2,
        [where, q, k, v, col, row, grad_mixed, states, second],
    )
    (layer_out,) = call(
        functools.partial(layer_kernel, tensor // 2),
        "layer",
        [shape(BF16, length, width)],
        [where, weight_own, *mine, *theirs, *normed_all, cross_got],
    )
    returned = after(returned, layer_out)
    inner_got = swap_core(*after([inner_send], *returned))
    returned_got = [swap_core(rows) for rows in returned]
    query_grad, key_grad, value_grad = call(
        functools.partial(outer_grad_kernel, chips - 1),
        "outer_grad",
        [both16] * 3,
        [where, keys, values, inner_keep, inner_got, *returned, *returned_got],
    )
    return layer_out, query_grad, key_grad, value_grad


def solution(mesh):
    in_specs = (
        P("seq", "tensor"),
        P("seq", "tensor"),
        P("seq", "tensor"),
        P("tensor", "seq"),
        P("tensor"),
        P("tensor", None),
        P("seq", "tensor"),
    )
    out_specs = (P("seq", "tensor"), P("seq", "tensor"), P("seq", "tensor"), P("seq", "tensor"))
    return jax.shard_map(
        on_device, mesh=mesh, in_specs=in_specs, out_specs=out_specs, check_vma=False
    )
```
